256 devices in a mesh: rows: 16 (over x, y), cols: 16 (over z, core).
Axes of the slice: x: 4, y: 4, z: 8, core: 2. Of those that a mesh axis runs over, the one named last changes fastest.
Arguments:
- latent1: bfloat16 [256, 1024, 320], P('rows', 'cols'), may hold values from -15 to 15, as said below
- norm1a_g: float32 [320], replicated, may hold values from 0.25 to 1.75
- norm1a_b: float32 [320], replicated, may hold values from -3 to 3
- conv1a_w: bfloat16 [3, 3, 320, 320], replicated, may hold values from -0.109375 to 0.109375
- norm1b_g: float32 [320], replicated, may hold values from 0.25 to 1.75
- norm1b_b: float32 [320], replicated, may hold values from -3 to 3
- conv1b_w: bfloat16 [3, 3, 320, 320], replicated, may hold values from -0.109375 to 0.109375
- conv1b_b: float32 [320], replicated, may hold values from -3 to 3
- feat3: bfloat16 [64, 256, 1280], P('rows', 'cols'), may hold values from -15 to 15, as said below
- adapter3: bfloat16 [64, 256, 1280], P('rows', 'cols'), may hold values from -15 to 15, as said below
- norm3a_g: float32 [1280], replicated, may hold values from 0.25 to 1.75
- norm3a_b: float32 [1280], replicated, may hold values from -3 to 3
- conv3a_w: bfloat16 [3, 3, 1280, 1280], P(None, None, None, 'cols'), may hold values from -0.0546875 to 0.0546875
- norm3b_g: float32 [1280], P('cols'), may hold values from 0.25 to 1.75
- norm3b_b: float32 [1280], P('cols'), may hold values from -3 to 3
- conv3b_w: bfloat16 [3, 3, 1280, 1280], P(None, None, None, 'cols'), may hold values from -0.0546875 to 0.0546875
- conv3b_b: float32 [1280], P('cols'), may hold values from -3 to 3
Outputs:
- out1: bfloat16 [256, 1024, 320], P('rows', 'cols')
- out3: bfloat16 [64, 256, 1280], P('rows', None, 'cols')
The draws below stay inside these ranges and needn't reach their ends.
Inputs may be any that keep to these rules, and one draw needn't show every extreme that they name: `latent1`: real values. `feat3`: real values. `adapter3`: real values.
All inputs are finite; a program needn't handle non-finite values.
Results may differ from the reference program's by a relative error of at most 0.0052.
Values may be sent and summed in bfloat16 or wider, within the bound.
A program may use at most 128 MiB of HBM per device.

```python
import jax
import jax.numpy as jnp
from jax import lax

C1 = 320
C3 = 1280
R1 = 256
K1 = 1024
R3 = 64
W3 = 256


def spread_field(key, height, width, chans):
    key_noise, key_chan = jax.random.split(key, 2)
    row_pos = jnp.arange(height, dtype=jnp.float32) / max(height - 1, 1)
    col_pos = jnp.arange(width, dtype=jnp.float32) / max(width - 1, 1)
    chan_shift = jnp.clip(0.4 * jax.random.normal(key_chan, (chans,), jnp.float32), -1.0, 1.0)
    noise = jnp.clip(jax.random.normal(key_noise, (height, width, chans), jnp.float32), -4.0, 4.0)
    scale = 1.0 + 2.0 * row_pos
    offset = 1.5 * row_pos[:, None, None] - 0.5 * col_pos[None, :, None] + chan_shift[None, None, :]
    return noise * scale[:, None, None] + offset


def draw_latent1(key, part):
    return spread_field(jax.random.fold_in(key, 11), R1, K1, C1).astype(jnp.bfloat16)


def draw_feat3(key, part):
    return spread_field(jax.random.fold_in(key, 12), R3, W3, C3).astype(jnp.bfloat16)


def draw_adapter3(key, part):
    return spread_field(jax.random.fold_in(key, 13), R3, W3, C3).astype(jnp.bfloat16)


def level_of(stream_key, extent, shards, smallest, largest):
    level = 1.0
    for position, blocks in shards:
        draws = jax.random.uniform(jax.random.fold_in(jax.random.fold_in(stream_key, 6), position), (blocks,), jnp.float32, smallest / len(shards), largest / len(shards))
        level = level * jnp.repeat(jnp.exp(draws), extent[position] // blocks).reshape((-1,) + (1,) * (len(extent) - 1 - position))
    return level


def centred(stream_key, dims, scale, reach, shards=(), kind=jnp.bfloat16):
    level = level_of(stream_key, dims, shards, -0.22, 0.18) if shards else 1.0
    array = jax.random.normal(stream_key, dims, jnp.float32) * scale * level
    return jnp.minimum(jnp.maximum(array, -reach), reach).astype(kind)


def setup_inputs(seed: int = 0) -> dict:
    key_list = jax.random.split(jax.random.key(seed), 18)
    latent1 = draw_latent1(jax.random.fold_in(key_list[17], 71), 0)
    norm1a_g = jnp.clip(1.0 + 0.15 * jax.random.normal(key_list[1], (C1,), jnp.float32), 0.25, 1.75)
    norm1a_b = centred(key_list[2], (C1,), 0.5, 3.0, (), jnp.float32)
    conv1a_w = centred(key_list[3], (3, 3, C1, C1), (9 * C1) ** -0.5, 0.109375)
    norm1b_g = jnp.clip(1.0 + 0.15 * jax.random.normal(key_list[4], (C1,), jnp.float32), 0.25, 1.75)
    norm1b_b = centred(key_list[5], (C1,), 0.5, 3.0, (), jnp.float32)
    conv1b_w = centred(key_list[6], (3, 3, C1, C1), (9 * C1) ** -0.5, 0.109375)
    conv1b_b = centred(key_list[7], (C1,), 0.5, 3.0, (), jnp.float32)
    feat3 = draw_feat3(jax.random.fold_in(key_list[17], 71), 0)
    adapter3 = draw_adapter3(jax.random.fold_in(key_list[17], 71), 0)
    norm3a_g = jnp.clip(1.0 + 0.15 * jax.random.normal(key_list[10], (C3,), jnp.float32), 0.25, 1.75)
    norm3a_b = centred(key_list[11], (C3,), 0.5, 3.0, (), jnp.float32)
    conv3a_w = centred(key_list[12], (3, 3, C3, C3), (9 * C3) ** -0.5, 0.0546875, ((3, 16),))
    norm3b_g = jnp.clip(1.0 + 0.15 * jax.random.normal(key_list[13], (C3,), jnp.float32), 0.25, 1.75)
    norm3b_b = centred(key_list[14], (C3,), 0.5, 3.0, ((0, 16),), jnp.float32)
    conv3b_w = centred(key_list[15], (3, 3, C3, C3), (9 * C3) ** -0.5, 0.0546875, ((3, 16),))
    conv3b_b = centred(key_list[16], (C3,), 0.5, 3.0, ((0, 16),), jnp.float32)
    return {"latent1": latent1, "norm1a_g": norm1a_g, "norm1a_b": norm1a_b, "conv1a_w": conv1a_w, "norm1b_g": norm1b_g, "norm1b_b": norm1b_b, "conv1b_w": conv1b_w, "conv1b_b": conv1b_b, "feat3": feat3, "adapter3": adapter3, "norm3a_g": norm3a_g, "norm3a_b": norm3a_b, "conv3a_w": conv3a_w, "norm3b_g": norm3b_g, "norm3b_b": norm3b_b, "conv3b_w": conv3b_w, "conv3b_b": conv3b_b}


norm_groups = 32
norm_eps = 1e-05

def conv_same(field, kernel):
    return lax.conv_general_dilated(field[None], kernel, (1, 1), ((1, 1), (1, 1)), dimension_numbers=('NHWC', 'HWIO', 'NHWC'), preferred_element_type=jnp.float32)[0]

def group_silu(value, gain, shift):
    height, width, chans = value.shape
    grouped = value.astype(jnp.float32).reshape(height, width, norm_groups, chans // norm_groups)
    count = height * width * (chans // norm_groups)
    mean = lax.optimization_barrier(jnp.sum(grouped, axis=(0, 1, 3))) / count
    square = lax.optimization_barrier(jnp.sum(grouped * grouped, axis=(0, 1, 3))) / count
    inverse = lax.rsqrt(square - mean * mean + norm_eps)
    normed = ((grouped - mean[:, None]) * inverse[:, None]).reshape(height, width, chans)
    return jax.nn.silu(normed * gain + shift).astype(jnp.bfloat16)

def reference(latent1, norm1a_g, norm1a_b, conv1a_w, norm1b_g, norm1b_b, conv1b_w, conv1b_b, feat3, adapter3, norm3a_g, norm3a_b, conv3a_w, norm3b_g, norm3b_b, conv3b_w, conv3b_b):
    act1 = group_silu(latent1, norm1a_g, norm1a_b)
    hid1 = conv_same(act1, conv1a_w)
    act2 = group_silu(hid1, norm1b_g, norm1b_b)
    out1 = (latent1.astype(jnp.float32) + conv_same(act2, conv1b_w) + conv1b_b).astype(jnp.bfloat16)
    joined = (feat3.astype(jnp.float32) + adapter3.astype(jnp.float32)).astype(jnp.bfloat16)
    act3 = group_silu(joined, norm3a_g, norm3a_b)
    hid3 = conv_same(act3, conv3a_w)
    act4 = group_silu(hid3, norm3b_g, norm3b_b)
    out3 = (joined.astype(jnp.float32) + conv_same(act4, conv3b_w) + conv3b_b).astype(jnp.bfloat16)
    return (out1, out3)
```

```python
import functools

import jax
import jax.numpy as jnp
from jax import lax
from jax.experimental import pallas as pl
from jax.experimental.pallas import tpu as pltpu
from jax.sharding import PartitionSpec as P

MESH = pl.DeviceIdType.MESH
F32 = jnp.float32
BF16 = jnp.bfloat16
EPS = 1e-05
R, C = 16, 16
Z = 8
C1, C3, OC = 320, 1280, 80
H1, W1 = 16, 64
H3, W3 = 4, 256
WP = 80
NT = (((1,), (1,)), ((), ()))
COUNT1 = float(R * H1 * C * W1 * (C1 // 32))
COUNT3 = float(R * H3 * W3 * (C3 // 32))


def iota(shape, dim):
    return lax.broadcasted_iota(jnp.int32, shape, dim)


def group_matrix(chans, width, offset):
    chan = iota((chans, 128), 0)
    first = (iota((chans, 128), 1) - offset) * width
    return jnp.where((chan >= first) & (chan < first + width), 1.0, 0.0).astype(F32)


def exact_dot(a, b, dims=(((1,), (0,)), ((), ()))):
    return lax.dot_general(a, b, dims, precision=lax.Precision.HIGHEST, preferred_element_type=F32)


def halves(value):
    return value + value * jnp.tanh(value)


def kernel(
    lat_h, g1a, b1a, w1a_h, g1b, b1b, w1b_h, c1b, feat_h, adap_h, g3a, b3a, w3a_h, g3b, b3b, w3b_h, c3b,
    out1_h, out3_h,
    lat, top, bottom, pack, side, act, hid, w1a, w1b, w3a, w3b, feat, adap, gat1, act3, gat2, prod,
    edge_s, edge_r, hid3, res, o1, o3, st_a1, st_a2, st_b1, st_b2, st_c,
    local_sem, ar_send, ar_recv, ring_send, ring_recv, mate_send, mate_recv, own_send,
    halo_send, halo_recv, edge_send, edge_recv,
):
    row = lax.axis_index("rows")
    col = lax.axis_index("cols")
    z = col // 2
    core = col % 2
    up = (row + R - 1) % R
    down = (row + 1) % R
    left = (col + C - 1) % C
    right = (col + 1) % C
    mate = z * 2 + (1 - core)

    def local(src, dst, index):
        return pltpu.make_async_copy(src, dst, local_sem.at[index])

    loads = {
        "feat": local(feat_h, feat, 0),
        "adap": local(adap_h, adap, 1),
        "lat": local(lat_h, lat, 2),
        "w1a": local(w1a_h, w1a, 3),
        "w3a": local(w3a_h, w3a, 4),
        "w1b": local(w1b_h, w1b, 5),
        "w3b": local(w3b_h, w3b, 6),
    }
    for copy in loads.values():
        copy.start()

    barrier = pltpu.get_barrier_semaphore()
    for step in range(1, R):
        pl.semaphore_signal(barrier, inc=1, device_id={"rows": (row + step) % R}, device_id_type=MESH)
    for step in range(1, C):
        pl.semaphore_signal(barrier, inc=1, device_id={"cols": (col + step) % C}, device_id_type=MESH)

    def spread(buf, axis, index):
        me = row if axis == "rows" else col

        def send(step, carry):
            pltpu.make_async_remote_copy(
                src_ref=buf.at[0],
                dst_ref=buf.at[step],
                send_sem=ar_send.at[index],
                recv_sem=ar_recv.at[index],
                device_id={axis: (me + step) % 16},
                device_id_type=MESH,
            ).start()
            return carry

        lax.fori_loop(1, 16, send, 0)

    def collect(buf, axis, index):
        rest = pltpu.make_async_remote_copy(
            src_ref=buf.at[pl.ds(1, 15)],
            dst_ref=buf.at[pl.ds(1, 15)],
            send_sem=ar_send.at[index],
            recv_sem=ar_recv.at[index],
            device_id={axis: ((row if axis == "rows" else col) + 1) % 16},
            device_id_type=MESH,
        )
        rest.wait_recv()
        rest.wait_send()
        return jnp.sum(buf[...], axis=0)

    def origin(direction, hop):
        return (z + Z - hop) % Z if direction == 0 else (z + hop) % Z

    def chunk(gat, slot, half):
        return gat.at[slot, pl.ds(2 * half, 2)]

    def ring_copy(which, gat, direction, hop, half):
        slot = 2 * origin(direction, hop - 1) + core
        target = 2 * ((z + 1) % Z if direction == 0 else (z + Z - 1) % Z) + core
        return pltpu.make_async_remote_copy(
            src_ref=chunk(gat, slot, half),
            dst_ref=chunk(gat, slot, half),
            send_sem=ring_send.at[which, direction, hop - 1, half],
            recv_sem=ring_recv.at[which, direction, hop - 1, half],
            device_id={"cols": target},
            device_id_type=MESH,
        )

    def ring_wait(which, gat, direction, hop, half):
        slot = 2 * origin(direction, hop) + core
        target = 2 * ((z + 1) % Z if direction == 0 else (z + Z - 1) % Z) + core
        pltpu.make_async_remote_copy(
            src_ref=chunk(gat, slot, half),
            dst_ref=chunk(gat, slot, half),
            send_sem=ring_send.at[which, direction, hop - 1, half],
            recv_sem=ring_recv.at[which, direction, hop - 1, half],
            device_id={"cols": target},
            device_id_type=MESH,
        ).wait_recv()

    def mate_copy(which, gat, direction, hop, half):
        slot = 2 * origin(direction, hop) + core
        return pltpu.make_async_remote_copy(
            src_ref=chunk(gat, slot, half),
            dst_ref=chunk(gat, slot, half),
            send_sem=mate_send.at[which, direction, hop, half],
            recv_sem=mate_recv.at[which, direction, hop, half],
            device_id={"cols": mate},
            device_id_type=MESH,
        )

    def mate_wait(which, gat, direction, hop, half):
        slot = 2 * origin(direction, hop) + (1 - core)
        pltpu.make_async_remote_copy(
            src_ref=chunk(gat, slot, half),
            dst_ref=chunk(gat, slot, half),
            send_sem=mate_send.at[which, direction, hop, half],
            recv_sem=mate_recv.at[which, direction, hop, half],
            device_id={"cols": mate},
            device_id_type=MESH,
        ).wait_recv()

    def arrivals(hop):
        if hop == 4:
            return [(0, 0), (1, 1)]
        return [(direction, half) for half in range(2) for direction in range(2)]

    sends = []

    def go(copy):
        copy.start()
        sends.append(copy)

    def ring_start(which, gat):
        for half in range(2):
            for direction in range(2):
                go(ring_copy(which, gat, direction, 1, half))
        for half in range(2):
            go(mate_copy(which, gat, 0, 0, half))

    def ring_step(which, gat, hop):
        for direction, half in arrivals(hop):
            ring_wait(which, gat, direction, hop, half)
            if (direction, half) in (arrivals(hop + 1) if hop < 4 else []):
                go(ring_copy(which, gat, direction, hop + 1, half))
            go(mate_copy(which, gat, direction, hop, half))

    def mate_step(which, gat, hop):
        if hop == 0:
            for half in range(2):
                mate_wait(which, gat, 0, 0, half)
        else:
            for direction, half in arrivals(hop):
                mate_wait(which, gat, direction, hop, half)

    loads["feat"].wait()
    loads["adap"].wait()
    js = jnp.zeros((8, C3), F32)
    jq = jnp.zeros((8, C3), F32)
    for i in range(H3):
        value = (feat[i].astype(F32) + adap[i].astype(F32)).astype(BF16)
        gat1[col, i] = value
        value = value.astype(F32).reshape(2, 8, C3)
        js = js + jnp.sum(value, axis=0)
        jq = jq + jnp.sum(value * value, axis=0)

    pl.semaphore_wait(barrier, R - 1 + C - 1)
    ring_start(0, gat1)

    loads["lat"].wait()

    def halo_copy(src, dst, index, target):
        return pltpu.make_async_remote_copy(
            src_ref=src,
            dst_ref=dst,
            send_sem=halo_send.at[index],
            recv_sem=halo_recv.at[index],
            device_id=target,
            device_id_type=MESH,
        )

    to_down = halo_copy(lat.at[pl.ds(H1 - 2, 2)], top, 0, {"rows": down})
    to_up = halo_copy(lat.at[pl.ds(0, 2)], bottom, 1, {"rows": up})
    to_down.start()
    to_up.start()

    ls = jnp.zeros((8, C1), F32)
    lq = jnp.zeros((8, C1), F32)
    for i in range(H1):
        value = lat[i].astype(F32).reshape(8, 8, C1)
        ls = ls + jnp.sum(value, axis=0)
        lq = lq + jnp.sum(value * value, axis=0)
    st_a1[0] = (
        exact_dot(ls, group_matrix(C1, 10, 0))
        + exact_dot(lq, group_matrix(C1, 10, 32))
        + exact_dot(js, group_matrix(C3, 40, 64))
        + exact_dot(jq, group_matrix(C3, 40, 96))
    )
    spread(st_a1, "rows", 0)

    to_down.wait()
    to_up.wait()

    def extended_row(i):
        if i < 2:
            return top[i]
        if i < H1 + 2:
            return lat[i - 2]
        return bottom[i - H1 - 2]

    for block in range(3):
        rows_here = [i for i in range(8 * block, 8 * block + 8) if i < H1 + 4]
        tiles = [jnp.zeros((8, C1), F32) for _ in range(4)]
        for i in rows_here:
            value = extended_row(i)
            first = value[0:16].astype(F32)
            last = value[48:64].astype(F32)
            here = iota((8, C1), 0) == i - 8 * block
            for j, piece in enumerate((last[14:15], last[15:16], first[0:1], first[1:2])):
                tiles[j] = jnp.where(here, jnp.broadcast_to(piece, (8, C1)), tiles[j])
        for j in range(4):
            pack[j // 2, j % 2, pl.ds(8 * block, 8), :] = tiles[j]
    to_right = halo_copy(pack.at[0], side.at[0], 2, {"cols": right})
    to_left = halo_copy(pack.at[1], side.at[1], 3, {"cols": left})
    to_right.start()
    to_left.start()

    st_a2[0] = collect(st_a1, "rows", 0)
    spread(st_a2, "cols", 1)
    ring_step(0, gat1, 1)

    def group_rates(total):
        total = jnp.sum(total, axis=0, keepdims=True)
        total = jnp.broadcast_to(total, (8, 128))
        lane = iota((8, 128), 1)
        count = jnp.where(lane < 64, COUNT1, COUNT3)
        squares = pltpu.roll(total, 96, 1)
        mean = total / count
        spread_of = squares / count - mean * mean
        live = (lane < 32) | ((lane >= 64) & (lane < 96))
        inverse = lax.rsqrt(jnp.where(live, spread_of, 1.0) + EPS)
        return jnp.where(live, mean, 0.0), jnp.where(live, inverse, 0.0)

    def channel_rates(rates, matrix, gain, shift):
        mean, inverse = (exact_dot(x, matrix, NT)[0:1] for x in rates)
        scale = inverse * gain
        return 0.5 * scale, 0.5 * (shift - mean * scale)

    rates = group_rates(collect(st_a2, "cols", 1))
    scale1, shift1 = channel_rates(rates, group_matrix(C1, 10, 0), g1a[...], b1a[...])
    scale3, shift3 = channel_rates(rates, group_matrix(C3, 40, 64), g3a[...], b3a[...])

    def put_row(i, value, live):
        value = jnp.where(live, halves(value), 0.0)
        act[i, :, 0:C1] = pltpu.roll(value, 1, 0).astype(BF16)
        act[i, :, C1 : 2 * C1] = value.astype(BF16)
        act[i, :, 2 * C1 : 3 * C1] = pltpu.roll(value, WP - 1, 0).astype(BF16)

    place = iota((WP, C1), 0)

    to_right.wait()
    to_left.wait()
    slab_place = iota((16, C1), 0)
    wide_ok = (place < W1) | ((place < W1 + 2) & (col < C - 1)) | ((place >= WP - 2) & (col > 0))

    def act1_rows(first, last):
        for i in range(first, last):
            slab = jnp.zeros((16, C1), F32)
            base = 8 * (i // 8)
            for target, which, j in ((0, 1, 0), (1, 1, 1), (14, 0, 0), (15, 0, 1)):
                piece = side[which, j, pl.ds(base, 8), :][i - base : i - base + 1]
                slab = jnp.where(slab_place == target, jnp.broadcast_to(piece, (16, C1)), slab)
            value = jnp.concatenate([extended_row(i).astype(F32), slab], axis=0)
            live = wide_ok
            if i < 2:
                live = live & (row > 0)
            if i >= H1 + 2:
                live = live & (row < R - 1)
            put_row(i, value * scale1 + shift1, live)

    act1_rows(0, 10)
    ring_step(0, gat1, 2)
    act1_rows(10, 20)

    def conv1(weights, first, count, width):
        total = None
        for dy in range(3):
            block = act[pl.ds(first + dy, count), 0:width, :].reshape(count * width, 3 * C1)
            part = jnp.dot(block, weights[dy], preferred_element_type=F32)
            total = part if total is None else total + part
        return total.reshape(count, width, C1)

    def norm3(slot):
        for i in range(H3):
            value = gat1[slot, i].astype(F32) * scale3 + shift3
            act3[slot, i] = halves(value).astype(BF16)

    def norm3_hop(hop):
        mate_step(0, gat1, hop)
        for direction in range(1 if hop in (0, 4) else 2):
            for k in range(2):
                norm3(2 * origin(direction, hop) + k)

    loads["w1a"].wait()
    hid[pl.ds(0, 6)] = conv1(w1a, 0, 6, WP)
    ring_step(0, gat1, 3)
    hid[pl.ds(6, 6)] = conv1(w1a, 6, 6, WP)
    norm3_hop(0)
    norm3_hop(1)
    ring_step(0, gat1, 4)
    hid[pl.ds(12, 6)] = conv1(w1a, 12, 6, WP)

    hs = jnp.zeros((8, C1), F32)
    hq = jnp.zeros((8, C1), F32)
    for i in range(H1):
        value = hid[i + 1, 0:W1, :].reshape(8, 8, C1)
        hs = hs + jnp.sum(value, axis=0)
        hq = hq + jnp.sum(value * value, axis=0)
    st_b1[0] = exact_dot(hs, group_matrix(C1, 10, 0)) + exact_dot(hq, group_matrix(C1, 10, 32))
    spread(st_b1, "rows", 2)

    norm3_hop(2)
    norm3_hop(3)
    norm3_hop(4)

    def taps(weights, source, dims):
        def one(i, carry):
            prod[i] = lax.dot_general(weights[...], source(i), dims, preferred_element_type=F32)
            return carry

        lax.fori_loop(0, H3, one, 0)

    lane3 = iota((OC, W3), 1)

    def combine(target):
        columns = []
        for dx in range(3):
            total = None
            for dy in range(3):
                i = target + dy - 1
                if 0 <= i < H3:
                    part = prod[i, pl.ds((3 * dy + dx) * OC, OC), :]
                    total = part if total is None else total + part
            columns.append(total)
        before = jnp.where(lane3 == 0, 0.0, pltpu.roll(columns[0], 1, 1))
        after = jnp.where(lane3 == W3 - 1, 0.0, pltpu.roll(columns[2], W3 - 1, 1))
        return before + columns[1] + after

    def edge_copies(which):
        return [
            pltpu.make_async_remote_copy(
                src_ref=edge_s.at[which, j],
                dst_ref=edge_r.at[which, j],
                send_sem=edge_send.at[which, j],
                recv_sem=edge_recv.at[which, j],
                device_id={"rows": target},
                device_id_type=MESH,
            )
            for j, target in ((0, down), (1, up))
        ]

    def edges_out(which):
        edge_s[which, 0] = combine(H3)
        edge_s[which, 1] = combine(-1)
        copies = edge_copies(which)
        for copy in copies:
            copy.start()
        return copies

    def edges_in(which):
        low = jnp.where(row > 0, edge_r[which, 0], 0.0)
        high = jnp.where(row < R - 1, edge_r[which, 1], 0.0)
        return low, high

    loads["w3a"].wait()
    taps(w3a, lambda i: act3[:, i].reshape(W3, C3), NT)
    copies = edges_out(0)
    st_b2[0] = collect(st_b1, "rows", 2)
    spread(st_b2, "cols", 3)
    for i in range(H3):
        hid3[i] = combine(i)
    for copy in copies:
        copy.wait()
    low, high = edges_in(0)
    hid3[0] = hid3[0] + low
    hid3[H3 - 1] = hid3[H3 - 1] + high

    fs = jnp.zeros((OC, W3), F32)
    fq = jnp.zeros((OC, W3), F32)
    for i in range(H3):
        value = hid3[i]
        fs = fs + value
        fq = fq + value * value
    fs = jnp.sum(fs, axis=1, keepdims=True)
    fq = jnp.sum(fq, axis=1, keepdims=True)
    lane = iota((OC, 128), 1)
    second = iota((OC, 128), 0) >= OC // 2
    group = jnp.where(second, 1, 0)
    laid = jnp.where(lane == group, fs, 0.0) + jnp.where(lane == group + 2, fq, 0.0)
    st_c[0] = jnp.sum(laid.reshape(OC // 8, 8, 128), axis=0)
    spread(st_c, "rows", 4)

    rates = group_rates(collect(st_b2, "cols", 3))
    scale2, shift2 = channel_rates(rates, group_matrix(C1, 10, 0), g1b[...], b1b[...])
    near_ok = (place < W1) | ((place == W1) & (col < C - 1)) | ((place == WP - 1) & (col > 0))

    def act2_rows(first, last):
        for i in range(first, last):
            live = near_ok
            if i == 0:
                live = live & (row > 0)
            if i == H1 + 1:
                live = live & (row < R - 1)
            put_row(i, hid[i] * scale2 + shift2, live)

    act2_rows(0, 6)

    total = jnp.sum(collect(st_c, "rows", 4), axis=0, keepdims=True)
    total = jnp.broadcast_to(total, (OC, 128)) / COUNT3
    mean = jnp.sum(jnp.where(lane == group, total, 0.0), axis=1, keepdims=True)
    square = jnp.sum(jnp.where(lane == group + 2, total, 0.0), axis=1, keepdims=True)
    inverse = lax.rsqrt(square - mean * mean + EPS)

    def upright(ref):
        eye = iota((OC, OC), 0) == iota((OC, OC), 1)
        return jnp.sum(jnp.where(eye, jnp.broadcast_to(ref[...], (OC, OC)), 0.0), axis=1, keepdims=True)

    scale4 = inverse * upright(g3b)
    shift4 = 0.5 * (upright(b3b) - mean * scale4)
    scale4 = 0.5 * scale4
    for i in range(H3):
        gat2[col, i] = halves(hid3[i] * scale4 + shift4).astype(BF16)
    ring_start(1, gat2)

    act2_rows(6, 18)
    loads["w1b"].wait()

    def out1_rows(first, count):
        value = conv1(w1b, first, count, W1) + c1b[...].reshape(1, 1, C1)
        o1[pl.ds(first, count)] = (lat[pl.ds(first, count)].astype(F32) + value).astype(BF16)

    ring_step(1, gat2, 1)
    out1_rows(0, 8)
    ring_step(1, gat2, 2)
    out1_rows(8, 8)
    write1 = local(o1, out1_h, 7)
    write1.start()
    ring_step(1, gat2, 3)

    pick = jnp.where(iota((OC, C3), 1) == iota((OC, C3), 0) + col * OC, 1.0, 0.0).astype(BF16)

    def residual(i, carry):
        res[i] = lax.dot_general(pick, gat1[:, i].reshape(W3, C3), NT, preferred_element_type=F32)
        return carry

    lax.fori_loop(0, H3, residual, 0)
    bias3 = upright(c3b)
    ring_step(1, gat2, 4)
    for hop in range(5):
        mate_step(1, gat2, hop)

    loads["w3b"].wait()
    taps(w3b, lambda i: gat2[:, i].reshape(C3, W3), (((1,), (0,)), ((), ())))
    copies = edges_out(1)
    for i in range(H3):
        res[i] = res[i] + combine(i) + bias3
    for copy in copies:
        copy.wait()
    low, high = edges_in(1)
    res[0] = res[0] + low
    res[H3 - 1] = res[H3 - 1] + high
    for i in range(H3):
        o3[i] = res[i].astype(BF16)
    write3 = local(o3, out3_h, 8)
    write3.start()
    for copy in sends:
        copy.wait_send()
    write1.wait()
    write3.wait()


def body(
    latent1, norm1a_g, norm1a_b, conv1a_w, norm1b_g, norm1b_b, conv1b_w, conv1b_b,
    feat3, adapter3, norm3a_g, norm3a_b, conv3a_w, norm3b_g, norm3b_b, conv3b_w, conv3b_b,
):
    def flat(x):
        return x.reshape(1, -1)

    def wide(w):
        return w.reshape(3, 3 * C1, C1)

    def tall(w):
        return jnp.swapaxes(w, 2, 3).reshape(9 * OC, C3)

    any_spec = pl.BlockSpec(memory_space=pl.ANY)
    vmem_spec = pl.BlockSpec(memory_space=pltpu.VMEM)
    operands = [
        (latent1, any_spec), (flat(norm1a_g), vmem_spec), (flat(norm1a_b), vmem_spec), (wide(conv1a_w), any_spec),
        (flat(norm1b_g), vmem_spec), (flat(norm1b_b), vmem_spec), (wide(conv1b_w), any_spec), (flat(conv1b_b), vmem_spec),
        (feat3, any_spec), (adapter3, any_spec), (flat(norm3a_g), vmem_spec), (flat(norm3a_b), vmem_spec),
        (tall(conv3a_w), any_spec), (flat(norm3b_g), vmem_spec), (flat(norm3b_b), vmem_spec),
        (tall(conv3b_w), any_spec), (flat(conv3b_b), vmem_spec),
    ]
    out1, out3 = pl.pallas_call(
        kernel,
        out_shape=(
            jax.ShapeDtypeStruct((H1, W1, C1), BF16),
            jax.ShapeDtypeStruct((H3, OC, W3), BF16),
        ),
        in_specs=[spec for _, spec in operands],
        out_specs=(any_spec, any_spec),
        scratch_shapes=[
            pltpu.VMEM((H1, W1, C1), BF16),
            pltpu.VMEM((2, W1, C1), BF16),
            pltpu.VMEM((2, W1, C1), BF16),
            pltpu.VMEM((2, 2, 24, C1), F32),
            pltpu.VMEM((2, 2, 24, C1), F32),
            pltpu.VMEM((H1 + 4, WP, 3 * C1), BF16),
            pltpu.VMEM((H1 + 2, WP, C1), F32),
            pltpu.VMEM((3, 3 * C1, C1), BF16),
            pltpu.VMEM((3, 3 * C1, C1), BF16),
            pltpu.VMEM((9 * OC, C3), BF16),
            pltpu.VMEM((9 * OC, C3), BF16),
            pltpu.VMEM((H3, 16, C3), BF16),
            pltpu.VMEM((H3, 16, C3), BF16),
            pltpu.VMEM((C, H3, 16, C3), BF16),
            pltpu.VMEM((C, H3, 16, C3), BF16),
            pltpu.VMEM((C, H3, OC, W3), BF16),
            pltpu.VMEM((H3, 9 * OC, W3), F32),
            pltpu.VMEM((2, 2, OC, W3), F32),
            pltpu.VMEM((2, 2, OC, W3), F32),
            pltpu.VMEM((H3, OC, W3), F32),
            pltpu.VMEM((H3, OC, W3), F32),
            pltpu.VMEM((H1, W1, C1), BF16),
            pltpu.VMEM((H3, OC, W3), BF16),
            pltpu.VMEM((16, 8, 128), F32),
            pltpu.VMEM((16, 8, 128), F32),
            pltpu.VMEM((16, 8, 128), F32),
            pltpu.VMEM((16, 8, 128), F32),
            pltpu.VMEM((16, 8, 128), F32),
            pltpu.SemaphoreType.DMA((9,)),
            pltpu.SemaphoreType.DMA((5,)),
            pltpu.SemaphoreType.DMA((5,)),
            pltpu.SemaphoreType.DMA((2, 2, 4, 2)),
            pltpu.SemaphoreType.DMA((2, 2, 4, 2)),
            pltpu.SemaphoreType.DMA((2, 2, 5, 2)),
            pltpu.SemaphoreType.DMA((2, 2, 5, 2)),
            pltpu.SemaphoreType.DMA((1,)),
            pltpu.SemaphoreType.DMA((4,)),
            pltpu.SemaphoreType.DMA((4,)),
            pltpu.SemaphoreType.DMA((2, 2)),
            pltpu.SemaphoreType.DMA((2, 2)),
        ],
        compiler_params=pltpu.CompilerParams(
            collective_id=0, has_side_effects=True, vmem_limit_bytes=56 * 1024 * 1024
        ),
    )(*[value for value, _ in operands])
    return out1, jnp.swapaxes(out3, 1, 2)


def solution(mesh):
    return jax.shard_map(
        body,
        mesh=mesh,
        in_specs=(
            P("rows", "cols", None), P(), P(), P(), P(), P(), P(), P(),
            P("rows", "cols", None), P("rows", "cols", None), P(), P(),
            P(None, None, None, "cols"), P("cols"), P("cols"), P(None, None, None, "cols"), P("cols"),
        ),
        out_specs=(P("rows", "cols", None), P("rows", None, "cols")),
        check_vma=False,
    )
```

```python
import functools

import jax
import jax.numpy as jnp
from jax import lax
from jax.experimental import pallas as pl
from jax.experimental.pallas import tpu as pltpu
from jax.sharding import PartitionSpec as P

MESH = pl.DeviceIdType.MESH
F32 = jnp.float32
BF16 = jnp.bfloat16
EPS = 1e-05
R, C = 16, 16
Z = 8
C1, C3, OC = 320, 1280, 80
H1, W1 = 16, 64
H3, W3 = 4, 256
WP = 80
NT = (((1,), (1,)), ((), ()))
COUNT1 = float(R * H1 * C * W1 * (C1 // 32))
COUNT3 = float(R * H3 * W3 * (C3 // 32))


def iota(shape, dim):
    return lax.broadcasted_iota(jnp.int32, shape, dim)


def group_matrix(chans, width, offset, dim):
    shape = (chans, 128) if dim == 0 else (128, chans)
    chan = iota(shape, dim)
    first = (iota(shape, 1 - dim) - offset) * width
    return jnp.where((chan >= first) & (chan < first + width), 1.0, 0.0).astype(BF16)


def exact_dot(a, ones):
    high = a.astype(BF16)
    rest = a - high.astype(F32)
    middle = rest.astype(BF16)
    low = (rest - middle.astype(F32)).astype(BF16)
    n = a.shape[0]
    out = jnp.dot(jnp.concatenate([high, middle, low], axis=0), ones, preferred_element_type=F32)
    return out[0:n] + out[n : 2 * n] + out[2 * n :]


def group_sums(sums, squares, ones, offset):
    both = exact_dot(jnp.concatenate([sums, squares], axis=0), ones)
    first = pltpu.roll(both[0:8], offset, 1) if offset else both[0:8]
    return first + pltpu.roll(both[8:16], offset + 32, 1)


def flat(ref):
    return ref[...].reshape(1, -1)


def halves(value):
    return value + value * jnp.tanh(value)


def kernel(
    lat_h, g1a_h, b1a_h, w1a_h, g1b_h, b1b_h, w1b_h, c1b_h,
    feat_h, adap_h, g3a_h, b3a_h, w3a_h, g3b_h, b3b_h, w3b_h, c3b_h,
    out1_h, out3_h,
    g1a, b1a, g1b, b1b, c1b, g3a, b3a, g3b, b3b, c3b,
    lat, top, bottom, pack, side, act, hid, w1a, w1b, w3a, w3b, feat, adap, gat1, act3, gat2, prod,
    edge_s, edge_r, hid3, res, o1, o3, st_a1, st_a2, st_b1, st_b2, st_c,
    local_sem, ar_send, ar_recv, ring_send, ring_recv, mate_send, mate_recv, own_send,
    halo_send, halo_recv, edge_send, edge_recv,
):
    row = lax.axis_index("rows")
    col = lax.axis_index("cols")
    z = col // 2
    core = col % 2
    up = (row + R - 1) % R
    down = (row + 1) % R
    left = (col + C - 1) % C
    right = (col + 1) % C
    mate = z * 2 + (1 - core)

    def local(src, dst, index):
        return pltpu.make_async_copy(src, dst, local_sem.at[index])

    loads = {
        "feat": local(feat_h, feat, 0),
        "adap": local(adap_h, adap, 1),
        "lat": local(lat_h, lat, 2),
        "w1a": local(w1a_h, w1a, 3),
        "w3a": local(w3a_h, w3a, 4),
        "w1b": local(w1b_h, w1b, 5),
        "w3b": local(w3b_h, w3b, 6),
    }
    small = [
        local(src, dst, 9 + i)
        for i, (src, dst) in enumerate(
            (
                (g1a_h, g1a), (b1a_h, b1a), (g1b_h, g1b), (b1b_h, b1b), (c1b_h, c1b),
                (g3a_h, g3a), (b3a_h, b3a), (g3b_h, g3b), (b3b_h, b3b), (c3b_h, c3b),
            )
        )
    ]
    for name in ("feat", "adap", "lat"):
        loads[name].start()

    barrier = pltpu.get_barrier_semaphore()
    for step in range(1, R):
        pl.semaphore_signal(barrier, inc=1, device_id={"rows": (row + step) % R}, device_id_type=MESH)
    for step in range(1, C):
        pl.semaphore_signal(barrier, inc=1, device_id={"cols": (col + step) % C}, device_id_type=MESH)

    def spread(buf, axis, index):
        me = row if axis == "rows" else col

        def send(step, carry):
            pltpu.make_async_remote_copy(
                src_ref=buf.at[0],
                dst_ref=buf.at[step],
                send_sem=ar_send.at[index],
                recv_sem=ar_recv.at[index],
                device_id={axis: (me + step) % 16},
                device_id_type=MESH,
            ).start()
            return carry

        lax.fori_loop(1, 16, send, 0)

    def collect(buf, axis, index):
        rest = pltpu.make_async_remote_copy(
            src_ref=buf.at[pl.ds(1, 15)],
            dst_ref=buf.at[pl.ds(1, 15)],
            send_sem=ar_send.at[index],
            recv_sem=ar_recv.at[index],
            device_id={axis: ((row if axis == "rows" else col) + 1) % 16},
            device_id_type=MESH,
        )
        rest.wait_recv()
        rest.wait_send()
        return jnp.sum(buf[...], axis=0)

    def origin(direction, hop):
        return (z + Z - hop) % Z if direction == 0 else (z + hop) % Z

    def chunk(gat, slot, half):
        return gat.at[slot, pl.ds(2 * half, 2)]

    def ring_copy(which, gat, direction, hop, half):
        slot = 2 * origin(direction, hop - 1) + core
        target = 2 * ((z + 1) % Z if direction == 0 else (z + Z - 1) % Z) + core
        return pltpu.make_async_remote_copy(
            src_ref=chunk(gat, slot, half),
            dst_ref=chunk(gat, slot, half),
            send_sem=ring_send.at[which, direction, hop - 1, half],
            recv_sem=ring_recv.at[which, direction, hop - 1, half],
            device_id={"cols": target},
            device_id_type=MESH,
        )

    def ring_wait(which, gat, direction, hop, half):
        slot = 2 * origin(direction, hop) + core
        target = 2 * ((z + 1) % Z if direction == 0 else (z + Z - 1) % Z) + core
        pltpu.make_async_remote_copy(
            src_ref=chunk(gat, slot, half),
            dst_ref=chunk(gat, slot, half),
            send_sem=ring_send.at[which, direction, hop - 1, half],
            recv_sem=ring_recv.at[which, direction, hop - 1, half],
            device_id={"cols": target},
            device_id_type=MESH,
        ).wait_recv()

    def mate_copy(which, gat, direction, hop, half):
        slot = 2 * origin(direction, hop) + core
        return pltpu.make_async_remote_copy(
            src_ref=chunk(gat, slot, half),
            dst_ref=chunk(gat, slot, half),
            send_sem=mate_send.at[which, direction, hop, half],
            recv_sem=mate_recv.at[which, direction, hop, half],
            device_id={"cols": mate},
            device_id_type=MESH,
        )

    def mate_wait(which, gat, direction, hop, half):
        slot = 2 * origin(direction, hop) + (1 - core)
        pltpu.make_async_remote_copy(
            src_ref=chunk(gat, slot, half),
            dst_ref=chunk(gat, slot, half),
            send_sem=mate_send.at[which, direction, hop, half],
            recv_sem=mate_recv.at[which, direction, hop, half],
            device_id={"cols": mate},
            device_id_type=MESH,
        ).wait_recv()

    def arrivals(hop):
        if hop == 4:
            return [(0, 0), (1, 1)]
        return [(direction, half) for half in range(2) for direction in range(2)]

    sends = []

    def go(copy):
        copy.start()
        sends.append(copy)

    def ring_start(which, gat):
        for half in range(2):
            for direction in range(2):
                go(ring_copy(which, gat, direction, 1, half))
        for half in range(2):
            go(mate_copy(which, gat, 0, 0, half))

    def ring_step(which, gat, hop, only=None):
        for direction, half in arrivals(hop):
            if only is not None and half != only:
                continue
            ring_wait(which, gat, direction, hop, half)
            if (direction, half) in (arrivals(hop + 1) if hop < 4 else []):
                go(ring_copy(which, gat, direction, hop + 1, half))
            go(mate_copy(which, gat, direction, hop, half))

    def mate_step(which, gat, hop):
        if hop == 0:
            for half in range(2):
                mate_wait(which, gat, 0, 0, half)
        else:
            for direction, half in arrivals(hop):
                mate_wait(which, gat, direction, hop, half)

    loads["feat"].wait()
    loads["adap"].wait()
    for copy in small:
        copy.start()
    for name in ("w1a", "w3a", "w1b", "w3b"):
        loads[name].start()
    js = jnp.zeros((8, C3), F32)
    jq = jnp.zeros((8, C3), F32)
    for i in range(H3):
        value = (feat[i].astype(F32) + adap[i].astype(F32)).astype(BF16)
        gat1[col, i] = value
        value = value.astype(F32).reshape(2, 8, C3)
        js = js + jnp.sum(value, axis=0)
        jq = jq + jnp.sum(value * value, axis=0)

    pl.semaphore_wait(barrier, R - 1 + C - 1)
    ring_start(0, gat1)
    joined_sums = group_sums(js, jq, group_matrix(C3, 40, 0, 0), 64)

    loads["lat"].wait()

    def halo_copy(src, dst, index, target):
        return pltpu.make_async_remote_copy(
            src_ref=src,
            dst_ref=dst,
            send_sem=halo_send.at[index],
            recv_sem=halo_recv.at[index],
            device_id=target,
            device_id_type=MESH,
        )

    to_down = halo_copy(lat.at[pl.ds(H1 - 2, 2)], top, 0, {"rows": down})
    to_up = halo_copy(lat.at[pl.ds(0, 2)], bottom, 1, {"rows": up})
    to_down.start()
    to_up.start()

    ls = jnp.zeros((8, C1), F32)
    lq = jnp.zeros((8, C1), F32)
    for i in range(H1):
        value = lat[i].astype(F32).reshape(8, 8, C1)
        ls = ls + jnp.sum(value, axis=0)
        lq = lq + jnp.sum(value * value, axis=0)
    ones1 = group_matrix(C1, 10, 0, 0)
    st_a1[0] = group_sums(ls, lq, ones1, 0) + joined_sums
    spread(st_a1, "rows", 0)

    to_down.wait()
    to_up.wait()

    def extended_row(i):
        if i < 2:
            return top[i]
        if i < H1 + 2:
            return lat[i - 2]
        return bottom[i - H1 - 2]

    for block in range(3):
        rows_here = [i for i in range(8 * block, 8 * block + 8) if i < H1 + 4]
        tiles = [jnp.zeros((8, C1), F32) for _ in range(4)]
        for i in rows_here:
            value = extended_row(i)
            first = value[0:16].astype(F32)
            last = value[48:64].astype(F32)
            here = iota((8, C1), 0) == i - 8 * block
            for j, piece in enumerate((last[14:15], last[15:16], first[0:1], first[1:2])):
                tiles[j] = jnp.where(here, jnp.broadcast_to(piece, (8, C1)), tiles[j])
        for j in range(4):
            pack[j // 2, j % 2, pl.ds(8 * block, 8), :] = tiles[j]
    to_right = halo_copy(pack.at[0], side.at[0], 2, {"cols": right})
    to_left = halo_copy(pack.at[1], side.at[1], 3, {"cols": left})
    to_right.start()
    to_left.start()

    ring_step(0, gat1, 1, 0)
    st_a2[0] = collect(st_a1, "rows", 0)
    spread(st_a2, "cols", 1)
    ring_step(0, gat1, 1, 1)

    def group_rates(total):
        total = jnp.sum(total, axis=0, keepdims=True)
        total = jnp.broadcast_to(total, (8, 128))
        lane = iota((8, 128), 1)
        count = jnp.where(lane < 64, COUNT1, COUNT3)
        squares = pltpu.roll(total, 96, 1)
        mean = total / count
        spread_of = squares / count - mean * mean
        live = (lane < 32) | ((lane >= 64) & (lane < 96))
        inverse = lax.rsqrt(jnp.where(live, spread_of, 1.0) + EPS)
        return jnp.where(live, mean, 0.0), jnp.where(live, inverse, 0.0)

    def channel_rates(rates, matrix, gain, shift):
        both = exact_dot(jnp.where(iota((8, 128), 0) == 0, *rates), matrix)
        mean, inverse = both[0:1], both[1:2]
        scale = inverse * gain
        return 0.5 * scale, 0.5 * (shift - mean * scale)

    for copy in small:
        copy.wait()
    rates = group_rates(collect(st_a2, "cols", 1))
    scale1, shift1 = channel_rates(rates, group_matrix(C1, 10, 0, 1), flat(g1a), flat(b1a))

    def put_row(i, value, live):
        value = jnp.where(live, halves(value), 0.0)
        act[i, :, 0:C1] = pltpu.roll(value, 1, 0).astype(BF16)
        act[i, :, C1 : 2 * C1] = value.astype(BF16)
        act[i, :, 2 * C1 : 3 * C1] = pltpu.roll(value, WP - 1, 0).astype(BF16)

    place = iota((WP, C1), 0)

    to_right.wait()
    to_left.wait()
    slab_place = iota((16, C1), 0)
    wide_ok = (place < W1) | ((place < W1 + 2) & (col < C - 1)) | ((place >= WP - 2) & (col > 0))

    def act1_rows(first, last):
        for i in range(first, last):
            slab = jnp.zeros((16, C1), F32)
            base = 8 * (i // 8)
            for target, which, j in ((0, 1, 0), (1, 1, 1), (14, 0, 0), (15, 0, 1)):
                piece = side[which, j, pl.ds(base, 8), :][i - base : i - base + 1]
                slab = jnp.where(slab_place == target, jnp.broadcast_to(piece, (16, C1)), slab)
            value = jnp.concatenate([extended_row(i).astype(F32), slab], axis=0)
            live = wide_ok
            if i < 2:
                live = live & (row > 0)
            if i >= H1 + 2:
                live = live & (row < R - 1)
            put_row(i, value * scale1 + shift1, live)

    ring_step(0, gat1, 2, 0)
    act1_rows(0, 20)
    ring_step(0, gat1, 2, 1)

    def conv1(weights, first, count, width):
        total = None
        for dy in range(3):
            block = act[pl.ds(first + dy, count), 0:width, :].reshape(count * width, 3 * C1)
            part = jnp.dot(block, weights[dy], preferred_element_type=F32)
            total = part if total is None else total + part
        return total.reshape(count, width, C1)

    def norm3(slot):
        for i in range(H3):
            value = gat1[slot, i].astype(F32) * scale3 + shift3
            act3[slot, i] = halves(value).astype(BF16)

    def norm3_hop(hop):
        mate_step(0, gat1, hop)
        for direction in range(1 if hop in (0, 4) else 2):
            for k in range(2):
                norm3(2 * origin(direction, hop) + k)

    loads["w1a"].wait()
    hid[pl.ds(0, 6)] = conv1(w1a, 0, 6, WP)
    scale3, shift3 = channel_rates(rates, group_matrix(C3, 40, 64, 1), flat(g3a), flat(b3a))
    ring_step(0, gat1, 3, 0)
    hid[pl.ds(6, 6)] = conv1(w1a, 6, 6, WP)
    norm3_hop(0)
    ring_step(0, gat1, 3, 1)
    hid[pl.ds(12, 6)] = conv1(w1a, 12, 6, WP)
    norm3_hop(1)
    ring_step(0, gat1, 4)

    hs = jnp.zeros((8, C1), F32)
    hq = jnp.zeros((8, C1), F32)
    for i in range(H1):
        value = hid[i + 1, 0:W1, :].reshape(8, 8, C1)
        hs = hs + jnp.sum(value, axis=0)
        hq = hq + jnp.sum(value * value, axis=0)
    st_b1[0] = group_sums(hs, hq, ones1, 0)
    spread(st_b1, "rows", 2)

    norm3_hop(2)
    norm3_hop(3)
    norm3_hop(4)

    def taps(weights, source, dims):
        def one(i, carry):
            prod[i] = lax.dot_general(weights[...], source(i), dims, preferred_element_type=F32)
            return carry

        lax.fori_loop(0, H3, one, 0)

    lane3 = iota((OC, W3), 1)

    def combine(target):
        columns = []
        for dx in range(3):
            total = None
            for dy in range(3):
                i = target + dy - 1
                if 0 <= i < H3:
                    part = prod[i, pl.ds((3 * dy + dx) * OC, OC), :]
                    total = part if total is None else total + part
            columns.append(total)
        before = jnp.where(lane3 == 0, 0.0, pltpu.roll(columns[0], 1, 1))
        after = jnp.where(lane3 == W3 - 1, 0.0, pltpu.roll(columns[2], W3 - 1, 1))
        return before + columns[1] + after

    def edge_copies(which):
        return [
            pltpu.make_async_remote_copy(
                src_ref=edge_s.at[which, j],
                dst_ref=edge_r.at[which, j],
                send_sem=edge_send.at[which, j],
                recv_sem=edge_recv.at[which, j],
                device_id={"rows": target},
                device_id_type=MESH,
            )
            for j, target in ((0, down), (1, up))
        ]

    def edges_out(which):
        edge_s[which, 0] = combine(H3)
        edge_s[which, 1] = combine(-1)
        copies = edge_copies(which)
        for copy in copies:
            copy.start()
        return copies

    def edges_in(which):
        low = jnp.where(row > 0, edge_r[which, 0], 0.0)
        high = jnp.where(row < R - 1, edge_r[which, 1], 0.0)
        return low, high

    loads["w3a"].wait()
    taps(w3a, lambda i: act3[:, i].reshape(W3, C3), NT)
    copies = edges_out(0)
    st_b2[0] = collect(st_b1, "rows", 2)
    spread(st_b2, "cols", 3)
    for i in range(H3):
        hid3[i] = combine(i)
    for copy in copies:
        copy.wait()
    low, high = edges_in(0)
    hid3[0] = hid3[0] + low
    hid3[H3 - 1] = hid3[H3 - 1] + high

    fs = jnp.zeros((OC, W3), F32)
    fq = jnp.zeros((OC, W3), F32)
    for i in range(H3):
        value = hid3[i]
        fs = fs + value
        fq = fq + value * value
    fs = jnp.sum(fs, axis=1, keepdims=True)
    fq = jnp.sum(fq, axis=1, keepdims=True)
    lane = iota((OC, 128), 1)
    second = iota((OC, 128), 0) >= OC // 2
    group = jnp.where(second, 1, 0)
    laid = jnp.where(lane == group, fs, 0.0) + jnp.where(lane == group + 2, fq, 0.0)
    st_c[0] = jnp.sum(laid.reshape(OC // 8, 8, 128), axis=0)
    spread(st_c, "rows", 4)

    rates = group_rates(collect(st_b2, "cols", 3))
    scale2, shift2 = channel_rates(rates, group_matrix(C1, 10, 0, 1), flat(g1b), flat(b1b))
    near_ok = (place < W1) | ((place == W1) & (col < C - 1)) | ((place == WP - 1) & (col > 0))

    def act2_rows(first, last):
        for i in range(first, last):
            live = near_ok
            if i == 0:
                live = live & (row > 0)
            if i == H1 + 1:
                live = live & (row < R - 1)
            put_row(i, hid[i] * scale2 + shift2, live)

    act2_rows(0, 6)

    total = jnp.sum(collect(st_c, "rows", 4), axis=0, keepdims=True)
    total = jnp.broadcast_to(total, (OC, 128)) / COUNT3
    mean = jnp.sum(jnp.where(lane == group, total, 0.0), axis=1, keepdims=True)
    square = jnp.sum(jnp.where(lane == group + 2, total, 0.0), axis=1, keepdims=True)
    inverse = lax.rsqrt(square - mean * mean + EPS)

    def upright(ref):
        eye = iota((OC, OC), 0) == iota((OC, OC), 1)
        return jnp.sum(jnp.where(eye, jnp.broadcast_to(flat(ref), (OC, OC)), 0.0), axis=1, keepdims=True)

    scale4 = inverse * upright(g3b)
    shift4 = 0.5 * (upright(b3b) - mean * scale4)
    scale4 = 0.5 * scale4
    for i in range(H3):
        gat2[col, i] = halves(hid3[i] * scale4 + shift4).astype(BF16)
    ring_start(1, gat2)

    act2_rows(6, 18)
    loads["w1b"].wait()

    def out1_rows(first, count):
        value = conv1(w1b, first, count, W1) + flat(c1b).reshape(1, 1, C1)
        o1[pl.ds(first, count)] = (lat[pl.ds(first, count)].astype(F32) + value).astype(BF16)

    ring_step(1, gat2, 1, 0)
    out1_rows(0, 4)
    ring_step(1, gat2, 1, 1)
    out1_rows(4, 4)
    ring_step(1, gat2, 2, 0)
    out1_rows(8, 4)
    ring_step(1, gat2, 2, 1)
    out1_rows(12, 4)
    write1 = local(o1, out1_h, 7)
    write1.start()
    ring_step(1, gat2, 3, 0)
    ring_step(1, gat2, 3, 1)

    pick = jnp.where(iota((OC, C3), 1) == iota((OC, C3), 0) + col * OC, 1.0, 0.0).astype(BF16)

    def residual(i, carry):
        res[i] = lax.dot_general(pick, gat1[:, i].reshape(W3, C3), NT, preferred_element_type=F32)
        return carry

    lax.fori_loop(0, H3, residual, 0)
    bias3 = upright(c3b)
    ring_step(1, gat2, 4)
    for hop in range(5):
        mate_step(1, gat2, hop)

    loads["w3b"].wait()
    taps(w3b, lambda i: gat2[:, i].reshape(C3, W3), (((1,), (0,)), ((), ())))
    copies = edges_out(1)
    for i in range(H3):
        res[i] = res[i] + combine(i) + bias3
    for copy in copies:
        copy.wait()
    low, high = edges_in(1)
    res[0] = res[0] + low
    res[H3 - 1] = res[H3 - 1] + high
    for i in range(H3):
        o3[i] = res[i].astype(BF16)
    write3 = local(o3, out3_h, 8)
    write3.start()
    for copy in sends:
        copy.wait_send()
    write1.wait()
    write3.wait()


def body(
    latent1, norm1a_g, norm1a_b, conv1a_w, norm1b_g, norm1b_b, conv1b_w, conv1b_b,
    feat3, adapter3, norm3a_g, norm3a_b, conv3a_w, norm3b_g, norm3b_b, conv3b_w, conv3b_b,
):
    def wide(w):
        return w.reshape(3, 3 * C1, C1)

    def tall(w):
        return jnp.swapaxes(w, 2, 3).reshape(9 * OC, C3)

    any_spec = pl.BlockSpec(memory_space=pl.ANY)
    operands = [
        (latent1, any_spec), (norm1a_g, any_spec), (norm1a_b, any_spec), (wide(conv1a_w), any_spec),
        (norm1b_g, any_spec), (norm1b_b, any_spec), (wide(conv1b_w), any_spec), (conv1b_b, any_spec),
        (feat3, any_spec), (adapter3, any_spec), (norm3a_g, any_spec), (norm3a_b, any_spec),
        (tall(conv3a_w), any_spec), (norm3b_g, any_spec), (norm3b_b, any_spec),
        (tall(conv3b_w), any_spec), (conv3b_b, any_spec),
    ]
    out1, out3 = pl.pallas_call(
        kernel,
        out_shape=(
            jax.ShapeDtypeStruct((H1, W1, C1), BF16),
            jax.ShapeDtypeStruct((H3, OC, W3), BF16),
        ),
        in_specs=[spec for _, spec in operands],
        out_specs=(any_spec, any_spec),
        scratch_shapes=[
            *[pltpu.VMEM((n,), F32) for n in (C1, C1, C1, C1, C1, C3, C3, OC, OC, OC)],
            pltpu.VMEM((H1, W1, C1), BF16),
            pltpu.VMEM((2, W1, C1), BF16),
            pltpu.VMEM((2, W1, C1), BF16),
            pltpu.VMEM((2, 2, 24, C1), F32),
            pltpu.VMEM((2, 2, 24, C1), F32),
            pltpu.VMEM((H1 + 4, WP, 3 * C1), BF16),
            pltpu.VMEM((H1 + 2, WP, C1), F32),
            pltpu.VMEM((3, 3 * C1, C1), BF16),
            pltpu.VMEM((3, 3 * C1, C1), BF16),
            pltpu.VMEM((9 * OC, C3), BF16),
            pltpu.VMEM((9 * OC, C3), BF16),
            pltpu.VMEM((H3, 16, C3), BF16),
            pltpu.VMEM((H3, 16, C3), BF16),
            pltpu.VMEM((C, H3, 16, C3), BF16),
            pltpu.VMEM((C, H3, 16, C3), BF16),
            pltpu.VMEM((C, H3, OC, W3), BF16),
            pltpu.VMEM((H3, 9 * OC, W3), F32),
            pltpu.VMEM((2, 2, OC, W3), F32),
            pltpu.VMEM((2, 2, OC, W3), F32),
            pltpu.VMEM((H3, OC, W3), F32),
            pltpu.VMEM((H3, OC, W3), F32),
            pltpu.VMEM((H1, W1, C1), BF16),
            pltpu.VMEM((H3, OC, W3), BF16),
            pltpu.VMEM((16, 8, 128), F32),
            pltpu.VMEM((16, 8, 128), F32),
            pltpu.VMEM((16, 8, 128), F32),
            pltpu.VMEM((16, 8, 128), F32),
            pltpu.VMEM((16, 8, 128), F32),
            pltpu.SemaphoreType.DMA((19,)),
            pltpu.SemaphoreType.DMA((5,)),
            pltpu.SemaphoreType.DMA((5,)),
            pltpu.SemaphoreType.DMA((2, 2, 4, 2)),
            pltpu.SemaphoreType.DMA((2, 2, 4, 2)),
            pltpu.SemaphoreType.DMA((2, 2, 5, 2)),
            pltpu.SemaphoreType.DMA((2, 2, 5, 2)),
            pltpu.SemaphoreType.DMA((1,)),
            pltpu.SemaphoreType.DMA((4,)),
            pltpu.SemaphoreType.DMA((4,)),
            pltpu.SemaphoreType.DMA((2, 2)),
            pltpu.SemaphoreType.DMA((2, 2)),
        ],
        compiler_params=pltpu.CompilerParams(
            collective_id=0, has_side_effects=True, vmem_limit_bytes=56 * 1024 * 1024
        ),
    )(*[value for value, _ in operands])
    return out1, jnp.swapaxes(out3, 1, 2)


def solution(mesh):
    return jax.shard_map(
        body,
        mesh=mesh,
        in_specs=(
            P("rows", "cols", None), P(), P(), P(), P(), P(), P(), P(),
            P("rows", "cols", None), P("rows", "cols", None), P(), P(),
            P(None, None, None, "cols"), P("cols"), P("cols"), P(None, None, None, "cols"), P("cols"),
        ),
        out_specs=(P("rows", "cols", None), P("rows", None, "cols")),
        check_vma=False,
    )
```

```python
import functools

import jax
import jax.numpy as jnp
from jax import lax
from jax.experimental import pallas as pl
from jax.experimental.pallas import tpu as pltpu
from jax.sharding import PartitionSpec as P

MESH = pl.DeviceIdType.MESH
F32 = jnp.float32
BF16 = jnp.bfloat16
EPS = 1e-05
R, C = 16, 16
Z = 8
C1, C3, OC = 320, 1280, 80
H1, W1 = 16, 64
H3, W3 = 4, 256
WP = 80
ORDER = (1, 2, 0, 3)
NT = (((1,), (1,)), ((), ()))
COUNT1 = float(R * H1 * C * W1 * (C1 // 32))
COUNT3 = float(R * H3 * W3 * (C3 // 32))


def iota(shape, dim):
    return lax.broadcasted_iota(jnp.int32, shape, dim)


def group_matrix(chans, width, offset, dim):
    shape = (chans, 128) if dim == 0 else (128, chans)
    chan = iota(shape, dim)
    first = (iota(shape, 1 - dim) - offset) * width
    return jnp.where((chan >= first) & (chan < first + width), 1.0, 0.0).astype(BF16)


def exact_dot(a, ones):
    high = a.astype(BF16)
    rest = a - high.astype(F32)
    middle = rest.astype(BF16)
    low = (rest - middle.astype(F32)).astype(BF16)
    n = a.shape[0]
    out = jnp.dot(jnp.concatenate([high, middle, low], axis=0), ones, preferred_element_type=F32)
    return out[0:n] + out[n : 2 * n] + out[2 * n :]


def group_sums(sums, squares, ones, offset):
    both = exact_dot(jnp.concatenate([sums, squares], axis=0), ones)
    first = pltpu.roll(both[0:8], offset, 1) if offset else both[0:8]
    return first + pltpu.roll(both[8:16], offset + 32, 1)


def flat(ref):
    return ref[...].reshape(1, -1)


def halves(value):
    return value + value * jnp.tanh(value)


def kernel(
    lat_h, g1a_h, b1a_h, w1a_h, g1b_h, b1b_h, w1b_h, c1b_h,
    feat_h, adap_h, g3a_h, b3a_h, w3a_h, g3b_h, b3b_h, w3b_h, c3b_h,
    out1_h, out3_h,
    g1a, b1a, g1b, b1b, c1b, g3a, b3a, g3b, b3b, c3b,
    lat, top, bottom, pack, side, act, hid, w1a, w1b, w3a, w3b, feat, adap, gat1, act3, gat2, prod,
    edge_s, edge_r, hid3, res, o1, o3, st_a1, st_a2, st_b1, st_b2, st_c, st_d, act4,
    local_sem, ar_send, ar_recv, ring_send, ring_recv, mate_send, mate_recv,
    halo_send, halo_recv, edge_send, edge_recv,
):
    row = lax.axis_index("rows")
    col = lax.axis_index("cols")
    z = col // 2
    core = col % 2
    up = (row + R - 1) % R
    down = (row + 1) % R
    left = (col + C - 1) % C
    right = (col + 1) % C
    mate = z * 2 + (1 - core)

    def local(src, dst, index):
        return pltpu.make_async_copy(src, dst, local_sem.at[index])

    loads = {
        "feat": local(feat_h, feat, 0),
        "adap": local(adap_h, adap, 1),
        "lat": local(lat_h, lat, 2),
        "w1a": local(w1a_h, w1a, 3),
        "w3a": local(w3a_h, w3a, 4),
        "w1b": local(w1b_h, w1b, 5),
        "w3b": local(w3b_h, w3b, 6),
    }
    small = [
        local(src, dst, 9 + i)
        for i, (src, dst) in enumerate(
            (
                (g1a_h, g1a), (b1a_h, b1a), (g1b_h, g1b), (b1b_h, b1b), (c1b_h, c1b),
                (g3a_h, g3a), (b3a_h, b3a), (g3b_h, g3b), (b3b_h, b3b), (c3b_h, c3b),
            )
        )
    ]
    for name in ("feat", "adap", "lat"):
        loads[name].start()

    barrier = pltpu.get_barrier_semaphore()
    for step in range(1, R):
        pl.semaphore_signal(barrier, inc=1, device_id={"rows": (row + step) % R}, device_id_type=MESH)
    for step in range(1, C):
        pl.semaphore_signal(barrier, inc=1, device_id={"cols": (col + step) % C}, device_id_type=MESH)

    def spread(buf, axis, index):
        me = row if axis == "rows" else col

        def send(step, carry):
            pltpu.make_async_remote_copy(
                src_ref=buf.at[0],
                dst_ref=buf.at[step],
                send_sem=ar_send.at[index],
                recv_sem=ar_recv.at[index],
                device_id={axis: (me + step) % 16},
                device_id_type=MESH,
            ).start()
            return carry

        lax.fori_loop(1, 16, send, 0)

    def arrived(buf, axis, index):
        rest = pltpu.make_async_remote_copy(
            src_ref=buf.at[pl.ds(1, 15)],
            dst_ref=buf.at[pl.ds(1, 15)],
            send_sem=ar_send.at[index],
            recv_sem=ar_recv.at[index],
            device_id={axis: ((row if axis == "rows" else col) + 1) % 16},
            device_id_type=MESH,
        )
        rest.wait_recv()
        rest.wait_send()

    def collect(buf, axis, index):
        arrived(buf, axis, index)
        return jnp.sum(buf[...], axis=0)

    def origin(direction, hop):
        return (z + Z - hop) % Z if direction == 0 else (z + hop) % Z

    def chunk(gat, slot, half):
        return gat.at[slot, half]

    def ring_copy(which, gat, direction, hop, half):
        slot = 2 * origin(direction, hop - 1) + core
        target = 2 * ((z + 1) % Z if direction == 0 else (z + Z - 1) % Z) + core
        return pltpu.make_async_remote_copy(
            src_ref=chunk(gat, slot, half),
            dst_ref=chunk(gat, slot, half),
            send_sem=ring_send.at[which, direction, hop - 1, half],
            recv_sem=ring_recv.at[which, direction, hop - 1, half],
            device_id={"cols": target},
            device_id_type=MESH,
        )

    def ring_wait(which, gat, direction, hop, half):
        slot = 2 * origin(direction, hop) + core
        target = 2 * ((z + 1) % Z if direction == 0 else (z + Z - 1) % Z) + core
        pltpu.make_async_remote_copy(
            src_ref=chunk(gat, slot, half),
            dst_ref=chunk(gat, slot, half),
            send_sem=ring_send.at[which, direction, hop - 1, half],
            recv_sem=ring_recv.at[which, direction, hop - 1, half],
            device_id={"cols": target},
            device_id_type=MESH,
        ).wait_recv()

    def mate_copy(which, gat, direction, hop, half):
        slot = 2 * origin(direction, hop) + core
        return pltpu.make_async_remote_copy(
            src_ref=chunk(gat, slot, half),
            dst_ref=chunk(gat, slot, half),
            send_sem=mate_send.at[which, direction, hop, half],
            recv_sem=mate_recv.at[which, direction, hop, half],
            device_id={"cols": mate},
            device_id_type=MESH,
        )

    def mate_wait(which, gat, direction, hop, half):
        slot = 2 * origin(direction, hop) + (1 - core)
        pltpu.make_async_remote_copy(
            src_ref=chunk(gat, slot, half),
            dst_ref=chunk(gat, slot, half),
            send_sem=mate_send.at[which, direction, hop, half],
            recv_sem=mate_recv.at[which, direction, hop, half],
            device_id={"cols": mate},
            device_id_type=MESH,
        ).wait_recv()

    def arrivals(hop, k):
        if hop == 4:
            return [(0, 1 - k), (1, 2 + k)]
        return [(0, ORDER[k]), (1, ORDER[k])]

    def steps(hop):
        return range(2 if hop == 4 else H3)

    sends = []

    def go(copy):
        copy.start()
        sends.append(copy)

    def ring_start(which, gat, parts):
        for part in parts:
            for direction in range(2):
                go(ring_copy(which, gat, direction, 1, part))
        for part in parts:
            go(mate_copy(which, gat, 0, 0, part))

    def ring_step(which, gat, hop, *ks):
        last = [pair for k in range(2) for pair in arrivals(4, k)]
        for k in ks:
            for direction, part in arrivals(hop, k):
                ring_wait(which, gat, direction, hop, part)
                if hop < 3 or (hop == 3 and (direction, part) in last):
                    go(ring_copy(which, gat, direction, hop + 1, part))
                go(mate_copy(which, gat, direction, hop, part))

    def mate_step(which, gat, hop):
        if hop == 0:
            for part in range(H3):
                mate_wait(which, gat, 0, 0, part)
        else:
            for k in steps(hop):
                for direction, part in arrivals(hop, k):
                    mate_wait(which, gat, direction, hop, part)

    loads["feat"].wait()
    loads["adap"].wait()
    for copy in small:
        copy.start()
    for name in ("w1a", "w3a", "w1b", "w3b"):
        loads[name].start()
    js = jnp.zeros((8, C3), F32)
    jq = jnp.zeros((8, C3), F32)
    for i in range(H3):
        value = (feat[i].astype(F32) + adap[i].astype(F32)).astype(BF16)
        gat1[col, i] = value
        value = value.astype(F32).reshape(2, 8, C3)
        js = js + jnp.sum(value, axis=0)
        jq = jq + jnp.sum(value * value, axis=0)

    pl.semaphore_wait(barrier, R - 1 + C - 1)
    ring_start(0, gat1, ORDER)
    joined_sums = group_sums(js, jq, group_matrix(C3, 40, 0, 0), 64)

    loads["lat"].wait()

    def halo_copy(src, dst, index, target):
        return pltpu.make_async_remote_copy(
            src_ref=src,
            dst_ref=dst,
            send_sem=halo_send.at[index],
            recv_sem=halo_recv.at[index],
            device_id=target,
            device_id_type=MESH,
        )

    to_down = halo_copy(lat.at[pl.ds(H1 - 2, 2)], top, 0, {"rows": down})
    to_up = halo_copy(lat.at[pl.ds(0, 2)], bottom, 1, {"rows": up})
    to_down.start()
    to_up.start()

    ls = jnp.zeros((8, C1), F32)
    lq = jnp.zeros((8, C1), F32)
    for i in range(H1):
        value = lat[i].astype(F32).reshape(8, 8, C1)
        ls = ls + jnp.sum(value, axis=0)
        lq = lq + jnp.sum(value * value, axis=0)
    ones1 = group_matrix(C1, 10, 0, 0)
    st_a1[0] = group_sums(ls, lq, ones1, 0) + joined_sums
    spread(st_a1, "rows", 0)

    to_down.wait()
    to_up.wait()

    def extended_row(i):
        if i < 2:
            return top[i]
        if i < H1 + 2:
            return lat[i - 2]
        return bottom[i - H1 - 2]

    for block in range(3):
        rows_here = [i for i in range(8 * block, 8 * block + 8) if i < H1 + 4]
        tiles = [jnp.zeros((8, C1), F32) for _ in range(4)]
        for i in rows_here:
            value = extended_row(i)
            first = value[0:16].astype(F32)
            last = value[48:64].astype(F32)
            here = iota((8, C1), 0) == i - 8 * block
            for j, piece in enumerate((last[14:15], last[15:16], first[0:1], first[1:2])):
                tiles[j] = jnp.where(here, jnp.broadcast_to(piece, (8, C1)), tiles[j])
        for j in range(4):
            pack[j // 2, j % 2, pl.ds(8 * block, 8), :] = tiles[j]
    to_right = halo_copy(pack.at[0], side.at[0], 2, {"cols": right})
    to_left = halo_copy(pack.at[1], side.at[1], 3, {"cols": left})
    to_right.start()
    to_left.start()

    ring_step(0, gat1, 1, 0, 1)
    st_a2[0] = collect(st_a1, "rows", 0)
    spread(st_a2, "cols", 1)
    ring_step(0, gat1, 1, 2, 3)

    def group_rates(total):
        total = jnp.sum(total, axis=0, keepdims=True)
        total = jnp.broadcast_to(total, (8, 128))
        lane = iota((8, 128), 1)
        count = jnp.where(lane < 64, COUNT1, COUNT3)
        squares = pltpu.roll(total, 96, 1)
        mean = total / count
        spread_of = squares / count - mean * mean
        live = (lane < 32) | ((lane >= 64) & (lane < 96))
        inverse = lax.rsqrt(jnp.where(live, spread_of, 1.0) + EPS)
        return jnp.where(live, mean, 0.0), jnp.where(live, inverse, 0.0)

    def channel_rates(rates, matrix, gain, shift):
        both = exact_dot(jnp.where(iota((8, 128), 0) == 0, *rates), matrix)
        mean, inverse = both[0:1], both[1:2]
        scale = inverse * gain
        return 0.5 * scale, 0.5 * (shift - mean * scale)

    for copy in small:
        copy.wait()
    rates = group_rates(collect(st_a2, "cols", 1))
    scale1, shift1 = channel_rates(rates, group_matrix(C1, 10, 0, 1), flat(g1a), flat(b1a))

    def put_row(i, value, live):
        value = jnp.where(live, halves(value), 0.0)
        act[i, :, 0:C1] = pltpu.roll(value, 1, 0).astype(BF16)
        act[i, :, C1 : 2 * C1] = value.astype(BF16)
        act[i, :, 2 * C1 : 3 * C1] = pltpu.roll(value, WP - 1, 0).astype(BF16)

    place = iota((WP, C1), 0)

    to_right.wait()
    to_left.wait()
    slab_place = iota((16, C1), 0)
    wide_ok = (place < W1) | ((place < W1 + 2) & (col < C - 1)) | ((place >= WP - 2) & (col > 0))

    def act1_rows(first, last):
        for i in range(first, last):
            slab = jnp.zeros((16, C1), F32)
            base = 8 * (i // 8)
            for target, which, j in ((0, 1, 0), (1, 1, 1), (14, 0, 0), (15, 0, 1)):
                piece = side[which, j, pl.ds(base, 8), :][i - base : i - base + 1]
                slab = jnp.where(slab_place == target, jnp.broadcast_to(piece, (16, C1)), slab)
            value = jnp.concatenate([extended_row(i).astype(F32), slab], axis=0)
            live = wide_ok
            if i < 2:
                live = live & (row > 0)
            if i >= H1 + 2:
                live = live & (row < R - 1)
            put_row(i, value * scale1 + shift1, live)

    ring_step(0, gat1, 2, 0, 1)
    act1_rows(0, 20)
    ring_step(0, gat1, 2, 2, 3)

    def conv1(weights, first, count, width):
        total = None
        for dy in range(3):
            block = act[pl.ds(first + dy, count), 0:width, :].reshape(count * width, 3 * C1)
            part = jnp.dot(block, weights[dy], preferred_element_type=F32)
            total = part if total is None else total + part
        return total.reshape(count, width, C1)

    def norm3(slot):
        for i in range(H3):
            value = gat1[slot, i].astype(F32) * scale3 + shift3
            act3[slot, i] = halves(value).astype(BF16)

    def norm3_hop(hop):
        mate_step(0, gat1, hop)
        for direction in range(1 if hop in (0, 4) else 2):
            for k in range(2):
                norm3(2 * origin(direction, hop) + k)

    loads["w1a"].wait()
    hid[pl.ds(0, 6)] = conv1(w1a, 0, 6, WP)
    scale3, shift3 = channel_rates(rates, group_matrix(C3, 40, 64, 1), flat(g3a), flat(b3a))
    ring_step(0, gat1, 3, 0, 1)
    hid[pl.ds(6, 6)] = conv1(w1a, 6, 6, WP)
    norm3_hop(0)
    ring_step(0, gat1, 3, 2, 3)
    hid[pl.ds(12, 6)] = conv1(w1a, 12, 6, WP)
    norm3_hop(1)
    ring_step(0, gat1, 4, 0, 1)

    hs = jnp.zeros((8, C1), F32)
    hq = jnp.zeros((8, C1), F32)
    for i in range(H1):
        value = hid[i + 1, 0:W1, :].reshape(8, 8, C1)
        hs = hs + jnp.sum(value, axis=0)
        hq = hq + jnp.sum(value * value, axis=0)
    st_b1[0] = group_sums(hs, hq, ones1, 0)
    spread(st_b1, "rows", 2)

    norm3_hop(2)
    norm3_hop(3)
    norm3_hop(4)

    def taps(weights, source, dims, rows_of):
        for i in rows_of:
            prod[i] = lax.dot_general(weights[...], source(i), dims, preferred_element_type=F32)

    lane3 = iota((OC, W3), 1)

    def combine(target):
        columns = []
        for dx in range(3):
            total = None
            for dy in range(3):
                i = target + dy - 1
                if 0 <= i < H3:
                    part = prod[i, pl.ds((3 * dy + dx) * OC, OC), :]
                    total = part if total is None else total + part
            columns.append(total)
        before = jnp.where(lane3 == 0, 0.0, pltpu.roll(columns[0], 1, 1))
        after = jnp.where(lane3 == W3 - 1, 0.0, pltpu.roll(columns[2], W3 - 1, 1))
        return before + columns[1] + after

    def edge_copies(which):
        return [
            pltpu.make_async_remote_copy(
                src_ref=edge_s.at[which, j],
                dst_ref=edge_r.at[which, j],
                send_sem=edge_send.at[which, j],
                recv_sem=edge_recv.at[which, j],
                device_id={"rows": target},
                device_id_type=MESH,
            )
            for j, target in ((0, down), (1, up))
        ]

    def edges_out(which):
        edge_s[which, 0] = combine(H3)
        edge_s[which, 1] = combine(-1)
        copies = edge_copies(which)
        for copy in copies:
            copy.start()
        return copies

    def edges_in(which):
        low = jnp.where(row > 0, edge_r[which, 0], 0.0)
        high = jnp.where(row < R - 1, edge_r[which, 1], 0.0)
        return low, high

    loads["w3a"].wait()
    taps(w3a, lambda i: act3[:, i].reshape(W3, C3), NT, (0, 3))
    copies = edges_out(0)
    taps(w3a, lambda i: act3[:, i].reshape(W3, C3), NT, (1, 2))
    for i in (1, 2):
        value = combine(i)
        hid3[i] = value
        gat2[col, i] = value.astype(BF16)
    ring_start(1, gat2, (1, 2))
    st_b2[0] = collect(st_b1, "rows", 2)
    spread(st_b2, "cols", 3)
    for i in (0, 3):
        hid3[i] = combine(i)
    for copy in copies:
        copy.wait()
    for i, border in zip((0, 3), edges_in(0)):
        value = hid3[i] + border
        hid3[i] = value
        gat2[col, i] = value.astype(BF16)
    ring_start(1, gat2, (0, 3))

    fs = jnp.zeros((OC, W3), F32)
    fq = jnp.zeros((OC, W3), F32)
    for i in range(H3):
        value = hid3[i]
        fs = fs + value
        fq = fq + value * value
    fs = jnp.sum(fs, axis=1, keepdims=True)
    fq = jnp.sum(fq, axis=1, keepdims=True)
    lane = iota((OC, 128), 1)
    second = iota((OC, 128), 0) >= OC // 2
    group = jnp.where(second, 1, 0)
    laid = jnp.where(lane == group, fs, 0.0) + jnp.where(lane == group + 2, fq, 0.0)
    st_c[0] = jnp.sum(laid.reshape(OC // 8, 8, 128), axis=0)
    spread(st_c, "rows", 4)

    rates = group_rates(collect(st_b2, "cols", 3))
    scale2, shift2 = channel_rates(rates, group_matrix(C1, 10, 0, 1), flat(g1b), flat(b1b))
    near_ok = (place < W1) | ((place == W1) & (col < C - 1)) | ((place == WP - 1) & (col > 0))

    def act2_rows(first, last):
        for i in range(first, last):
            live = near_ok
            if i == 0:
                live = live & (row > 0)
            if i == H1 + 1:
                live = live & (row < R - 1)
            put_row(i, hid[i] * scale2 + shift2, live)

    ring_step(1, gat2, 1, 0, 1)
    act2_rows(0, 9)

    total = jnp.sum(collect(st_c, "rows", 4), axis=0, keepdims=True)
    total = jnp.broadcast_to(total, (OC, 128)) / COUNT3
    mean = jnp.sum(jnp.where(lane == group, total, 0.0), axis=1, keepdims=True)
    square = jnp.sum(jnp.where(lane == group + 2, total, 0.0), axis=1, keepdims=True)
    inverse = lax.rsqrt(square - mean * mean + EPS)

    def upright(ref):
        eye = iota((OC, OC), 0) == iota((OC, OC), 1)
        return jnp.sum(jnp.where(eye, jnp.broadcast_to(flat(ref), (OC, OC)), 0.0), axis=1, keepdims=True)

    scale4 = inverse * upright(g3b)
    shift4 = 0.5 * (upright(b3b) - mean * scale4)
    scale4 = 0.5 * scale4
    eye = iota((OC, 128), 0) == iota((OC, 128), 1)
    as_rows = [jnp.sum(jnp.where(eye, x, 0.0), axis=0, keepdims=True) for x in (scale4, shift4)]
    st_d[0] = jnp.where(iota((8, 128), 0) == 0, *as_rows)
    spread(st_d, "cols", 5)

    act2_rows(9, 18)
    ring_step(1, gat2, 1, 2, 3)
    loads["w1b"].wait()

    def norm4(slot):
        block = st_d[(col + C - slot) % C]
        scale, shift = (jnp.sum(jnp.where(eye, block[j : j + 1], 0.0), axis=1, keepdims=True) for j in range(2))
        for i in range(H3):
            act4[slot, i] = halves(gat2[slot, i].astype(F32) * scale + shift).astype(BF16)

    def norm4_hop(hop):
        mate_step(1, gat2, hop)
        for direction in range(1 if hop in (0, 4) else 2):
            for k in range(2):
                norm4(2 * origin(direction, hop) + k)

    def out1_rows(first, count):
        value = conv1(w1b, first, count, W1) + flat(c1b).reshape(1, 1, C1)
        o1[pl.ds(first, count)] = (lat[pl.ds(first, count)].astype(F32) + value).astype(BF16)

    out1_rows(0, 4)
    ring_step(1, gat2, 2, 0, 1)
    arrived(st_d, "cols", 5)
    norm4_hop(0)
    out1_rows(4, 4)
    ring_step(1, gat2, 2, 2, 3)
    out1_rows(8, 4)
    norm4_hop(1)
    ring_step(1, gat2, 3, 0, 1)
    out1_rows(12, 4)
    write1 = local(o1, out1_h, 7)
    write1.start()
    ring_step(1, gat2, 3, 2, 3)

    pick = jnp.where(iota((OC, C3), 1) == iota((OC, C3), 0) + col * OC, 1.0, 0.0).astype(BF16)

    def residual(i, carry):
        res[i] = lax.dot_general(pick, gat1[:, i].reshape(W3, C3), NT, preferred_element_type=F32)
        return carry

    lax.fori_loop(0, H3, residual, 0)
    bias3 = upright(c3b)
    norm4_hop(2)
    ring_step(1, gat2, 4, 0, 1)
    norm4_hop(3)
    norm4_hop(4)

    loads["w3b"].wait()
    taps(w3b, lambda i: act4[:, i].reshape(C3, W3), (((1,), (0,)), ((), ())), (0, 3))
    copies = edges_out(1)
    taps(w3b, lambda i: act4[:, i].reshape(C3, W3), (((1,), (0,)), ((), ())), (1, 2))
    for i in range(H3):
        res[i] = res[i] + combine(i) + bias3
    for copy in copies:
        copy.wait()
    low, high = edges_in(1)
    res[0] = res[0] + low
    res[H3 - 1] = res[H3 - 1] + high
    for i in range(H3):
        o3[i] = res[i].astype(BF16)
    write3 = local(o3, out3_h, 8)
    write3.start()
    for copy in sends:
        copy.wait_send()
    write1.wait()
    write3.wait()


def body(
    latent1, norm1a_g, norm1a_b, conv1a_w, norm1b_g, norm1b_b, conv1b_w, conv1b_b,
    feat3, adapter3, norm3a_g, norm3a_b, conv3a_w, norm3b_g, norm3b_b, conv3b_w, conv3b_b,
):
    def wide(w):
        return w.reshape(3, 3 * C1, C1)

    def tall(w):
        return jnp.swapaxes(w, 2, 3).reshape(9 * OC, C3)

    any_spec = pl.BlockSpec(memory_space=pl.ANY)
    operands = [
        (latent1, any_spec), (norm1a_g, any_spec), (norm1a_b, any_spec), (wide(conv1a_w), any_spec),
        (norm1b_g, any_spec), (norm1b_b, any_spec), (wide(conv1b_w), any_spec), (conv1b_b, any_spec),
        (feat3, any_spec), (adapter3, any_spec), (norm3a_g, any_spec), (norm3a_b, any_spec),
        (tall(conv3a_w), any_spec), (norm3b_g, any_spec), (norm3b_b, any_spec),
        (tall(conv3b_w), any_spec), (conv3b_b, any_spec),
    ]
    out1, out3 = pl.pallas_call(
        kernel,
        out_shape=(
            jax.ShapeDtypeStruct((H1, W1, C1), BF16),
            jax.ShapeDtypeStruct((H3, OC, W3), BF16),
        ),
        in_specs=[spec for _, spec in operands],
        out_specs=(any_spec, any_spec),
        scratch_shapes=[
            *[pltpu.VMEM((n,), F32) for n in (C1, C1, C1, C1, C1, C3, C3, OC, OC, OC)],
            pltpu.VMEM((H1, W1, C1), BF16),
            pltpu.VMEM((2, W1, C1), BF16),
            pltpu.VMEM((2, W1, C1), BF16),
            pltpu.VMEM((2, 2, 24, C1), F32),
            pltpu.VMEM((2, 2, 24, C1), F32),
            pltpu.VMEM((H1 + 4, WP, 3 * C1), BF16),
            pltpu.VMEM((H1 + 2, WP, C1), F32),
            pltpu.VMEM((3, 3 * C1, C1), BF16),
            pltpu.VMEM((3, 3 * C1, C1), BF16),
            pltpu.VMEM((9 * OC, C3), BF16),
            pltpu.VMEM((9 * OC, C3), BF16),
            pltpu.VMEM((H3, 16, C3), BF16),
            pltpu.VMEM((H3, 16, C3), BF16),
            pltpu.VMEM((C, H3, 16, C3), BF16),
            pltpu.VMEM((C, H3, 16, C3), BF16),
            pltpu.VMEM((C, H3, OC, W3), BF16),
            pltpu.VMEM((H3, 9 * OC, W3), F32),
            pltpu.VMEM((2, 2, OC, W3), F32),
            pltpu.VMEM((2, 2, OC, W3), F32),
            pltpu.VMEM((H3, OC, W3), F32),
            pltpu.VMEM((H3, OC, W3), F32),
            pltpu.VMEM((H1, W1, C1), BF16),
            pltpu.VMEM((H3, OC, W3), BF16),
            pltpu.VMEM((16, 8, 128), F32),
            pltpu.VMEM((16, 8, 128), F32),
            pltpu.VMEM((16, 8, 128), F32),
            pltpu.VMEM((16, 8, 128), F32),
            pltpu.VMEM((16, 8, 128), F32),
            pltpu.VMEM((16, 8, 128), F32),
            pltpu.VMEM((C, H3, OC, W3), BF16),
            pltpu.SemaphoreType.DMA((19,)),
            pltpu.SemaphoreType.DMA((6,)),
            pltpu.SemaphoreType.DMA((6,)),
            pltpu.SemaphoreType.DMA((2, 2, 4, 4)),
            pltpu.SemaphoreType.DMA((2, 2, 4, 4)),
            pltpu.SemaphoreType.DMA((2, 2, 5, 4)),
            pltpu.SemaphoreType.DMA((2, 2, 5, 4)),
            pltpu.SemaphoreType.DMA((4,)),
            pltpu.SemaphoreType.DMA((4,)),
            pltpu.SemaphoreType.DMA((2, 2)),
            pltpu.SemaphoreType.DMA((2, 2)),
        ],
        compiler_params=pltpu.CompilerParams(
            collective_id=0, has_side_effects=True, vmem_limit_bytes=56 * 1024 * 1024
        ),
    )(*[value for value, _ in operands])
    return out1, jnp.swapaxes(out3, 1, 2)


def solution(mesh):
    return jax.shard_map(
        body,
        mesh=mesh,
        in_specs=(
            P("rows", "cols", None), P(), P(), P(), P(), P(), P(), P(),
            P("rows", "cols", None), P("rows", "cols", None), P(), P(),
            P(None, None, None, "cols"), P("cols"), P("cols"), P(None, None, None, "cols"), P("cols"),
        ),
        out_specs=(P("rows", "cols", None), P("rows", None, "cols")),
        check_vma=False,
    )
```

```python
import functools

import jax
import jax.numpy as jnp
from jax import lax
from jax.experimental import pallas as pl
from jax.experimental.pallas import tpu as pltpu
from jax.sharding import PartitionSpec as P

MESH = pl.DeviceIdType.MESH
F32 = jnp.float32
BF16 = jnp.bfloat16
EPS = 1e-05
R, C = 16, 16
Z = 8
C1, C3, OC = 320, 1280, 80
H1, W1 = 16, 64
H3, W3 = 4, 256
WP = 80
ORDER = (1, 2, 0, 3)
NT = (((1,), (1,)), ((), ()))
COUNT1 = float(R * H1 * C * W1 * (C1 // 32))
COUNT3 = float(R * H3 * W3 * (C3 // 32))


def iota(shape, dim):
    return lax.broadcasted_iota(jnp.int32, shape, dim)


def group_matrix(chans, width, offset, dim):
    shape = (chans, 128) if dim == 0 else (128, chans)
    chan = iota(shape, dim)
    first = (iota(shape, 1 - dim) - offset) * width
    return jnp.where((chan >= first) & (chan < first + width), 1.0, 0.0).astype(BF16)


def exact_dot(a, ones):
    high = a.astype(BF16)
    rest = a - high.astype(F32)
    middle = rest.astype(BF16)
    low = (rest - middle.astype(F32)).astype(BF16)
    n = a.shape[0]
    out = jnp.dot(jnp.concatenate([high, middle, low], axis=0), ones, preferred_element_type=F32)
    return out[0:n] + out[n : 2 * n] + out[2 * n :]


def group_sums(sums, squares, ones, offset):
    both = exact_dot(jnp.concatenate([sums, squares], axis=0), ones)
    first = pltpu.roll(both[0:8], offset, 1) if offset else both[0:8]
    return first + pltpu.roll(both[8:16], offset + 32, 1)


def flat(ref):
    return ref[...].reshape(1, -1)


def halves(value):
    return value + value * jnp.tanh(value)


def kernel(
    lat_h, g1a_h, b1a_h, w1a_h, g1b_h, b1b_h, w1b_h, c1b_h,
    feat_h, adap_h, g3a_h, b3a_h, w3a_h, g3b_h, b3b_h, w3b_h, c3b_h,
    out1_h, out3_h,
    g1a, b1a, g1b, b1b, c1b, g3a, b3a, g3b, b3b, c3b,
    lat, top, bottom, pack, side, act, hid, w1a, w1b, w3a, w3b, feat, adap, gat1, act3, gat2, prod,
    edge_s, edge_r, hid3, res, o1, o3, st_a1, st_a2, st_b1, st_b2, st_c, st_d, act4,
    local_sem, ar_send, ar_recv, ring_send, ring_recv, mate_send, mate_recv,
    halo_send, halo_recv, edge_send, edge_recv,
):
    row = lax.axis_index("rows")
    col = lax.axis_index("cols")
    z = col // 2
    core = col % 2
    up = (row + R - 1) % R
    down = (row + 1) % R
    left = (col + C - 1) % C
    right = (col + 1) % C
    mate = z * 2 + (1 - core)

    def local(src, dst, index):
        return pltpu.make_async_copy(src, dst, local_sem.at[index])

    loads = {
        "feat": local(feat_h, feat, 0),
        "adap": local(adap_h, adap, 1),
        "lat": local(lat_h, lat, 2),
        "w1a": local(w1a_h, w1a, 3),
        "w3a": local(w3a_h, w3a, 4),
        "w1b": local(w1b_h, w1b, 5),
        "w3b": local(w3b_h, w3b, 6),
    }
    small = [
        local(src, dst, 9 + i)
        for i, (src, dst) in enumerate(
            (
                (g1a_h, g1a), (b1a_h, b1a), (g1b_h, g1b), (b1b_h, b1b), (c1b_h, c1b),
                (g3a_h, g3a), (b3a_h, b3a), (g3b_h, g3b), (b3b_h, b3b), (c3b_h, c3b),
            )
        )
    ]
    for name in ("feat", "adap", "lat"):
        loads[name].start()

    barrier = pltpu.get_barrier_semaphore()
    for step in range(1, R):
        pl.semaphore_signal(barrier, inc=1, device_id={"rows": (row + step) % R}, device_id_type=MESH)
    for step in range(1, C):
        pl.semaphore_signal(barrier, inc=1, device_id={"cols": (col + step) % C}, device_id_type=MESH)

    def spread(buf, axis, index):
        me = row if axis == "rows" else col

        def send(step, carry):
            pltpu.make_async_remote_copy(
                src_ref=buf.at[0],
                dst_ref=buf.at[step],
                send_sem=ar_send.at[index],
                recv_sem=ar_recv.at[index],
                device_id={axis: (me + step) % 16},
                device_id_type=MESH,
            ).start()
            return carry

        lax.fori_loop(1, 16, send, 0)

    def arrived(buf, axis, index):
        rest = pltpu.make_async_remote_copy(
            src_ref=buf.at[pl.ds(1, 15)],
            dst_ref=buf.at[pl.ds(1, 15)],
            send_sem=ar_send.at[index],
            recv_sem=ar_recv.at[index],
            device_id={axis: ((row if axis == "rows" else col) + 1) % 16},
            device_id_type=MESH,
        )
        rest.wait_recv()
        rest.wait_send()

    def collect(buf, axis, index):
        arrived(buf, axis, index)
        return jnp.sum(buf[...], axis=0)

    def origin(direction, hop):
        return (z + Z - hop) % Z if direction == 0 else (z + hop) % Z

    def chunk(gat, slot, half):
        return gat.at[slot, half]

    def ring_copy(which, gat, direction, hop, half):
        slot = 2 * origin(direction, hop - 1) + core
        target = 2 * ((z + 1) % Z if direction == 0 else (z + Z - 1) % Z) + core
        return pltpu.make_async_remote_copy(
            src_ref=chunk(gat, slot, half),
            dst_ref=chunk(gat, slot, half),
            send_sem=ring_send.at[which, direction, hop - 1, half],
            recv_sem=ring_recv.at[which, direction, hop - 1, half],
            device_id={"cols": target},
            device_id_type=MESH,
        )

    def ring_wait(which, gat, direction, hop, half):
        slot = 2 * origin(direction, hop) + core
        target = 2 * ((z + 1) % Z if direction == 0 else (z + Z - 1) % Z) + core
        pltpu.make_async_remote_copy(
            src_ref=chunk(gat, slot, half),
            dst_ref=chunk(gat, slot, half),
            send_sem=ring_send.at[which, direction, hop - 1, half],
            recv_sem=ring_recv.at[which, direction, hop - 1, half],
            device_id={"cols": target},
            device_id_type=MESH,
        ).wait_recv()

    def whole(gat, slot, direction, hop):
        if hop == 4:
            return gat.at[slot, pl.ds(2 * direction, 2)]
        return gat.at[slot]

    def mate_copy(which, gat, direction, hop, side_core):
        part = whole(gat, 2 * origin(direction, hop) + side_core, direction, hop)
        return pltpu.make_async_remote_copy(
            src_ref=part,
            dst_ref=part,
            send_sem=mate_send.at[which, direction, hop],
            recv_sem=mate_recv.at[which, direction, hop],
            device_id={"cols": mate},
            device_id_type=MESH,
        )

    def arrivals(hop, k):
        if hop == 4:
            return [(0, 1 - k), (1, 2 + k)]
        return [(0, ORDER[k]), (1, ORDER[k])]

    def steps(hop):
        return range(2 if hop == 4 else H3)

    sends = []

    def go(copy):
        copy.start()
        sends.append(copy)

    def ring_start(which, gat, parts):
        for part in parts:
            for direction in range(2):
                go(ring_copy(which, gat, direction, 1, part))
        if 3 in parts:
            go(mate_copy(which, gat, 0, 0, core))

    def ring_step(which, gat, hop, *ks):
        last = [pair for k in range(2) for pair in arrivals(4, k)]
        for k in ks:
            for direction, part in arrivals(hop, k):
                ring_wait(which, gat, direction, hop, part)
                if hop < 3 or (hop == 3 and (direction, part) in last):
                    go(ring_copy(which, gat, direction, hop + 1, part))
                if k == steps(hop)[-1]:
                    go(mate_copy(which, gat, direction, hop, core))

    def mate_step(which, gat, hop):
        for direction in range(1 if hop == 0 else 2):
            mate_copy(which, gat, direction, hop, 1 - core).wait_recv()

    loads["feat"].wait()
    loads["adap"].wait()
    for copy in small:
        copy.start()
    for name in ("w1a", "w3a", "w1b", "w3b"):
        loads[name].start()
    js = jnp.zeros((8, C3), F32)
    jq = jnp.zeros((8, C3), F32)
    for i in range(H3):
        value = (feat[i].astype(F32) + adap[i].astype(F32)).astype(BF16)
        gat1[col, i] = value
        value = value.astype(F32).reshape(2, 8, C3)
        js = js + jnp.sum(value, axis=0)
        jq = jq + jnp.sum(value * value, axis=0)

    pl.semaphore_wait(barrier, R - 1 + C - 1)
    ring_start(0, gat1, ORDER)
    joined_sums = group_sums(js, jq, group_matrix(C3, 40, 0, 0), 64)

    loads["lat"].wait()

    def halo_copy(src, dst, index, target):
        return pltpu.make_async_remote_copy(
            src_ref=src,
            dst_ref=dst,
            send_sem=halo_send.at[index],
            recv_sem=halo_recv.at[index],
            device_id=target,
            device_id_type=MESH,
        )

    to_down = halo_copy(lat.at[pl.ds(H1 - 2, 2)], top, 0, {"rows": down})
    to_up = halo_copy(lat.at[pl.ds(0, 2)], bottom, 1, {"rows": up})
    to_down.start()
    to_up.start()

    ls = jnp.zeros((8, C1), F32)
    lq = jnp.zeros((8, C1), F32)
    for i in range(H1):
        value = lat[i].astype(F32).reshape(8, 8, C1)
        ls = ls + jnp.sum(value, axis=0)
        lq = lq + jnp.sum(value * value, axis=0)
    ones1 = group_matrix(C1, 10, 0, 0)
    st_a1[0] = group_sums(ls, lq, ones1, 0) + joined_sums
    spread(st_a1, "rows", 0)
    ring_step(0, gat1, 1, 0, 1)

    to_down.wait()
    to_up.wait()

    def extended_row(i):
        if i < 2:
            return top[i]
        if i < H1 + 2:
            return lat[i - 2]
        return bottom[i - H1 - 2]

    for block in range(3):
        rows_here = [i for i in range(8 * block, 8 * block + 8) if i < H1 + 4]
        tiles = [jnp.zeros((8, C1), F32) for _ in range(4)]
        for i in rows_here:
            value = extended_row(i)
            first = value[0:16].astype(F32)
            last = value[48:64].astype(F32)
            here = iota((8, C1), 0) == i - 8 * block
            for j, piece in enumerate((last[14:15], last[15:16], first[0:1], first[1:2])):
                tiles[j] = jnp.where(here, jnp.broadcast_to(piece, (8, C1)), tiles[j])
        for j in range(4):
            pack[j // 2, j % 2, pl.ds(8 * block, 8), :] = tiles[j]
    to_right = halo_copy(pack.at[0], side.at[0], 2, {"cols": right})
    to_left = halo_copy(pack.at[1], side.at[1], 3, {"cols": left})
    to_right.start()
    to_left.start()

    ring_step(0, gat1, 1, 2, 3)
    st_a2[0] = collect(st_a1, "rows", 0)
    spread(st_a2, "cols", 1)
    ring_step(0, gat1, 2, 0, 1, 2, 3)
    to_right.wait()
    to_left.wait()
    ring_step(0, gat1, 3, 0, 1)

    def group_rates(total):
        total = jnp.sum(total, axis=0, keepdims=True)
        total = jnp.broadcast_to(total, (8, 128))
        lane = iota((8, 128), 1)
        count = jnp.where(lane < 64, COUNT1, COUNT3)
        squares = pltpu.roll(total, 96, 1)
        mean = total / count
        spread_of = squares / count - mean * mean
        live = (lane < 32) | ((lane >= 64) & (lane < 96))
        inverse = lax.rsqrt(jnp.where(live, spread_of, 1.0) + EPS)
        return jnp.where(live, mean, 0.0), jnp.where(live, inverse, 0.0)

    def channel_rates(rates, matrix, gain, shift):
        both = exact_dot(jnp.where(iota((8, 128), 0) == 0, *rates), matrix)
        mean, inverse = both[0:1], both[1:2]
        scale = inverse * gain
        return 0.5 * scale, 0.5 * (shift - mean * scale)

    for copy in small:
        copy.wait()
    rates = group_rates(collect(st_a2, "cols", 1))
    scale1, shift1 = channel_rates(rates, group_matrix(C1, 10, 0, 1), flat(g1a), flat(b1a))

    def put_row(i, value, live):
        value = jnp.where(live, halves(value), 0.0)
        act[i, :, 0:C1] = pltpu.roll(value, 1, 0).astype(BF16)
        act[i, :, C1 : 2 * C1] = value.astype(BF16)
        act[i, :, 2 * C1 : 3 * C1] = pltpu.roll(value, WP - 1, 0).astype(BF16)

    place = iota((WP, C1), 0)

    slab_place = iota((16, C1), 0)
    wide_ok = (place < W1) | ((place < W1 + 2) & (col < C - 1)) | ((place >= WP - 2) & (col > 0))

    def act1_rows(first, last):
        for i in range(first, last):
            slab = jnp.zeros((16, C1), F32)
            base = 8 * (i // 8)
            for target, which, j in ((0, 1, 0), (1, 1, 1), (14, 0, 0), (15, 0, 1)):
                piece = side[which, j, pl.ds(base, 8), :][i - base : i - base + 1]
                slab = jnp.where(slab_place == target, jnp.broadcast_to(piece, (16, C1)), slab)
            value = jnp.concatenate([extended_row(i).astype(F32), slab], axis=0)
            live = wide_ok
            if i < 2:
                live = live & (row > 0)
            if i >= H1 + 2:
                live = live & (row < R - 1)
            put_row(i, value * scale1 + shift1, live)

    act1_rows(0, 20)
    ring_step(0, gat1, 3, 2, 3)

    def conv1(weights, first, count, width):
        total = None
        for dy in range(3):
            block = act[pl.ds(first + dy, count), 0:width, :].reshape(count * width, 3 * C1)
            part = jnp.dot(block, weights[dy], preferred_element_type=F32)
            total = part if total is None else total + part
        return total.reshape(count, width, C1)

    def norm3(slot):
        for i in range(H3):
            value = gat1[slot, i].astype(F32) * scale3 + shift3
            act3[slot, i] = halves(value).astype(BF16)

    def norm3_hop(hop):
        mate_step(0, gat1, hop)
        for direction in range(1 if hop in (0, 4) else 2):
            for k in range(2):
                norm3(2 * origin(direction, hop) + k)

    loads["w1a"].wait()
    hid[pl.ds(0, 6)] = conv1(w1a, 0, 6, WP)
    scale3, shift3 = channel_rates(rates, group_matrix(C3, 40, 64, 1), flat(g3a), flat(b3a))
    norm3_hop(0)
    norm3_hop(1)
    ring_step(0, gat1, 4, 0, 1)
    hid[pl.ds(6, 6)] = conv1(w1a, 6, 6, WP)
    norm3_hop(2)
    hid[pl.ds(12, 6)] = conv1(w1a, 12, 6, WP)

    hs = jnp.zeros((8, C1), F32)
    hq = jnp.zeros((8, C1), F32)
    for i in range(H1):
        value = hid[i + 1, 0:W1, :].reshape(8, 8, C1)
        hs = hs + jnp.sum(value, axis=0)
        hq = hq + jnp.sum(value * value, axis=0)
    st_b1[0] = group_sums(hs, hq, ones1, 0)
    spread(st_b1, "rows", 2)

    norm3_hop(3)
    norm3_hop(4)

    def taps(weights, source, dims, rows_of):
        for i in rows_of:
            prod[i] = lax.dot_general(weights[...], source(i), dims, preferred_element_type=F32)

    lane3 = iota((OC, W3), 1)

    def combine(target):
        columns = []
        for dx in range(3):
            total = None
            for dy in range(3):
                i = target + dy - 1
                if 0 <= i < H3:
                    part = prod[i, pl.ds((3 * dy + dx) * OC, OC), :]
                    total = part if total is None else total + part
            columns.append(total)
        before = jnp.where(lane3 == 0, 0.0, pltpu.roll(columns[0], 1, 1))
        after = jnp.where(lane3 == W3 - 1, 0.0, pltpu.roll(columns[2], W3 - 1, 1))
        return before + columns[1] + after

    def edge_copies(which):
        return [
            pltpu.make_async_remote_copy(
                src_ref=edge_s.at[which, j],
                dst_ref=edge_r.at[which, j],
                send_sem=edge_send.at[which, j],
                recv_sem=edge_recv.at[which, j],
                device_id={"rows": target},
                device_id_type=MESH,
            )
            for j, target in ((0, down), (1, up))
        ]

    def edges_out(which):
        edge_s[which, 0] = combine(H3)
        edge_s[which, 1] = combine(-1)
        copies = edge_copies(which)
        for copy in copies:
            copy.start()
        return copies

    def edges_in(which):
        low = jnp.where(row > 0, edge_r[which, 0], 0.0)
        high = jnp.where(row < R - 1, edge_r[which, 1], 0.0)
        return low, high

    loads["w3a"].wait()
    taps(w3a, lambda i: act3[:, i].reshape(W3, C3), NT, (0, 3))
    copies = edges_out(0)
    taps(w3a, lambda i: act3[:, i].reshape(W3, C3), NT, (1, 2))
    for i in (1, 2):
        value = combine(i)
        hid3[i] = value
        gat2[col, i] = value.astype(BF16)
    ring_start(1, gat2, (1, 2))
    for i in (0, 3):
        hid3[i] = combine(i)
    for copy in copies:
        copy.wait()
    for i, border in zip((0, 3), edges_in(0)):
        value = hid3[i] + border
        hid3[i] = value
        gat2[col, i] = value.astype(BF16)
    ring_start(1, gat2, (0, 3))

    fs = jnp.zeros((OC, W3), F32)
    fq = jnp.zeros((OC, W3), F32)
    for i in range(H3):
        value = hid3[i]
        fs = fs + value
        fq = fq + value * value
    fs = jnp.sum(fs, axis=1, keepdims=True)
    fq = jnp.sum(fq, axis=1, keepdims=True)
    lane = iota((OC, 128), 1)
    second = iota((OC, 128), 0) >= OC // 2
    group = jnp.where(second, 1, 0)
    laid = jnp.where(lane == group, fs, 0.0) + jnp.where(lane == group + 2, fq, 0.0)
    st_c[0] = jnp.sum(laid.reshape(OC // 8, 8, 128), axis=0)
    spread(st_c, "rows", 4)

    pick = jnp.where(iota((OC, C3), 1) == iota((OC, C3), 0) + col * OC, 1.0, 0.0).astype(BF16)

    def residual(i, carry):
        res[i] = lax.dot_general(pick, gat1[:, i].reshape(W3, C3), NT, preferred_element_type=F32)
        return carry

    lax.fori_loop(0, H3, residual, 0)
    ring_step(1, gat2, 1, 0, 1)
    st_b2[0] = collect(st_b1, "rows", 2)
    spread(st_b2, "cols", 3)

    total = jnp.sum(collect(st_c, "rows", 4), axis=0, keepdims=True)
    total = jnp.broadcast_to(total, (OC, 128)) / COUNT3
    mean = jnp.sum(jnp.where(lane == group, total, 0.0), axis=1, keepdims=True)
    square = jnp.sum(jnp.where(lane == group + 2, total, 0.0), axis=1, keepdims=True)
    inverse = lax.rsqrt(square - mean * mean + EPS)

    def upright(ref):
        eye = iota((OC, OC), 0) == iota((OC, OC), 1)
        return jnp.sum(jnp.where(eye, jnp.broadcast_to(flat(ref), (OC, OC)), 0.0), axis=1, keepdims=True)

    scale4 = inverse * upright(g3b)
    shift4 = 0.5 * (upright(b3b) - mean * scale4)
    scale4 = 0.5 * scale4
    eye = iota((OC, 128), 0) == iota((OC, 128), 1)
    as_rows = [jnp.sum(jnp.where(eye, x, 0.0), axis=0, keepdims=True) for x in (scale4, shift4)]
    st_d[0] = jnp.where(iota((8, 128), 0) == 0, *as_rows)
    spread(st_d, "cols", 5)

    ring_step(1, gat2, 1, 2, 3)
    ring_step(1, gat2, 2, 0, 1, 2)
    rates = group_rates(collect(st_b2, "cols", 3))
    scale2, shift2 = channel_rates(rates, group_matrix(C1, 10, 0, 1), flat(g1b), flat(b1b))
    near_ok = (place < W1) | ((place == W1) & (col < C - 1)) | ((place == WP - 1) & (col > 0))

    def act2_rows(first, last):
        for i in range(first, last):
            live = near_ok
            if i == 0:
                live = live & (row > 0)
            if i == H1 + 1:
                live = live & (row < R - 1)
            put_row(i, hid[i] * scale2 + shift2, live)

    act2_rows(0, 18)
    ring_step(1, gat2, 2, 3)
    ring_step(1, gat2, 3, 0)
    loads["w1b"].wait()

    def norm4(slot):
        block = st_d[(col + C - slot) % C]
        scale, shift = (jnp.sum(jnp.where(eye, block[j : j + 1], 0.0), axis=1, keepdims=True) for j in range(2))
        for i in range(H3):
            act4[slot, i] = halves(gat2[slot, i].astype(F32) * scale + shift).astype(BF16)

    def norm4_hop(hop):
        mate_step(1, gat2, hop)
        for direction in range(1 if hop in (0, 4) else 2):
            for k in range(2):
                norm4(2 * origin(direction, hop) + k)

    def out1_rows(first, count):
        value = conv1(w1b, first, count, W1) + flat(c1b).reshape(1, 1, C1)
        o1[pl.ds(first, count)] = (lat[pl.ds(first, count)].astype(F32) + value).astype(BF16)

    out1_rows(0, 4)
    arrived(st_d, "cols", 5)
    norm4_hop(0)
    ring_step(1, gat2, 3, 1, 2)
    out1_rows(4, 4)
    norm4_hop(1)
    ring_step(1, gat2, 3, 3)
    out1_rows(8, 4)
    ring_step(1, gat2, 4, 0)
    out1_rows(12, 4)
    write1 = local(o1, out1_h, 7)
    write1.start()
    ring_step(1, gat2, 4, 1)
    bias3 = upright(c3b)
    norm4_hop(2)
    norm4_hop(3)
    norm4_hop(4)

    loads["w3b"].wait()
    taps(w3b, lambda i: act4[:, i].reshape(C3, W3), (((1,), (0,)), ((), ())), (0, 3))
    copies = edges_out(1)
    taps(w3b, lambda i: act4[:, i].reshape(C3, W3), (((1,), (0,)), ((), ())), (1, 2))
    for i in range(H3):
        res[i] = res[i] + combine(i) + bias3
    for copy in copies:
        copy.wait()
    low, high = edges_in(1)
    res[0] = res[0] + low
    res[H3 - 1] = res[H3 - 1] + high
    for i in range(H3):
        o3[i] = res[i].astype(BF16)
    write3 = local(o3, out3_h, 8)
    write3.start()
    for copy in sends:
        copy.wait_send()
    write1.wait()
    write3.wait()


def body(
    latent1, norm1a_g, norm1a_b, conv1a_w, norm1b_g, norm1b_b, conv1b_w, conv1b_b,
    feat3, adapter3, norm3a_g, norm3a_b, conv3a_w, norm3b_g, norm3b_b, conv3b_w, conv3b_b,
):
    def wide(w):
        return w.reshape(3, 3 * C1, C1)

    def tall(w):
        return jnp.swapaxes(w, 2, 3).reshape(9 * OC, C3)

    any_spec = pl.BlockSpec(memory_space=pl.ANY)
    operands = [
        (latent1, any_spec), (norm1a_g, any_spec), (norm1a_b, any_spec), (wide(conv1a_w), any_spec),
        (norm1b_g, any_spec), (norm1b_b, any_spec), (wide(conv1b_w), any_spec), (conv1b_b, any_spec),
        (feat3, any_spec), (adapter3, any_spec), (norm3a_g, any_spec), (norm3a_b, any_spec),
        (tall(conv3a_w), any_spec), (norm3b_g, any_spec), (norm3b_b, any_spec),
        (tall(conv3b_w), any_spec), (conv3b_b, any_spec),
    ]
    out1, out3 = pl.pallas_call(
        kernel,
        out_shape=(
            jax.ShapeDtypeStruct((H1, W1, C1), BF16),
            jax.ShapeDtypeStruct((H3, OC, W3), BF16),
        ),
        in_specs=[spec for _, spec in operands],
        out_specs=(any_spec, any_spec),
        scratch_shapes=[
            *[pltpu.VMEM((n,), F32) for n in (C1, C1, C1, C1, C1, C3, C3, OC, OC, OC)],
            pltpu.VMEM((H1, W1, C1), BF16),
            pltpu.VMEM((2, W1, C1), BF16),
            pltpu.VMEM((2, W1, C1), BF16),
            pltpu.VMEM((2, 2, 24, C1), F32),
            pltpu.VMEM((2, 2, 24, C1), F32),
            pltpu.VMEM((H1 + 4, WP, 3 * C1), BF16),
            pltpu.VMEM((H1 + 2, WP, C1), F32),
            pltpu.VMEM((3, 3 * C1, C1), BF16),
            pltpu.VMEM((3, 3 * C1, C1), BF16),
            pltpu.VMEM((9 * OC, C3), BF16),
            pltpu.VMEM((9 * OC, C3), BF16),
            pltpu.VMEM((H3, 16, C3), BF16),
            pltpu.VMEM((H3, 16, C3), BF16),
            pltpu.VMEM((C, H3, 16, C3), BF16),
            pltpu.VMEM((C, H3, 16, C3), BF16),
            pltpu.VMEM((C, H3, OC, W3), BF16),
            pltpu.VMEM((H3, 9 * OC, W3), F32),
            pltpu.VMEM((2, 2, OC, W3), F32),
            pltpu.VMEM((2, 2, OC, W3), F32),
            pltpu.VMEM((H3, OC, W3), F32),
            pltpu.VMEM((H3, OC, W3), F32),
            pltpu.VMEM((H1, W1, C1), BF16),
            pltpu.VMEM((H3, OC, W3), BF16),
            pltpu.VMEM((16, 8, 128), F32),
            pltpu.VMEM((16, 8, 128), F32),
            pltpu.VMEM((16, 8, 128), F32),
            pltpu.VMEM((16, 8, 128), F32),
            pltpu.VMEM((16, 8, 128), F32),
            pltpu.VMEM((16, 8, 128), F32),
            pltpu.VMEM((C, H3, OC, W3), BF16),
            pltpu.SemaphoreType.DMA((19,)),
            pltpu.SemaphoreType.DMA((6,)),
            pltpu.SemaphoreType.DMA((6,)),
            pltpu.SemaphoreType.DMA((2, 2, 4, 4)),
            pltpu.SemaphoreType.DMA((2, 2, 4, 4)),
            pltpu.SemaphoreType.DMA((2, 2, 5)),
            pltpu.SemaphoreType.DMA((2, 2, 5)),
            pltpu.SemaphoreType.DMA((4,)),
            pltpu.SemaphoreType.DMA((4,)),
            pltpu.SemaphoreType.DMA((2, 2)),
            pltpu.SemaphoreType.DMA((2, 2)),
        ],
        compiler_params=pltpu.CompilerParams(
            collective_id=0, has_side_effects=True, vmem_limit_bytes=56 * 1024 * 1024
        ),
    )(*[value for value, _ in operands])
    return out1, jnp.swapaxes(out3, 1, 2)


def solution(mesh):
    return jax.shard_map(
        body,
        mesh=mesh,
        in_specs=(
            P("rows", "cols", None), P(), P(), P(), P(), P(), P(), P(),
            P("rows", "cols", None), P("rows", "cols", None), P(), P(),
            P(None, None, None, "cols"), P("cols"), P("cols"), P(None, None, None, "cols"), P("cols"),
        ),
        out_specs=(P("rows", "cols", None), P("rows", None, "cols")),
        check_vma=False,
    )
```

```python
import functools

import jax
import jax.numpy as jnp
from jax import lax
from jax.experimental import pallas as pl
from jax.experimental.pallas import tpu as pltpu
from jax.sharding import PartitionSpec as P

MESH = pl.DeviceIdType.MESH
F32 = jnp.float32
BF16 = jnp.bfloat16
EPS = 1e-05
R, C = 16, 16
Z = 8
C1, C3, OC = 320, 1280, 80
H1, W1 = 16, 64
H3, W3 = 4, 256
WP = 80
ORDERS = ((0, 3, 1, 2), (1, 2, 0, 3))
NT = (((1,), (1,)), ((), ()))
COUNT1 = float(R * H1 * C * W1 * (C1 // 32))
COUNT3 = float(R * H3 * W3 * (C3 // 32))


def iota(shape, dim):
    return lax.broadcasted_iota(jnp.int32, shape, dim)


def group_matrix(chans, width, offset, dim):
    shape = (chans, 128) if dim == 0 else (128, chans)
    chan = iota(shape, dim)
    first = (iota(shape, 1 - dim) - offset) * width
    return jnp.where((chan >= first) & (chan < first + width), 1.0, 0.0).astype(BF16)


def exact_dot(a, ones):
    high = a.astype(BF16)
    rest = a - high.astype(F32)
    middle = rest.astype(BF16)
    low = (rest - middle.astype(F32)).astype(BF16)
    n = a.shape[0]
    out = jnp.dot(jnp.concatenate([high, middle, low], axis=0), ones, preferred_element_type=F32)
    return out[0:n] + out[n : 2 * n] + out[2 * n :]


def group_sums(sums, squares, ones, offset):
    both = exact_dot(jnp.concatenate([sums, squares], axis=0), ones)
    first = pltpu.roll(both[0:8], offset, 1) if offset else both[0:8]
    return first + pltpu.roll(both[8:16], offset + 32, 1)


def flat(ref):
    return ref[...].reshape(1, -1)


def halves(value):
    return value + value * jnp.tanh(value)


def kernel(
    lat_h, g1a_h, b1a_h, w1a_h, g1b_h, b1b_h, w1b_h, c1b_h,
    feat_h, adap_h, g3a_h, b3a_h, w3a_h, g3b_h, b3b_h, w3b_h, c3b_h,
    out1_h, out3_h,
    g1a, b1a, g1b, b1b, c1b, g3a, b3a, g3b, b3b, c3b,
    lat, top, bottom, pack, side, act, hid, w1a, w1b, w3a, w3b, feat, adap, gat1, act3, gat2, prod,
    edge_s, edge_r, hid3, res, o1, o3, st_a1, st_a2, st_b1, st_b2, st_c, st_d, act4,
    local_sem, ar_send, ar_recv, ring_send, ring_recv, mate_send, mate_recv,
    halo_send, halo_recv, edge_send, edge_recv,
):
    row = lax.axis_index("rows")
    col = lax.axis_index("cols")
    z = col // 2
    core = col % 2
    up = (row + R - 1) % R
    down = (row + 1) % R
    left = (col + C - 1) % C
    right = (col + 1) % C
    mate = z * 2 + (1 - core)

    def local(src, dst, index):
        return pltpu.make_async_copy(src, dst, local_sem.at[index])

    loads = {
        "feat": local(feat_h, feat, 0),
        "adap": local(adap_h, adap, 1),
        "lat": local(lat_h, lat, 2),
        "w1a": local(w1a_h, w1a, 3),
        "w3a": local(w3a_h, w3a, 4),
        "w1b": local(w1b_h, w1b, 5),
        "w3b": local(w3b_h, w3b, 6),
    }
    small = [
        local(src, dst, 9 + i)
        for i, (src, dst) in enumerate(
            (
                (g1a_h, g1a), (b1a_h, b1a), (g1b_h, g1b), (b1b_h, b1b), (c1b_h, c1b),
                (g3a_h, g3a), (b3a_h, b3a), (g3b_h, g3b), (b3b_h, b3b), (c3b_h, c3b),
            )
        )
    ]
    for name in ("feat", "adap", "lat"):
        loads[name].start()

    barrier = pltpu.get_barrier_semaphore()
    for step in range(1, R):
        pl.semaphore_signal(barrier, inc=1, device_id={"rows": (row + step) % R}, device_id_type=MESH)
    for step in range(1, C):
        pl.semaphore_signal(barrier, inc=1, device_id={"cols": (col + step) % C}, device_id_type=MESH)

    def spread(buf, axis, index):
        me = row if axis == "rows" else col

        def send(step, carry):
            pltpu.make_async_remote_copy(
                src_ref=buf.at[0],
                dst_ref=buf.at[step],
                send_sem=ar_send.at[index],
                recv_sem=ar_recv.at[index],
                device_id={axis: (me + step) % 16},
                device_id_type=MESH,
            ).start()
            return carry

        lax.fori_loop(1, 16, send, 0)

    def arrived(buf, axis, index):
        rest = pltpu.make_async_remote_copy(
            src_ref=buf.at[pl.ds(1, 15)],
            dst_ref=buf.at[pl.ds(1, 15)],
            send_sem=ar_send.at[index],
            recv_sem=ar_recv.at[index],
            device_id={axis: ((row if axis == "rows" else col) + 1) % 16},
            device_id_type=MESH,
        )
        rest.wait_recv()
        rest.wait_send()

    def collect(buf, axis, index):
        arrived(buf, axis, index)
        return jnp.sum(buf[...], axis=0)

    def origin(direction, hop):
        return (z + Z - hop) % Z if direction == 0 else (z + hop) % Z

    def chunk(gat, slot, half):
        return gat.at[slot, half]

    def ring_copy(which, gat, direction, hop, half):
        slot = 2 * origin(direction, hop - 1) + core
        target = 2 * ((z + 1) % Z if direction == 0 else (z + Z - 1) % Z) + core
        return pltpu.make_async_remote_copy(
            src_ref=chunk(gat, slot, half),
            dst_ref=chunk(gat, slot, half),
            send_sem=ring_send.at[which, direction, hop - 1, half],
            recv_sem=ring_recv.at[which, direction, hop - 1, half],
            device_id={"cols": target},
            device_id_type=MESH,
        )

    def ring_wait(which, gat, direction, hop, half):
        slot = 2 * origin(direction, hop) + core
        target = 2 * ((z + 1) % Z if direction == 0 else (z + Z - 1) % Z) + core
        pltpu.make_async_remote_copy(
            src_ref=chunk(gat, slot, half),
            dst_ref=chunk(gat, slot, half),
            send_sem=ring_send.at[which, direction, hop - 1, half],
            recv_sem=ring_recv.at[which, direction, hop - 1, half],
            device_id={"cols": target},
            device_id_type=MESH,
        ).wait_recv()

    def mate_copy(which, gat, direction, hop, side_core):
        part = gat.at[2 * origin(direction, min(hop, 4)) + side_core]
        if hop >= 4:
            part = part.at[dict(arrivals(which, 4, hop - 4))[direction]]
        return pltpu.make_async_remote_copy(
            src_ref=part,
            dst_ref=part,
            send_sem=mate_send.at[which, direction, hop],
            recv_sem=mate_recv.at[which, direction, hop],
            device_id={"cols": mate},
            device_id_type=MESH,
        )

    def arrivals(which, hop, k):
        order = ORDERS[which]
        if hop == 4:
            return list(enumerate(sorted(order[2 * k : 2 * k + 2])))
        return [(0, order[k]), (1, order[k])]

    sends = []

    def go(copy):
        copy.start()
        sends.append(copy)

    def ring_start(which, gat, parts):
        for part in parts:
            for direction in range(2):
                go(ring_copy(which, gat, direction, 1, part))
        if 3 in parts:
            go(mate_copy(which, gat, 0, 0, core))

    def ring_step(which, gat, hop, *ks):
        last = [pair for k in range(2) for pair in arrivals(which, 4, k)]
        for k in ks:
            for direction, part in arrivals(which, hop, k):
                ring_wait(which, gat, direction, hop, part)
                if hop < 3 or (hop == 3 and (direction, part) in last):
                    go(ring_copy(which, gat, direction, hop + 1, part))
                if hop == 4:
                    go(mate_copy(which, gat, direction, 4 + k, core))
                elif k == 3:
                    go(mate_copy(which, gat, direction, hop, core))

    def mate_step(which, gat, hop):
        for direction in range(1 if hop == 0 else 2):
            mate_copy(which, gat, direction, hop, 1 - core).wait_recv()

    loads["feat"].wait()
    loads["adap"].wait()
    for copy in small:
        copy.start()
    for name in ("w1a", "w3a", "w1b", "w3b"):
        loads[name].start()
    js = jnp.zeros((8, C3), F32)
    jq = jnp.zeros((8, C3), F32)
    for i in range(H3):
        value = (feat[i].astype(F32) + adap[i].astype(F32)).astype(BF16)
        gat1[col, i] = value
        value = value.astype(F32).reshape(2, 8, C3)
        js = js + jnp.sum(value, axis=0)
        jq = jq + jnp.sum(value * value, axis=0)

    pl.semaphore_wait(barrier, R - 1 + C - 1)
    ring_start(0, gat1, ORDERS[0])
    joined_sums = group_sums(js, jq, group_matrix(C3, 40, 0, 0), 64)

    loads["lat"].wait()

    def halo_copy(src, dst, index, target):
        return pltpu.make_async_remote_copy(
            src_ref=src,
            dst_ref=dst,
            send_sem=halo_send.at[index],
            recv_sem=halo_recv.at[index],
            device_id=target,
            device_id_type=MESH,
        )

    to_down = halo_copy(lat.at[pl.ds(H1 - 2, 2)], top, 0, {"rows": down})
    to_up = halo_copy(lat.at[pl.ds(0, 2)], bottom, 1, {"rows": up})
    to_down.start()
    to_up.start()

    ls = jnp.zeros((8, C1), F32)
    lq = jnp.zeros((8, C1), F32)
    for i in range(H1):
        value = lat[i].astype(F32).reshape(8, 8, C1)
        ls = ls + jnp.sum(value, axis=0)
        lq = lq + jnp.sum(value * value, axis=0)
    ones1 = group_matrix(C1, 10, 0, 0)
    st_a1[0] = group_sums(ls, lq, ones1, 0) + joined_sums
    spread(st_a1, "rows", 0)
    ring_step(0, gat1, 1, 0, 1, 2)

    to_down.wait()
    to_up.wait()

    def extended_row(i):
        if i < 2:
            return top[i]
        if i < H1 + 2:
            return lat[i - 2]
        return bottom[i - H1 - 2]

    for block in range(3):
        rows_here = [i for i in range(8 * block, 8 * block + 8) if i < H1 + 4]
        tiles = [jnp.zeros((8, C1), F32) for _ in range(4)]
        for i in rows_here:
            value = extended_row(i)
            first = value[0:16].astype(F32)
            last = value[48:64].astype(F32)
            here = iota((8, C1), 0) == i - 8 * block
            for j, piece in enumerate((last[14:15], last[15:16], first[0:1], first[1:2])):
                tiles[j] = jnp.where(here, jnp.broadcast_to(piece, (8, C1)), tiles[j])
        for j in range(4):
            pack[j // 2, j % 2, pl.ds(8 * block, 8), :] = tiles[j]
    to_right = halo_copy(pack.at[0], side.at[0], 2, {"cols": right})
    to_left = halo_copy(pack.at[1], side.at[1], 3, {"cols": left})
    to_right.start()
    to_left.start()

    ring_step(0, gat1, 1, 3)
    st_a2[0] = collect(st_a1, "rows", 0)
    spread(st_a2, "cols", 1)
    ring_step(0, gat1, 2, 0, 1, 2, 3)
    def group_rates(total):
        total = jnp.sum(total, axis=0, keepdims=True)
        total = jnp.broadcast_to(total, (8, 128))
        lane = iota((8, 128), 1)
        count = jnp.where(lane < 64, COUNT1, COUNT3)
        squares = pltpu.roll(total, 96, 1)
        mean = total / count
        spread_of = squares / count - mean * mean
        live = (lane < 32) | ((lane >= 64) & (lane < 96))
        inverse = lax.rsqrt(jnp.where(live, spread_of, 1.0) + EPS)
        return jnp.where(live, mean, 0.0), jnp.where(live, inverse, 0.0)

    def channel_rates(rates, matrix, gain, shift):
        both = exact_dot(jnp.where(iota((8, 128), 0) == 0, *rates), matrix)
        mean, inverse = both[0:1], both[1:2]
        scale = inverse * gain
        return 0.5 * scale, 0.5 * (shift - mean * scale)

    for copy in small:
        copy.wait()
    rates = group_rates(collect(st_a2, "cols", 1))
    scale1, shift1 = channel_rates(rates, group_matrix(C1, 10, 0, 1), flat(g1a), flat(b1a))

    def put_row(i, value, live):
        value = jnp.where(live, halves(value), 0.0)
        act[i, :, 0:C1] = pltpu.roll(value, 1, 0).astype(BF16)
        act[i, :, C1 : 2 * C1] = value.astype(BF16)
        act[i, :, 2 * C1 : 3 * C1] = pltpu.roll(value, WP - 1, 0).astype(BF16)

    place = iota((WP, C1), 0)

    slab_place = iota((16, C1), 0)
    wide_ok = (place < W1) | ((place < W1 + 2) & (col < C - 1)) | ((place >= WP - 2) & (col > 0))

    def act1_rows(first, last):
        for i in range(first, last):
            slab = jnp.zeros((16, C1), F32)
            base = 8 * (i // 8)
            for target, which, j in ((0, 1, 0), (1, 1, 1), (14, 0, 0), (15, 0, 1)):
                piece = side[which, j, pl.ds(base, 8), :][i - base : i - base + 1]
                slab = jnp.where(slab_place == target, jnp.broadcast_to(piece, (16, C1)), slab)
            value = jnp.concatenate([extended_row(i).astype(F32), slab], axis=0)
            live = wide_ok
            if i < 2:
                live = live & (row > 0)
            if i >= H1 + 2:
                live = live & (row < R - 1)
            put_row(i, value * scale1 + shift1, live)

    to_right.wait()
    to_left.wait()
    act1_rows(0, 20)
    ring_step(0, gat1, 3, 0, 1)

    def conv1(weights, first, count, width):
        total = None
        for dy in range(3):
            block = act[pl.ds(first + dy, count), 0:width, :].reshape(count * width, 3 * C1)
            part = jnp.dot(block, weights[dy], preferred_element_type=F32)
            total = part if total is None else total + part
        return total.reshape(count, width, C1)

    def norm3(slot, parts):
        for i in parts:
            value = gat1[slot, i].astype(F32) * scale3 + shift3
            act3[slot, i] = halves(value).astype(BF16)

    def norm_hop(which, gat, norm, hop):
        mate_step(which, gat, hop)
        parts = range(H3) if hop < 4 else ORDERS[which][2 * hop - 8 : 2 * hop - 6]
        for direction in range(1 if hop == 0 or hop >= 4 else 2):
            for k in range(2):
                norm(2 * origin(direction, min(hop, 4)) + k, parts)

    def norm3_hop(hop):
        norm_hop(0, gat1, norm3, hop)

    loads["w1a"].wait()
    hid[pl.ds(0, 6)] = conv1(w1a, 0, 6, WP)
    ring_step(0, gat1, 3, 2, 3)
    scale3, shift3 = channel_rates(rates, group_matrix(C3, 40, 64, 1), flat(g3a), flat(b3a))
    hid[pl.ds(6, 6)] = conv1(w1a, 6, 6, WP)
    for hop in range(4):
        norm3_hop(hop)

    def taps(weights, source, dims, i, first, last):
        prod[i, pl.ds(first, last - first), :] = lax.dot_general(
            weights[pl.ds(first, last - first), :], source(i), dims, preferred_element_type=F32
        )

    BAND = 3 * OC

    def border_taps(*args):
        taps(*args, 0, 2 * BAND, 3 * BAND)
        taps(*args, 3, 0, BAND)

    def other_taps(*args):
        for i in (1, 2):
            taps(*args, i, 0, 3 * BAND)
        taps(*args, 0, 0, 2 * BAND)
        taps(*args, 3, BAND, 3 * BAND)

    lane3 = iota((OC, W3), 1)

    def combine(target):
        columns = []
        for dx in range(3):
            total = None
            for dy in range(3):
                i = target + dy - 1
                if 0 <= i < H3:
                    part = prod[i, pl.ds((3 * dy + dx) * OC, OC), :]
                    total = part if total is None else total + part
            columns.append(total)
        before = jnp.where(lane3 == 0, 0.0, pltpu.roll(columns[0], 1, 1))
        after = jnp.where(lane3 == W3 - 1, 0.0, pltpu.roll(columns[2], W3 - 1, 1))
        return before + columns[1] + after

    def edge_copies(which):
        return [
            pltpu.make_async_remote_copy(
                src_ref=edge_s.at[which, j],
                dst_ref=edge_r.at[which, j],
                send_sem=edge_send.at[which, j],
                recv_sem=edge_recv.at[which, j],
                device_id={"rows": target},
                device_id_type=MESH,
            )
            for j, target in ((0, down), (1, up))
        ]

    def edges_out(which):
        edge_s[which, 0] = combine(H3).astype(BF16)
        edge_s[which, 1] = combine(-1).astype(BF16)
        copies = edge_copies(which)
        for copy in copies:
            copy.start()
        return copies

    def edges_in(which):
        low = jnp.where(row > 0, edge_r[which, 0].astype(F32), 0.0)
        high = jnp.where(row < R - 1, edge_r[which, 1].astype(F32), 0.0)
        return low, high

    loads["w3a"].wait()
    first3 = (w3a, lambda i: act3[:, i].reshape(W3, C3), NT)
    ring_step(0, gat1, 4, 0)
    norm3_hop(4)
    border_taps(*first3)
    copies = edges_out(0)
    ring_step(0, gat1, 4, 1)
    norm3_hop(5)
    other_taps(*first3)
    for i in (1, 2):
        value = combine(i)
        hid3[i] = value
        gat2[col, i] = value.astype(BF16)
    ring_start(1, gat2, (1, 2))
    for i in (0, 3):
        hid3[i] = combine(i)
    for copy in copies:
        copy.wait()
    for i, border in zip((0, 3), edges_in(0)):
        value = hid3[i] + border
        hid3[i] = value
        gat2[col, i] = value.astype(BF16)
    ring_start(1, gat2, (0, 3))

    fs = jnp.zeros((OC, W3), F32)
    fq = jnp.zeros((OC, W3), F32)
    for i in range(H3):
        value = hid3[i]
        fs = fs + value
        fq = fq + value * value
    fs = jnp.sum(fs, axis=1, keepdims=True)
    fq = jnp.sum(fq, axis=1, keepdims=True)
    lane = iota((OC, 128), 1)
    second = iota((OC, 128), 0) >= OC // 2
    group = jnp.where(second, 1, 0)
    laid = jnp.where(lane == group, fs, 0.0) + jnp.where(lane == group + 2, fq, 0.0)
    st_c[0] = jnp.sum(laid.reshape(OC // 8, 8, 128), axis=0)
    spread(st_c, "rows", 4)

    hid[pl.ds(12, 6)] = conv1(w1a, 12, 6, WP)
    hs = jnp.zeros((8, C1), F32)
    hq = jnp.zeros((8, C1), F32)
    for i in range(H1):
        value = hid[i + 1, 0:W1, :].reshape(8, 8, C1)
        hs = hs + jnp.sum(value, axis=0)
        hq = hq + jnp.sum(value * value, axis=0)
    st_b1[0] = group_sums(hs, hq, ones1, 0)
    spread(st_b1, "rows", 2)

    ring_step(1, gat2, 1, 0, 1, 2, 3)

    total = jnp.sum(collect(st_c, "rows", 4), axis=0, keepdims=True)
    total = jnp.broadcast_to(total, (OC, 128)) / COUNT3
    mean = jnp.sum(jnp.where(lane == group, total, 0.0), axis=1, keepdims=True)
    square = jnp.sum(jnp.where(lane == group + 2, total, 0.0), axis=1, keepdims=True)
    inverse = lax.rsqrt(square - mean * mean + EPS)

    def upright(ref):
        eye = iota((OC, OC), 0) == iota((OC, OC), 1)
        return jnp.sum(jnp.where(eye, jnp.broadcast_to(flat(ref), (OC, OC)), 0.0), axis=1, keepdims=True)

    scale4 = inverse * upright(g3b)
    shift4 = 0.5 * (upright(b3b) - mean * scale4)
    scale4 = 0.5 * scale4
    eye = iota((OC, 128), 0) == iota((OC, 128), 1)
    as_rows = [jnp.sum(jnp.where(eye, x, 0.0), axis=0, keepdims=True) for x in (scale4, shift4)]
    st_d[0] = jnp.where(iota((8, 128), 0) == 0, *as_rows)
    spread(st_d, "cols", 5)

    ring_step(1, gat2, 2, 0, 1)
    st_b2[0] = collect(st_b1, "rows", 2)
    spread(st_b2, "cols", 3)

    pick = jnp.where(iota((OC, C3), 1) == iota((OC, C3), 0) + col * OC, 1.0, 0.0).astype(BF16)

    def residual(i, carry):
        res[i] = lax.dot_general(pick, gat1[:, i].reshape(W3, C3), NT, preferred_element_type=F32)
        return carry

    lax.fori_loop(0, H3, residual, 0)
    ring_step(1, gat2, 2, 2, 3)

    rates = group_rates(collect(st_b2, "cols", 3))
    scale2, shift2 = channel_rates(rates, group_matrix(C1, 10, 0, 1), flat(g1b), flat(b1b))
    near_ok = (place < W1) | ((place == W1) & (col < C - 1)) | ((place == WP - 1) & (col > 0))

    def act2_rows(first, last):
        for i in range(first, last):
            live = near_ok
            if i == 0:
                live = live & (row > 0)
            if i == H1 + 1:
                live = live & (row < R - 1)
            put_row(i, hid[i] * scale2 + shift2, live)

    act2_rows(0, 18)
    ring_step(1, gat2, 3, 0, 1)
    loads["w1b"].wait()

    def norm4(slot, parts):
        block = st_d[(col + C - slot) % C]
        scale, shift = (jnp.sum(jnp.where(eye, block[j : j + 1], 0.0), axis=1, keepdims=True) for j in range(2))
        for i in parts:
            act4[slot, i] = halves(gat2[slot, i].astype(F32) * scale + shift).astype(BF16)

    def norm4_hop(hop):
        norm_hop(1, gat2, norm4, hop)

    def out1_rows(first, count):
        value = conv1(w1b, first, count, W1) + flat(c1b).reshape(1, 1, C1)
        o1[pl.ds(first, count)] = (lat[pl.ds(first, count)].astype(F32) + value).astype(BF16)

    out1_rows(0, 4)
    ring_step(1, gat2, 3, 2, 3)
    out1_rows(4, 4)
    arrived(st_d, "cols", 5)
    for hop in range(4):
        norm4_hop(hop)
    loads["w3b"].wait()
    second3 = (w3b, lambda i: act4[:, i].reshape(C3, W3), (((1,), (0,)), ((), ())))
    bias3 = upright(c3b)
    out1_rows(8, 4)
    ring_step(1, gat2, 4, 0)
    norm4_hop(4)
    ring_step(1, gat2, 4, 1)
    norm4_hop(5)
    border_taps(*second3)
    copies = edges_out(1)
    other_taps(*second3)
    out1_rows(12, 4)
    write1 = local(o1, out1_h, 7)
    write1.start()
    for i in range(H3):
        res[i] = res[i] + combine(i) + bias3
    for copy in copies:
        copy.wait()
    low, high = edges_in(1)
    res[0] = res[0] + low
    res[H3 - 1] = res[H3 - 1] + high
    for i in range(H3):
        o3[i] = res[i].astype(BF16)
    write3 = local(o3, out3_h, 8)
    write3.start()
    for copy in sends:
        copy.wait_send()
    write1.wait()
    write3.wait()


def body(
    latent1, norm1a_g, norm1a_b, conv1a_w, norm1b_g, norm1b_b, conv1b_w, conv1b_b,
    feat3, adapter3, norm3a_g, norm3a_b, conv3a_w, norm3b_g, norm3b_b, conv3b_w, conv3b_b,
):
    def wide(w):
        return w.reshape(3, 3 * C1, C1)

    def tall(w):
        return jnp.swapaxes(w, 2, 3).reshape(9 * OC, C3)

    any_spec = pl.BlockSpec(memory_space=pl.ANY)
    operands = [
        (latent1, any_spec), (norm1a_g, any_spec), (norm1a_b, any_spec), (wide(conv1a_w), any_spec),
        (norm1b_g, any_spec), (norm1b_b, any_spec), (wide(conv1b_w), any_spec), (conv1b_b, any_spec),
        (feat3, any_spec), (adapter3, any_spec), (norm3a_g, any_spec), (norm3a_b, any_spec),
        (tall(conv3a_w), any_spec), (norm3b_g, any_spec), (norm3b_b, any_spec),
        (tall(conv3b_w), any_spec), (conv3b_b, any_spec),
    ]
    out1, out3 = pl.pallas_call(
        kernel,
        out_shape=(
            jax.ShapeDtypeStruct((H1, W1, C1), BF16),
            jax.ShapeDtypeStruct((H3, OC, W3), BF16),
        ),
        in_specs=[spec for _, spec in operands],
        out_specs=(any_spec, any_spec),
        scratch_shapes=[
            *[pltpu.VMEM((n,), F32) for n in (C1, C1, C1, C1, C1, C3, C3, OC, OC, OC)],
            pltpu.VMEM((H1, W1, C1), BF16),
            pltpu.VMEM((2, W1, C1), BF16),
            pltpu.VMEM((2, W1, C1), BF16),
            pltpu.VMEM((2, 2, 24, C1), F32),
            pltpu.VMEM((2, 2, 24, C1), F32),
            pltpu.VMEM((H1 + 4, WP, 3 * C1), BF16),
            pltpu.VMEM((H1 + 2, WP, C1), F32),
            pltpu.VMEM((3, 3 * C1, C1), BF16),
            pltpu.VMEM((3, 3 * C1, C1), BF16),
            pltpu.VMEM((9 * OC, C3), BF16),
            pltpu.VMEM((9 * OC, C3), BF16),
            pltpu.VMEM((H3, 16, C3), BF16),
            pltpu.VMEM((H3, 16, C3), BF16),
            pltpu.VMEM((C, H3, 16, C3), BF16),
            pltpu.VMEM((C, H3, 16, C3), BF16),
            pltpu.VMEM((C, H3, OC, W3), BF16),
            pltpu.VMEM((H3, 9 * OC, W3), F32),
            pltpu.VMEM((2, 2, OC, W3), BF16),
            pltpu.VMEM((2, 2, OC, W3), BF16),
            pltpu.VMEM((H3, OC, W3), F32),
            pltpu.VMEM((H3, OC, W3), F32),
            pltpu.VMEM((H1, W1, C1), BF16),
            pltpu.VMEM((H3, OC, W3), BF16),
            pltpu.VMEM((16, 8, 128), F32),
            pltpu.VMEM((16, 8, 128), F32),
            pltpu.VMEM((16, 8, 128), F32),
            pltpu.VMEM((16, 8, 128), F32),
            pltpu.VMEM((16, 8, 128), F32),
            pltpu.VMEM((16, 8, 128), F32),
            pltpu.VMEM((C, H3, OC, W3), BF16),
            pltpu.SemaphoreType.DMA((19,)),
            pltpu.SemaphoreType.DMA((6,)),
            pltpu.SemaphoreType.DMA((6,)),
            pltpu.SemaphoreType.DMA((2, 2, 4, 4)),
            pltpu.SemaphoreType.DMA((2, 2, 4, 4)),
            pltpu.SemaphoreType.DMA((2, 2, 6)),
            pltpu.SemaphoreType.DMA((2, 2, 6)),
            pltpu.SemaphoreType.DMA((4,)),
            pltpu.SemaphoreType.DMA((4,)),
            pltpu.SemaphoreType.DMA((2, 2)),
            pltpu.SemaphoreType.DMA((2, 2)),
        ],
        compiler_params=pltpu.CompilerParams(
            collective_id=0, has_side_effects=True, vmem_limit_bytes=56 * 1024 * 1024
        ),
    )(*[value for value, _ in operands])
    return out1, jnp.swapaxes(out3, 1, 2)


def solution(mesh):
    return jax.shard_map(
        body,
        mesh=mesh,
        in_specs=(
            P("rows", "cols", None), P(), P(), P(), P(), P(), P(), P(),
            P("rows", "cols", None), P("rows", "cols", None), P(), P(),
            P(None, None, None, "cols"), P("cols"), P("cols"), P(None, None, None, "cols"), P("cols"),
        ),
        out_specs=(P("rows", "cols", None), P("rows", None, "cols")),
        check_vma=False,
    )
```

```python
import functools

import jax
import jax.numpy as jnp
from jax import lax
from jax.experimental import pallas as pl
from jax.experimental.pallas import tpu as pltpu
from jax.sharding import PartitionSpec as P

MESH = pl.DeviceIdType.MESH
F32 = jnp.float32
BF16 = jnp.bfloat16
EPS = 1e-05
R, C = 16, 16
Z = 8
C1, C3, OC = 320, 1280, 80
H1, W1 = 16, 64
H3, W3 = 4, 256
WP = 80
ORDERS = ((0, 3, 1, 2), (1, 2, 0, 3))
NT = (((1,), (1,)), ((), ()))
COUNT1 = float(R * H1 * C * W1 * (C1 // 32))
COUNT3 = float(R * H3 * W3 * (C3 // 32))


def iota(shape, dim):
    return lax.broadcasted_iota(jnp.int32, shape, dim)


def group_matrix(chans, width, offset, dim):
    shape = (chans, 128) if dim == 0 else (128, chans)
    chan = iota(shape, dim)
    first = (iota(shape, 1 - dim) - offset) * width
    return jnp.where((chan >= first) & (chan < first + width), 1.0, 0.0).astype(BF16)


def exact_dot(a, ones):
    high = a.astype(BF16)
    rest = a - high.astype(F32)
    middle = rest.astype(BF16)
    low = (rest - middle.astype(F32)).astype(BF16)
    n = a.shape[0]
    out = jnp.dot(jnp.concatenate([high, middle, low], axis=0), ones, preferred_element_type=F32)
    return out[0:n] + out[n : 2 * n] + out[2 * n :]


def group_sums(sums, squares, ones, offset):
    both = exact_dot(jnp.concatenate([sums, squares], axis=0), ones)
    first = pltpu.roll(both[0:8], offset, 1) if offset else both[0:8]
    return first + pltpu.roll(both[8:16], offset + 32, 1)


def flat(ref):
    return ref[...].reshape(1, -1)


def halves(value):
    return value + value * jnp.tanh(value)


def kernel(
    lat_h, g1a_h, b1a_h, w1a_h, g1b_h, b1b_h, w1b_h, c1b_h,
    feat_h, adap_h, g3a_h, b3a_h, w3a_h, g3b_h, b3b_h, w3b_h, c3b_h,
    out1_h, out3_h,
    g1a, b1a, g1b, b1b, c1b, g3a, b3a, g3b, b3b, c3b,
    lat, top, bottom, pack, side, act, hid, w1a, w1b, w3a, w3b, feat, adap, gat1, act3, gat2, prod,
    edge_s, edge_r, hid3, res, o1, o3, st_a1, st_a2, st_b1, st_b2, st_c, st_d, act4,
    local_sem, ar_send, ar_recv, ring_send, ring_recv, mate_send, mate_recv,
    halo_send, halo_recv, edge_send, edge_recv,
):
    row = lax.axis_index("rows")
    col = lax.axis_index("cols")
    z = col // 2
    core = col % 2
    up = (row + R - 1) % R
    down = (row + 1) % R
    left = (col + C - 1) % C
    right = (col + 1) % C
    mate = z * 2 + (1 - core)

    def local(src, dst, index):
        return pltpu.make_async_copy(src, dst, local_sem.at[index])

    loads = {
        "feat": local(feat_h, feat, 0),
        "adap": local(adap_h, adap, 1),
        "lat": local(lat_h, lat, 2),
        "w1a": local(w1a_h, w1a, 3),
        "w3a": local(w3a_h, w3a, 4),
        "w1b": local(w1b_h, w1b, 5),
        "w3b": local(w3b_h, w3b, 6),
    }
    small = [
        local(src, dst, 9 + i)
        for i, (src, dst) in enumerate(
            (
                (g1a_h, g1a), (b1a_h, b1a), (g1b_h, g1b), (b1b_h, b1b), (c1b_h, c1b),
                (g3a_h, g3a), (b3a_h, b3a), (g3b_h, g3b), (b3b_h, b3b), (c3b_h, c3b),
            )
        )
    ]
    for name in ("feat", "adap", "lat"):
        loads[name].start()

    barrier = pltpu.get_barrier_semaphore()
    for step in range(1, R):
        pl.semaphore_signal(barrier, inc=1, device_id={"rows": (row + step) % R}, device_id_type=MESH)
    for step in range(1, C):
        pl.semaphore_signal(barrier, inc=1, device_id={"cols": (col + step) % C}, device_id_type=MESH)

    def spread(buf, axis, index):
        me = row if axis == "rows" else col

        def send(step, carry):
            pltpu.make_async_remote_copy(
                src_ref=buf.at[0],
                dst_ref=buf.at[step],
                send_sem=ar_send.at[index],
                recv_sem=ar_recv.at[index],
                device_id={axis: (me + step) % 16},
                device_id_type=MESH,
            ).start()
            return carry

        lax.fori_loop(1, 16, send, 0)

    def arrived(buf, axis, index):
        rest = pltpu.make_async_remote_copy(
            src_ref=buf.at[pl.ds(1, 15)],
            dst_ref=buf.at[pl.ds(1, 15)],
            send_sem=ar_send.at[index],
            recv_sem=ar_recv.at[index],
            device_id={axis: ((row if axis == "rows" else col) + 1) % 16},
            device_id_type=MESH,
        )
        rest.wait_recv()
        rest.wait_send()

    def collect(buf, axis, index):
        arrived(buf, axis, index)
        return jnp.sum(buf[...], axis=0)

    def origin(direction, hop):
        return (z + Z - hop) % Z if direction == 0 else (z + hop) % Z

    def chunk(gat, slot, half):
        return gat.at[slot, half]

    def ring_copy(which, gat, direction, hop, half):
        slot = 2 * origin(direction, hop - 1) + core
        target = 2 * ((z + 1) % Z if direction == 0 else (z + Z - 1) % Z) + core
        return pltpu.make_async_remote_copy(
            src_ref=chunk(gat, slot, half),
            dst_ref=chunk(gat, slot, half),
            send_sem=ring_send.at[which, direction, hop - 1, half],
            recv_sem=ring_recv.at[which, direction, hop - 1, half],
            device_id={"cols": target},
            device_id_type=MESH,
        )

    def ring_wait(which, gat, direction, hop, half):
        slot = 2 * origin(direction, hop) + core
        target = 2 * ((z + 1) % Z if direction == 0 else (z + Z - 1) % Z) + core
        pltpu.make_async_remote_copy(
            src_ref=chunk(gat, slot, half),
            dst_ref=chunk(gat, slot, half),
            send_sem=ring_send.at[which, direction, hop - 1, half],
            recv_sem=ring_recv.at[which, direction, hop - 1, half],
            device_id={"cols": target},
            device_id_type=MESH,
        ).wait_recv()

    def mate_copy(which, gat, direction, hop, side_core):
        part = gat.at[2 * origin(direction, min(hop, 4)) + side_core]
        if hop >= 4:
            part = part.at[dict(arrivals(which, 4, hop - 4))[direction]]
        return pltpu.make_async_remote_copy(
            src_ref=part,
            dst_ref=part,
            send_sem=mate_send.at[which, direction, hop],
            recv_sem=mate_recv.at[which, direction, hop],
            device_id={"cols": mate},
            device_id_type=MESH,
        )

    def arrivals(which, hop, k):
        order = ORDERS[which]
        if hop == 4:
            return list(enumerate(sorted(order[2 * k : 2 * k + 2])))
        return [(0, order[k]), (1, order[k])]

    sends = []

    def go(copy):
        copy.start()
        sends.append(copy)

    def ring_start(which, gat, parts):
        for part in parts:
            for direction in range(2):
                go(ring_copy(which, gat, direction, 1, part))
        if 3 in parts:
            go(mate_copy(which, gat, 0, 0, core))

    def ring_step(which, gat, hop, *ks):
        last = [pair for k in range(2) for pair in arrivals(which, 4, k)]
        for k in ks:
            for direction, part in arrivals(which, hop, k):
                ring_wait(which, gat, direction, hop, part)
                if hop < 3 or (hop == 3 and (direction, part) in last):
                    go(ring_copy(which, gat, direction, hop + 1, part))
                if hop == 4:
                    go(mate_copy(which, gat, direction, 4 + k, core))
                elif k == 3:
                    go(mate_copy(which, gat, direction, hop, core))

    def mate_step(which, gat, hop):
        for direction in range(1 if hop == 0 else 2):
            mate_copy(which, gat, direction, hop, 1 - core).wait_recv()

    loads["feat"].wait()
    loads["adap"].wait()
    for copy in small:
        copy.start()
    for name in ("w1a", "w3a", "w1b", "w3b"):
        loads[name].start()
    js = jnp.zeros((8, C3), F32)
    jq = jnp.zeros((8, C3), F32)
    for i in range(H3):
        value = (feat[i].astype(F32) + adap[i].astype(F32)).astype(BF16)
        gat1[col, i] = value
        value = value.astype(F32).reshape(2, 8, C3)
        js = js + jnp.sum(value, axis=0)
        jq = jq + jnp.sum(value * value, axis=0)

    pl.semaphore_wait(barrier, R - 1 + C - 1)
    ring_start(0, gat1, ORDERS[0])
    joined_sums = group_sums(js, jq, group_matrix(C3, 40, 0, 0), 64)

    loads["lat"].wait()

    def halo_copy(src, dst, index, target):
        return pltpu.make_async_remote_copy(
            src_ref=src,
            dst_ref=dst,
            send_sem=halo_send.at[index],
            recv_sem=halo_recv.at[index],
            device_id=target,
            device_id_type=MESH,
        )

    to_down = halo_copy(lat.at[pl.ds(H1 - 2, 2)], top, 0, {"rows": down})
    to_up = halo_copy(lat.at[pl.ds(0, 2)], bottom, 1, {"rows": up})
    to_down.start()
    to_up.start()

    ls = jnp.zeros((8, C1), F32)
    lq = jnp.zeros((8, C1), F32)
    for i in range(H1):
        value = lat[i].astype(F32).reshape(8, 8, C1)
        ls = ls + jnp.sum(value, axis=0)
        lq = lq + jnp.sum(value * value, axis=0)
    ones1 = group_matrix(C1, 10, 0, 0)
    st_a1[0] = group_sums(ls, lq, ones1, 0) + joined_sums
    spread(st_a1, "rows", 0)
    ring_step(0, gat1, 1, 0, 1, 2)

    to_down.wait()
    to_up.wait()

    def extended_row(i):
        if i < 2:
            return top[i]
        if i < H1 + 2:
            return lat[i - 2]
        return bottom[i - H1 - 2]

    for block in range(3):
        rows_here = [i for i in range(8 * block, 8 * block + 8) if i < H1 + 4]
        tiles = [jnp.zeros((8, C1), F32) for _ in range(4)]
        for i in rows_here:
            value = extended_row(i)
            first = value[0:16].astype(F32)
            last = value[48:64].astype(F32)
            here = iota((8, C1), 0) == i - 8 * block
            for j, piece in enumerate((last[14:15], last[15:16], first[0:1], first[1:2])):
                tiles[j] = jnp.where(here, jnp.broadcast_to(piece, (8, C1)), tiles[j])
        for j in range(4):
            pack[j // 2, j % 2, pl.ds(8 * block, 8), :] = tiles[j]
    to_right = halo_copy(pack.at[0], side.at[0], 2, {"cols": right})
    to_left = halo_copy(pack.at[1], side.at[1], 3, {"cols": left})
    to_right.start()
    to_left.start()

    ring_step(0, gat1, 1, 3)
    st_a2[0] = collect(st_a1, "rows", 0)
    spread(st_a2, "cols", 1)
    ring_step(0, gat1, 2, 0, 1, 2, 3)
    def group_rates(total):
        total = jnp.sum(total, axis=0, keepdims=True)
        total = jnp.broadcast_to(total, (8, 128))
        lane = iota((8, 128), 1)
        count = jnp.where(lane < 64, COUNT1, COUNT3)
        squares = pltpu.roll(total, 96, 1)
        mean = total / count
        spread_of = squares / count - mean * mean
        live = (lane < 32) | ((lane >= 64) & (lane < 96))
        inverse = lax.rsqrt(jnp.where(live, spread_of, 1.0) + EPS)
        return jnp.where(live, mean, 0.0), jnp.where(live, inverse, 0.0)

    def channel_rates(rates, matrix, gain, shift):
        both = exact_dot(jnp.where(iota((8, 128), 0) == 0, *rates), matrix)
        mean, inverse = both[0:1], both[1:2]
        scale = inverse * gain
        return 0.5 * scale, 0.5 * (shift - mean * scale)

    for copy in small:
        copy.wait()
    rates = group_rates(collect(st_a2, "cols", 1))
    scale1, shift1 = channel_rates(rates, group_matrix(C1, 10, 0, 1), flat(g1a), flat(b1a))

    def put_row(i, value, live):
        value = jnp.where(live, halves(value), 0.0)
        act[i, :, 0:C1] = pltpu.roll(value, 1, 0).astype(BF16)
        act[i, :, C1 : 2 * C1] = value.astype(BF16)
        act[i, :, 2 * C1 : 3 * C1] = pltpu.roll(value, WP - 1, 0).astype(BF16)

    place = iota((WP, C1), 0)

    slab_place = iota((16, C1), 0)
    wide_ok = (place < W1) | ((place < W1 + 2) & (col < C - 1)) | ((place >= WP - 2) & (col > 0))

    def act1_rows(first, last):
        for i in range(first, last):
            slab = jnp.zeros((16, C1), F32)
            base = 8 * (i // 8)
            for target, which, j in ((0, 1, 0), (1, 1, 1), (14, 0, 0), (15, 0, 1)):
                piece = side[which, j, pl.ds(base, 8), :][i - base : i - base + 1]
                slab = jnp.where(slab_place == target, jnp.broadcast_to(piece, (16, C1)), slab)
            value = jnp.concatenate([extended_row(i).astype(F32), slab], axis=0)
            live = wide_ok
            if i < 2:
                live = live & (row > 0)
            if i >= H1 + 2:
                live = live & (row < R - 1)
            put_row(i, value * scale1 + shift1, live)

    to_right.wait()
    to_left.wait()
    act1_rows(0, 20)
    ring_step(0, gat1, 3, 0, 1)

    def conv1(weights, first, count, width):
        total = None
        for dy in range(3):
            block = act[pl.ds(first + dy, count), 0:width, :].reshape(count * width, 3 * C1)
            part = jnp.dot(block, weights[dy], preferred_element_type=F32)
            total = part if total is None else total + part
        return total.reshape(count, width, C1)

    def norm3(slot, parts):
        for i in parts:
            value = gat1[slot, i].astype(F32) * scale3 + shift3
            act3[slot, i] = halves(value).astype(BF16)

    def norm_hop(which, gat, norm, hop):
        mate_step(which, gat, hop)
        parts = range(H3) if hop < 4 else ORDERS[which][2 * hop - 8 : 2 * hop - 6]
        for direction in range(1 if hop == 0 or hop >= 4 else 2):
            for k in range(2):
                norm(2 * origin(direction, min(hop, 4)) + k, parts)

    def norm3_hop(hop):
        norm_hop(0, gat1, norm3, hop)

    loads["w1a"].wait()
    hid[pl.ds(0, 6)] = conv1(w1a, 0, 6, WP)
    ring_step(0, gat1, 3, 2, 3)
    scale3, shift3 = channel_rates(rates, group_matrix(C3, 40, 64, 1), flat(g3a), flat(b3a))
    hid[pl.ds(6, 6)] = conv1(w1a, 6, 6, WP)
    for hop in range(4):
        norm3_hop(hop)

    def taps(weights, source, dims, i, first, last):
        prod[i, pl.ds(first, last - first), :] = lax.dot_general(
            weights[pl.ds(first, last - first), :], source(i), dims, preferred_element_type=F32
        )

    BAND = 3 * OC

    def border_taps(*args):
        taps(*args, 0, 2 * BAND, 3 * BAND)
        taps(*args, 3, 0, BAND)

    def other_taps(*args):
        for i in (1, 2):
            taps(*args, i, 0, 3 * BAND)
        taps(*args, 0, 0, 2 * BAND)
        taps(*args, 3, BAND, 3 * BAND)

    lane3 = iota((OC, W3), 1)

    def combine(target):
        columns = []
        for dx in range(3):
            total = None
            for dy in range(3):
                i = target + dy - 1
                if 0 <= i < H3:
                    part = prod[i, pl.ds((3 * dy + dx) * OC, OC), :]
                    total = part if total is None else total + part
            columns.append(total)
        before = jnp.where(lane3 == 0, 0.0, pltpu.roll(columns[0], 1, 1))
        after = jnp.where(lane3 == W3 - 1, 0.0, pltpu.roll(columns[2], W3 - 1, 1))
        return before + columns[1] + after

    def edge_copies(which):
        return [
            pltpu.make_async_remote_copy(
                src_ref=edge_s.at[which, j],
                dst_ref=edge_r.at[which, j],
                send_sem=edge_send.at[which, j],
                recv_sem=edge_recv.at[which, j],
                device_id={"rows": target},
                device_id_type=MESH,
            )
            for j, target in ((0, down), (1, up))
        ]

    def edges_out(which):
        edge_s[which, 0] = combine(H3).astype(BF16)
        edge_s[which, 1] = combine(-1).astype(BF16)
        copies = edge_copies(which)
        for copy in copies:
            copy.start()
        return copies

    def edges_in(which):
        low = jnp.where(row > 0, edge_r[which, 0].astype(F32), 0.0)
        high = jnp.where(row < R - 1, edge_r[which, 1].astype(F32), 0.0)
        return low, high

    loads["w3a"].wait()
    first3 = (w3a, lambda i: act3[:, i].reshape(W3, C3), NT)
    ring_step(0, gat1, 4, 0)
    norm3_hop(4)
    border_taps(*first3)
    copies = edges_out(0)
    ring_step(0, gat1, 4, 1)
    norm3_hop(5)
    other_taps(*first3)
    for i in (1, 2):
        value = combine(i)
        hid3[i] = value
        gat2[col, i] = value.astype(BF16)
    ring_start(1, gat2, (1, 2))
    for i in (0, 3):
        hid3[i] = combine(i)
    for copy in copies:
        copy.wait()
    for i, border in zip((0, 3), edges_in(0)):
        value = hid3[i] + border
        hid3[i] = value
        gat2[col, i] = value.astype(BF16)
    ring_start(1, gat2, (0, 3))

    fs = jnp.zeros((OC, W3), F32)
    fq = jnp.zeros((OC, W3), F32)
    for i in range(H3):
        value = hid3[i]
        fs = fs + value
        fq = fq + value * value
    fs = jnp.sum(fs, axis=1, keepdims=True)
    fq = jnp.sum(fq, axis=1, keepdims=True)
    lane = iota((OC, 128), 1)
    second = iota((OC, 128), 0) >= OC // 2
    group = jnp.where(second, 1, 0)
    laid = jnp.where(lane == group, fs, 0.0) + jnp.where(lane == group + 2, fq, 0.0)
    st_c[0] = jnp.sum(laid.reshape(OC // 8, 8, 128), axis=0)
    spread(st_c, "rows", 4)

    hid[pl.ds(12, 6)] = conv1(w1a, 12, 6, WP)
    hs = jnp.zeros((8, C1), F32)
    hq = jnp.zeros((8, C1), F32)
    for i in range(H1):
        value = hid[i + 1, 0:W1, :].reshape(8, 8, C1)
        hs = hs + jnp.sum(value, axis=0)
        hq = hq + jnp.sum(value * value, axis=0)
    st_b1[0] = group_sums(hs, hq, ones1, 0)
    spread(st_b1, "rows", 2)

    ring_step(1, gat2, 1, 0, 1, 2, 3)

    total = jnp.sum(collect(st_c, "rows", 4), axis=0, keepdims=True)
    total = jnp.broadcast_to(total, (OC, 128)) / COUNT3
    mean = jnp.sum(jnp.where(lane == group, total, 0.0), axis=1, keepdims=True)
    square = jnp.sum(jnp.where(lane == group + 2, total, 0.0), axis=1, keepdims=True)
    inverse = lax.rsqrt(square - mean * mean + EPS)

    def upright(ref):
        eye = iota((OC, OC), 0) == iota((OC, OC), 1)
        return jnp.sum(jnp.where(eye, jnp.broadcast_to(flat(ref), (OC, OC)), 0.0), axis=1, keepdims=True)

    scale4 = inverse * upright(g3b)
    shift4 = 0.5 * (upright(b3b) - mean * scale4)
    scale4 = 0.5 * scale4
    eye = iota((OC, 128), 0) == iota((OC, 128), 1)
    as_rows = [jnp.sum(jnp.where(eye, x, 0.0), axis=0, keepdims=True) for x in (scale4, shift4)]
    st_d[0] = jnp.where(iota((8, 128), 0) == 0, *as_rows)
    spread(st_d, "cols", 5)

    ring_step(1, gat2, 2, 0, 1)
    st_b2[0] = collect(st_b1, "rows", 2)
    spread(st_b2, "cols", 3)

    pick = jnp.where(iota((OC, C3), 1) == iota((OC, C3), 0) + col * OC, 1.0, 0.0).astype(BF16)

    def residual(i, carry):
        res[i] = lax.dot_general(pick, gat1[:, i].reshape(W3, C3), NT, preferred_element_type=F32)
        return carry

    lax.fori_loop(0, H3, residual, 0)
    ring_step(1, gat2, 2, 2, 3)

    rates = group_rates(collect(st_b2, "cols", 3))
    scale2, shift2 = channel_rates(rates, group_matrix(C1, 10, 0, 1), flat(g1b), flat(b1b))
    near_ok = (place < W1) | ((place == W1) & (col < C - 1)) | ((place == WP - 1) & (col > 0))

    def act2_rows(first, last):
        for i in range(first, last):
            live = near_ok
            if i == 0:
                live = live & (row > 0)
            if i == H1 + 1:
                live = live & (row < R - 1)
            put_row(i, hid[i] * scale2 + shift2, live)

    act2_rows(0, 18)
    ring_step(1, gat2, 3, 0, 1)
    loads["w1b"].wait()

    def norm4(slot, parts):
        block = st_d[(col + C - slot) % C]
        scale, shift = (jnp.sum(jnp.where(eye, block[j : j + 1], 0.0), axis=1, keepdims=True) for j in range(2))
        for i in parts:
            act4[slot, i] = halves(gat2[slot, i].astype(F32) * scale + shift).astype(BF16)

    def norm4_hop(hop):
        norm_hop(1, gat2, norm4, hop)

    def out1_rows(first, count):
        value = conv1(w1b, first, count, W1) + flat(c1b).reshape(1, 1, C1)
        o1[pl.ds(first, count)] = (lat[pl.ds(first, count)].astype(F32) + value).astype(BF16)

    out1_rows(0, 4)
    ring_step(1, gat2, 3, 2, 3)
    out1_rows(4, 4)
    arrived(st_d, "cols", 5)
    for hop in range(4):
        norm4_hop(hop)
    loads["w3b"].wait()
    second3 = (w3b, lambda i: act4[:, i].reshape(C3, W3), (((1,), (0,)), ((), ())))
    bias3 = upright(c3b)
    out1_rows(8, 4)
    ring_step(1, gat2, 4, 0)
    norm4_hop(4)
    ring_step(1, gat2, 4, 1)
    norm4_hop(5)
    border_taps(*second3)
    copies = edges_out(1)
    other_taps(*second3)
    out1_rows(12, 4)
    write1 = local(o1, out1_h, 7)
    write1.start()
    for i in range(H3):
        res[i] = res[i] + combine(i) + bias3
    for copy in copies:
        copy.wait()
    low, high = edges_in(1)
    res[0] = res[0] + low
    res[H3 - 1] = res[H3 - 1] + high
    for i in range(H3):
        o3[i] = res[i].astype(BF16)
    write3 = local(o3, out3_h, 8)
    write3.start()
    for copy in sends:
        copy.wait_send()
    write1.wait()
    write3.wait()


def deliver(from1, from3, to1, to3, held1, held3, load_sem, store_sem):
    pieces = [(from3, held3, to3)]
    pieces += [tuple(x.at[pl.ds(4 * i, 4)] for x in (from1, held1, to1)) for i in range(H1 // 4)]
    loads = [pltpu.make_async_copy(a, b, load_sem.at[i]) for i, (a, b, _) in enumerate(pieces)]
    stores = [pltpu.make_async_copy(b, c, store_sem.at[i]) for i, (_, b, c) in enumerate(pieces)]
    for copy in loads:
        copy.start()
    for load, store in zip(loads, stores):
        load.wait()
        store.start()
    for copy in stores:
        copy.wait()


def body(
    latent1, norm1a_g, norm1a_b, conv1a_w, norm1b_g, norm1b_b, conv1b_w, conv1b_b,
    feat3, adapter3, norm3a_g, norm3a_b, conv3a_w, norm3b_g, norm3b_b, conv3b_w, conv3b_b,
):
    def wide(w):
        return w.reshape(3, 3 * C1, C1)

    def tall(w):
        return jnp.swapaxes(w, 2, 3).reshape(9 * OC, C3)

    any_spec = pl.BlockSpec(memory_space=pl.ANY)
    operands = [
        (latent1, any_spec), (norm1a_g, any_spec), (norm1a_b, any_spec), (wide(conv1a_w), any_spec),
        (norm1b_g, any_spec), (norm1b_b, any_spec), (wide(conv1b_w), any_spec), (conv1b_b, any_spec),
        (feat3, any_spec), (adapter3, any_spec), (norm3a_g, any_spec), (norm3a_b, any_spec),
        (tall(conv3a_w), any_spec), (norm3b_g, any_spec), (norm3b_b, any_spec),
        (tall(conv3b_w), any_spec), (conv3b_b, any_spec),
    ]
    out1, out3 = pl.pallas_call(
        kernel,
        out_shape=(
            jax.ShapeDtypeStruct((H1, W1, C1), BF16),
            jax.ShapeDtypeStruct((H3, OC, W3), BF16),
        ),
        in_specs=[spec for _, spec in operands],
        out_specs=(any_spec, any_spec),
        scratch_shapes=[
            *[pltpu.VMEM((n,), F32) for n in (C1, C1, C1, C1, C1, C3, C3, OC, OC, OC)],
            pltpu.VMEM((H1, W1, C1), BF16),
            pltpu.VMEM((2, W1, C1), BF16),
            pltpu.VMEM((2, W1, C1), BF16),
            pltpu.VMEM((2, 2, 24, C1), F32),
            pltpu.VMEM((2, 2, 24, C1), F32),
            pltpu.VMEM((H1 + 4, WP, 3 * C1), BF16),
            pltpu.VMEM((H1 + 2, WP, C1), F32),
            pltpu.VMEM((3, 3 * C1, C1), BF16),
            pltpu.VMEM((3, 3 * C1, C1), BF16),
            pltpu.VMEM((9 * OC, C3), BF16),
            pltpu.VMEM((9 * OC, C3), BF16),
            pltpu.VMEM((H3, 16, C3), BF16),
            pltpu.VMEM((H3, 16, C3), BF16),
            pltpu.VMEM((C, H3, 16, C3), BF16),
            pltpu.VMEM((C, H3, 16, C3), BF16),
            pltpu.VMEM((C, H3, OC, W3), BF16),
            pltpu.VMEM((H3, 9 * OC, W3), F32),
            pltpu.VMEM((2, 2, OC, W3), BF16),
            pltpu.VMEM((2, 2, OC, W3), BF16),
            pltpu.VMEM((H3, OC, W3), F32),
            pltpu.VMEM((H3, OC, W3), F32),
            pltpu.VMEM((H1, W1, C1), BF16),
            pltpu.VMEM((H3, OC, W3), BF16),
            pltpu.VMEM((16, 8, 128), F32),
            pltpu.VMEM((16, 8, 128), F32),
            pltpu.VMEM((16, 8, 128), F32),
            pltpu.VMEM((16, 8, 128), F32),
            pltpu.VMEM((16, 8, 128), F32),
            pltpu.VMEM((16, 8, 128), F32),
            pltpu.VMEM((C, H3, OC, W3), BF16),
            pltpu.SemaphoreType.DMA((19,)),
            pltpu.SemaphoreType.DMA((6,)),
            pltpu.SemaphoreType.DMA((6,)),
            pltpu.SemaphoreType.DMA((2, 2, 4, 4)),
            pltpu.SemaphoreType.DMA((2, 2, 4, 4)),
            pltpu.SemaphoreType.DMA((2, 2, 6)),
            pltpu.SemaphoreType.DMA((2, 2, 6)),
            pltpu.SemaphoreType.DMA((4,)),
            pltpu.SemaphoreType.DMA((4,)),
            pltpu.SemaphoreType.DMA((2, 2)),
            pltpu.SemaphoreType.DMA((2, 2)),
        ],
        compiler_params=pltpu.CompilerParams(
            collective_id=0, has_side_effects=True, vmem_limit_bytes=56 * 1024 * 1024
        ),
    )(*[value for value, _ in operands])
    out1, out3 = pl.pallas_call(
        deliver,
        out_shape=(
            jax.ShapeDtypeStruct((H1, W1, C1), BF16),
            jax.ShapeDtypeStruct((H3, OC, W3), BF16),
        ),
        in_specs=[any_spec, any_spec],
        out_specs=(any_spec, any_spec),
        scratch_shapes=[
            pltpu.VMEM((H1, W1, C1), BF16),
            pltpu.VMEM((H3, OC, W3), BF16),
            pltpu.SemaphoreType.DMA((5,)),
            pltpu.SemaphoreType.DMA((5,)),
        ],
    )(out1, out3)
    return out1, jnp.swapaxes(out3, 1, 2)


def solution(mesh):
    return jax.shard_map(
        body,
        mesh=mesh,
        in_specs=(
            P("rows", "cols", None), P(), P(), P(), P(), P(), P(), P(),
            P("rows", "cols", None), P("rows", "cols", None), P(), P(),
            P(None, None, None, "cols"), P("cols"), P("cols"), P(None, None, None, "cols"), P("cols"),
        ),
        out_specs=(P("rows", "cols", None), P("rows", None, "cols")),
        check_vma=False,
    )
```

```python
import functools

import jax
import jax.numpy as jnp
from jax import lax
from jax.experimental import pallas as pl
from jax.experimental.pallas import tpu as pltpu
from jax.sharding import PartitionSpec as P

MESH = pl.DeviceIdType.MESH
F32 = jnp.float32
BF16 = jnp.bfloat16
EPS = 1e-05
R, C = 16, 16
Z = 8
C1, C3, OC = 320, 1280, 80
H1, W1 = 16, 64
H3, W3 = 4, 256
WP = 80
ORDERS = ((0, 3, 1, 2), (1, 2, 0, 3))
NT = (((1,), (1,)), ((), ()))
COUNT1 = float(R * H1 * C * W1 * (C1 // 32))
COUNT3 = float(R * H3 * W3 * (C3 // 32))


def iota(shape, dim):
    return lax.broadcasted_iota(jnp.int32, shape, dim)


def group_matrix(chans, width, offset, dim):
    shape = (chans, 128) if dim == 0 else (128, chans)
    chan = iota(shape, dim)
    first = (iota(shape, 1 - dim) - offset) * width
    return jnp.where((chan >= first) & (chan < first + width), 1.0, 0.0).astype(BF16)


def exact_dot(a, ones):
    high = a.astype(BF16)
    rest = a - high.astype(F32)
    middle = rest.astype(BF16)
    low = (rest - middle.astype(F32)).astype(BF16)
    n = a.shape[0]
    out = jnp.dot(jnp.concatenate([high, middle, low], axis=0), ones, preferred_element_type=F32)
    return out[0:n] + out[n : 2 * n] + out[2 * n :]


def group_sums(sums, squares, ones, offset):
    both = exact_dot(jnp.concatenate([sums, squares], axis=0), ones)
    first = pltpu.roll(both[0:8], offset, 1) if offset else both[0:8]
    return first + pltpu.roll(both[8:16], offset + 32, 1)


def flat(ref):
    return ref[...].reshape(1, -1)


def halves(value):
    return value + value * jnp.tanh(value)


def kernel(
    lat_h, g1a_h, b1a_h, w1a_h, g1b_h, b1b_h, w1b_h, c1b_h,
    feat_h, adap_h, g3a_h, b3a_h, w3a_h, g3b_h, b3b_h, w3b_h, c3b_h,
    out1_h, out3_h,
    g1a, b1a, g1b, b1b, c1b, g3a, b3a, g3b, b3b, c3b,
    lat, top, bottom, pack, side, act, hid, w1a, w1b, w3a, w3b, feat, adap, gat1, act3, gat2, prod,
    edge_s, edge_r, hid3, res, o1, o3, st_a1, st_a2, st_b1, st_b2, st_c, st_d, act4,
    local_sem, ar_send, ar_recv, ring_send, ring_recv, mate_send, mate_recv,
    halo_send, halo_recv, edge_send, edge_recv,
):
    row = lax.axis_index("rows")
    col = lax.axis_index("cols")
    z = col // 2
    core = col % 2
    up = (row + R - 1) % R
    down = (row + 1) % R
    left = (col + C - 1) % C
    right = (col + 1) % C
    mate = z * 2 + (1 - core)

    def local(src, dst, index):
        return pltpu.make_async_copy(src, dst, local_sem.at[index])

    loads = {
        "feat": local(feat_h, feat, 0),
        "adap": local(adap_h, adap, 1),
        "lat": local(lat_h, lat, 2),
        "w1a": local(w1a_h, w1a, 3),
        "w3a": local(w3a_h, w3a, 4),
        "w1b": local(w1b_h, w1b, 5),
        "w3b": local(w3b_h, w3b, 6),
    }
    small = [
        local(src, dst, 9 + i)
        for i, (src, dst) in enumerate(
            (
                (g1a_h, g1a), (b1a_h, b1a), (g1b_h, g1b), (b1b_h, b1b), (c1b_h, c1b),
                (g3a_h, g3a), (b3a_h, b3a), (g3b_h, g3b), (b3b_h, b3b), (c3b_h, c3b),
            )
        )
    ]
    for name in ("feat", "adap", "lat"):
        loads[name].start()

    barrier = pltpu.get_barrier_semaphore()
    for step in range(1, R):
        pl.semaphore_signal(barrier, inc=1, device_id={"rows": (row + step) % R}, device_id_type=MESH)
    for step in range(1, C):
        pl.semaphore_signal(barrier, inc=1, device_id={"cols": (col + step) % C}, device_id_type=MESH)

    def spread(buf, axis, index):
        me = row if axis == "rows" else col

        def send(step, carry):
            pltpu.make_async_remote_copy(
                src_ref=buf.at[0],
                dst_ref=buf.at[step],
                send_sem=ar_send.at[index],
                recv_sem=ar_recv.at[index],
                device_id={axis: (me + step) % 16},
                device_id_type=MESH,
            ).start()
            return carry

        lax.fori_loop(1, 16, send, 0)

    def arrived(buf, axis, index):
        rest = pltpu.make_async_remote_copy(
            src_ref=buf.at[pl.ds(1, 15)],
            dst_ref=buf.at[pl.ds(1, 15)],
            send_sem=ar_send.at[index],
            recv_sem=ar_recv.at[index],
            device_id={axis: ((row if axis == "rows" else col) + 1) % 16},
            device_id_type=MESH,
        )
        rest.wait_recv()
        rest.wait_send()

    def collect(buf, axis, index):
        arrived(buf, axis, index)
        return jnp.sum(buf[...], axis=0)

    def origin(direction, hop):
        return (z + Z - hop) % Z if direction == 0 else (z + hop) % Z

    def chunk(gat, slot, half):
        return gat.at[slot, half]

    def ring_copy(which, gat, direction, hop, half):
        slot = 2 * origin(direction, hop - 1) + core
        target = 2 * ((z + 1) % Z if direction == 0 else (z + Z - 1) % Z) + core
        return pltpu.make_async_remote_copy(
            src_ref=chunk(gat, slot, half),
            dst_ref=chunk(gat, slot, half),
            send_sem=ring_send.at[which, direction, hop - 1, half],
            recv_sem=ring_recv.at[which, direction, hop - 1, half],
            device_id={"cols": target},
            device_id_type=MESH,
        )

    def ring_wait(which, gat, direction, hop, half):
        slot = 2 * origin(direction, hop) + core
        target = 2 * ((z + 1) % Z if direction == 0 else (z + Z - 1) % Z) + core
        pltpu.make_async_remote_copy(
            src_ref=chunk(gat, slot, half),
            dst_ref=chunk(gat, slot, half),
            send_sem=ring_send.at[which, direction, hop - 1, half],
            recv_sem=ring_recv.at[which, direction, hop - 1, half],
            device_id={"cols": target},
            device_id_type=MESH,
        ).wait_recv()

    def mate_copy(which, gat, direction, hop, side_core):
        part = gat.at[2 * origin(direction, min(hop, 4)) + side_core]
        if hop >= 4:
            part = part.at[dict(arrivals(which, 4, hop - 4))[direction]]
        return pltpu.make_async_remote_copy(
            src_ref=part,
            dst_ref=part,
            send_sem=mate_send.at[which, direction, hop],
            recv_sem=mate_recv.at[which, direction, hop],
            device_id={"cols": mate},
            device_id_type=MESH,
        )

    def arrivals(which, hop, k):
        order = ORDERS[which]
        if hop == 4:
            return list(enumerate(sorted(order[2 * k : 2 * k + 2])))
        return [(0, order[k]), (1, order[k])]

    sends = []

    def go(copy):
        copy.start()
        sends.append(copy)

    def ring_start(which, gat, parts):
        for part in parts:
            for direction in range(2):
                go(ring_copy(which, gat, direction, 1, part))
        if 3 in parts:
            go(mate_copy(which, gat, 0, 0, core))

    def ring_step(which, gat, hop, *ks):
        last = [pair for k in range(2) for pair in arrivals(which, 4, k)]
        for k in ks:
            for direction, part in arrivals(which, hop, k):
                ring_wait(which, gat, direction, hop, part)
                if hop < 3 or (hop == 3 and (direction, part) in last):
                    go(ring_copy(which, gat, direction, hop + 1, part))
                if hop == 4:
                    go(mate_copy(which, gat, direction, 4 + k, core))
                elif k == 3:
                    go(mate_copy(which, gat, direction, hop, core))

    def mate_step(which, gat, hop):
        for direction in range(1 if hop == 0 else 2):
            mate_copy(which, gat, direction, hop, 1 - core).wait_recv()

    loads["feat"].wait()
    loads["adap"].wait()
    for copy in small:
        copy.start()
    for name in ("w1a", "w3a", "w1b", "w3b"):
        loads[name].start()
    js = jnp.zeros((8, C3), F32)
    jq = jnp.zeros((8, C3), F32)
    for i in range(H3):
        value = (feat[i].astype(F32) + adap[i].astype(F32)).astype(BF16)
        gat1[col, i] = value
        value = value.astype(F32).reshape(2, 8, C3)
        js = js + jnp.sum(value, axis=0)
        jq = jq + jnp.sum(value * value, axis=0)

    pl.semaphore_wait(barrier, R - 1 + C - 1)
    ring_start(0, gat1, ORDERS[0])
    joined_sums = group_sums(js, jq, group_matrix(C3, 40, 0, 0), 64)

    loads["lat"].wait()

    def halo_copy(src, dst, index, target):
        return pltpu.make_async_remote_copy(
            src_ref=src,
            dst_ref=dst,
            send_sem=halo_send.at[index],
            recv_sem=halo_recv.at[index],
            device_id=target,
            device_id_type=MESH,
        )

    to_down = halo_copy(lat.at[pl.ds(H1 - 2, 2)], top, 0, {"rows": down})
    to_up = halo_copy(lat.at[pl.ds(0, 2)], bottom, 1, {"rows": up})
    to_down.start()
    to_up.start()

    ls = jnp.zeros((8, C1), F32)
    lq = jnp.zeros((8, C1), F32)
    for i in range(H1):
        value = lat[i].astype(F32).reshape(8, 8, C1)
        ls = ls + jnp.sum(value, axis=0)
        lq = lq + jnp.sum(value * value, axis=0)
    ones1 = group_matrix(C1, 10, 0, 0)
    st_a1[0] = group_sums(ls, lq, ones1, 0) + joined_sums
    spread(st_a1, "rows", 0)
    ring_step(0, gat1, 1, 0, 1, 2)

    to_down.wait()
    to_up.wait()

    def extended_row(i):
        if i < 2:
            return top[i]
        if i < H1 + 2:
            return lat[i - 2]
        return bottom[i - H1 - 2]

    for block in range(3):
        rows_here = [i for i in range(8 * block, 8 * block + 8) if i < H1 + 4]
        tiles = [jnp.zeros((8, C1), F32) for _ in range(4)]
        for i in rows_here:
            value = extended_row(i)
            first = value[0:16].astype(F32)
            last = value[48:64].astype(F32)
            here = iota((8, C1), 0) == i - 8 * block
            for j, piece in enumerate((last[14:15], last[15:16], first[0:1], first[1:2])):
                tiles[j] = jnp.where(here, jnp.broadcast_to(piece, (8, C1)), tiles[j])
        for j in range(4):
            pack[j // 2, j % 2, pl.ds(8 * block, 8), :] = tiles[j]
    to_right = halo_copy(pack.at[0], side.at[0], 2, {"cols": right})
    to_left = halo_copy(pack.at[1], side.at[1], 3, {"cols": left})
    to_right.start()
    to_left.start()

    ring_step(0, gat1, 1, 3)
    st_a2[0] = collect(st_a1, "rows", 0)
    spread(st_a2, "cols", 1)
    ring_step(0, gat1, 2, 0, 1, 2, 3)
    def group_rates(total):
        total = jnp.sum(total, axis=0, keepdims=True)
        total = jnp.broadcast_to(total, (8, 128))
        lane = iota((8, 128), 1)
        count = jnp.where(lane < 64, COUNT1, COUNT3)
        squares = pltpu.roll(total, 96, 1)
        mean = total / count
        spread_of = squares / count - mean * mean
        live = (lane < 32) | ((lane >= 64) & (lane < 96))
        inverse = lax.rsqrt(jnp.where(live, spread_of, 1.0) + EPS)
        return jnp.where(live, mean, 0.0), jnp.where(live, inverse, 0.0)

    def channel_rates(rates, matrix, gain, shift):
        both = exact_dot(jnp.where(iota((8, 128), 0) == 0, *rates), matrix)
        mean, inverse = both[0:1], both[1:2]
        scale = inverse * gain
        return 0.5 * scale, 0.5 * (shift - mean * scale)

    for copy in small:
        copy.wait()
    rates = group_rates(collect(st_a2, "cols", 1))
    scale1, shift1 = channel_rates(rates, group_matrix(C1, 10, 0, 1), flat(g1a), flat(b1a))

    def put_row(i, value, live):
        value = jnp.where(live, halves(value), 0.0)
        act[i, :, 0:C1] = pltpu.roll(value, 1, 0).astype(BF16)
        act[i, :, C1 : 2 * C1] = value.astype(BF16)
        act[i, :, 2 * C1 : 3 * C1] = pltpu.roll(value, WP - 1, 0).astype(BF16)

    place = iota((WP, C1), 0)

    slab_place = iota((16, C1), 0)
    wide_ok = (place < W1) | ((place < W1 + 2) & (col < C - 1)) | ((place >= WP - 2) & (col > 0))

    def act1_rows(first, last):
        for i in range(first, last):
            slab = jnp.zeros((16, C1), F32)
            base = 8 * (i // 8)
            for target, which, j in ((0, 1, 0), (1, 1, 1), (14, 0, 0), (15, 0, 1)):
                piece = side[which, j, pl.ds(base, 8), :][i - base : i - base + 1]
                slab = jnp.where(slab_place == target, jnp.broadcast_to(piece, (16, C1)), slab)
            value = jnp.concatenate([extended_row(i).astype(F32), slab], axis=0)
            live = wide_ok
            if i < 2:
                live = live & (row > 0)
            if i >= H1 + 2:
                live = live & (row < R - 1)
            put_row(i, value * scale1 + shift1, live)

    to_right.wait()
    to_left.wait()
    act1_rows(0, 20)
    ring_step(0, gat1, 3, 0, 1)

    def conv1(weights, first, count, width):
        total = None
        for dy in range(3):
            block = act[pl.ds(first + dy, count), 0:width, :].reshape(count * width, 3 * C1)
            part = jnp.dot(block, weights[dy], preferred_element_type=F32)
            total = part if total is None else total + part
        return total.reshape(count, width, C1)

    def norm3(slot, parts):
        for i in parts:
            value = gat1[slot, i].astype(F32) * scale3 + shift3
            act3[slot, i] = halves(value).astype(BF16)

    def norm_hop(which, gat, norm, hop):
        mate_step(which, gat, hop)
        parts = range(H3) if hop < 4 else ORDERS[which][2 * hop - 8 : 2 * hop - 6]
        for direction in range(1 if hop == 0 or hop >= 4 else 2):
            for k in range(2):
                norm(2 * origin(direction, min(hop, 4)) + k, parts)

    def norm3_hop(hop):
        norm_hop(0, gat1, norm3, hop)

    loads["w1a"].wait()
    hid[pl.ds(0, 6)] = conv1(w1a, 0, 6, WP)
    ring_step(0, gat1, 3, 2, 3)
    scale3, shift3 = channel_rates(rates, group_matrix(C3, 40, 64, 1), flat(g3a), flat(b3a))
    hid[pl.ds(6, 6)] = conv1(w1a, 6, 6, WP)
    for hop in range(4):
        norm3_hop(hop)

    def taps(weights, source, dims, i, first, last):
        prod[i, pl.ds(first, last - first), :] = lax.dot_general(
            weights[pl.ds(first, last - first), :], source(i), dims, preferred_element_type=F32
        )

    BAND = 3 * OC

    def border_taps(*args):
        taps(*args, 0, 2 * BAND, 3 * BAND)
        taps(*args, 3, 0, BAND)

    def other_taps(*args):
        for i in (1, 2):
            taps(*args, i, 0, 3 * BAND)
        taps(*args, 0, 0, 2 * BAND)
        taps(*args, 3, BAND, 3 * BAND)

    lane3 = iota((OC, W3), 1)

    def combine(target):
        columns = []
        for dx in range(3):
            total = None
            for dy in range(3):
                i = target + dy - 1
                if 0 <= i < H3:
                    part = prod[i, pl.ds((3 * dy + dx) * OC, OC), :]
                    total = part if total is None else total + part
            columns.append(total)
        before = jnp.where(lane3 == 0, 0.0, pltpu.roll(columns[0], 1, 1))
        after = jnp.where(lane3 == W3 - 1, 0.0, pltpu.roll(columns[2], W3 - 1, 1))
        return before + columns[1] + after

    def edge_copies(which):
        return [
            pltpu.make_async_remote_copy(
                src_ref=edge_s.at[which, j],
                dst_ref=edge_r.at[which, j],
                send_sem=edge_send.at[which, j],
                recv_sem=edge_recv.at[which, j],
                device_id={"rows": target},
                device_id_type=MESH,
            )
            for j, target in ((0, down), (1, up))
        ]

    def edges_out(which):
        edge_s[which, 0] = combine(H3).astype(BF16)
        edge_s[which, 1] = combine(-1).astype(BF16)
        copies = edge_copies(which)
        for copy in copies:
            copy.start()
        return copies

    def edges_in(which):
        low = jnp.where(row > 0, edge_r[which, 0].astype(F32), 0.0)
        high = jnp.where(row < R - 1, edge_r[which, 1].astype(F32), 0.0)
        return low, high

    loads["w3a"].wait()
    first3 = (w3a, lambda i: act3[:, i].reshape(W3, C3), NT)
    ring_step(0, gat1, 4, 0)
    norm3_hop(4)
    border_taps(*first3)
    copies = edges_out(0)
    ring_step(0, gat1, 4, 1)
    norm3_hop(5)
    other_taps(*first3)
    for i in (1, 2):
        value = combine(i)
        hid3[i] = value
        gat2[col, i] = value.astype(BF16)
    ring_start(1, gat2, (1, 2))
    for i in (0, 3):
        hid3[i] = combine(i)
    for copy in copies:
        copy.wait()
    for i, border in zip((0, 3), edges_in(0)):
        value = hid3[i] + border
        hid3[i] = value
        gat2[col, i] = value.astype(BF16)
    ring_start(1, gat2, (0, 3))

    fs = jnp.zeros((OC, W3), F32)
    fq = jnp.zeros((OC, W3), F32)
    for i in range(H3):
        value = hid3[i]
        fs = fs + value
        fq = fq + value * value
    fs = jnp.sum(fs, axis=1, keepdims=True)
    fq = jnp.sum(fq, axis=1, keepdims=True)
    lane = iota((OC, 128), 1)
    second = iota((OC, 128), 0) >= OC // 2
    group = jnp.where(second, 1, 0)
    laid = jnp.where(lane == group, fs, 0.0) + jnp.where(lane == group + 2, fq, 0.0)
    st_c[0] = jnp.sum(laid.reshape(OC // 8, 8, 128), axis=0)
    spread(st_c, "rows", 4)

    hid[pl.ds(12, 6)] = conv1(w1a, 12, 6, WP)
    hs = jnp.zeros((8, C1), F32)
    hq = jnp.zeros((8, C1), F32)
    for i in range(H1):
        value = hid[i + 1, 0:W1, :].reshape(8, 8, C1)
        hs = hs + jnp.sum(value, axis=0)
        hq = hq + jnp.sum(value * value, axis=0)
    st_b1[0] = group_sums(hs, hq, ones1, 0)
    spread(st_b1, "rows", 2)

    ring_step(1, gat2, 1, 0, 1, 2, 3)

    total = jnp.sum(collect(st_c, "rows", 4), axis=0, keepdims=True)
    total = jnp.broadcast_to(total, (OC, 128)) / COUNT3
    mean = jnp.sum(jnp.where(lane == group, total, 0.0), axis=1, keepdims=True)
    square = jnp.sum(jnp.where(lane == group + 2, total, 0.0), axis=1, keepdims=True)
    inverse = lax.rsqrt(square - mean * mean + EPS)

    def upright(ref):
        eye = iota((OC, OC), 0) == iota((OC, OC), 1)
        return jnp.sum(jnp.where(eye, jnp.broadcast_to(flat(ref), (OC, OC)), 0.0), axis=1, keepdims=True)

    scale4 = inverse * upright(g3b)
    shift4 = 0.5 * (upright(b3b) - mean * scale4)
    scale4 = 0.5 * scale4
    eye = iota((OC, 128), 0) == iota((OC, 128), 1)
    as_rows = [jnp.sum(jnp.where(eye, x, 0.0), axis=0, keepdims=True) for x in (scale4, shift4)]
    st_d[0] = jnp.where(iota((8, 128), 0) == 0, *as_rows)
    spread(st_d, "cols", 5)

    ring_step(1, gat2, 2, 0, 1)
    st_b2[0] = collect(st_b1, "rows", 2)
    spread(st_b2, "cols", 3)

    pick = jnp.where(iota((OC, C3), 1) == iota((OC, C3), 0) + col * OC, 1.0, 0.0).astype(BF16)

    def residual(i, carry):
        res[i] = lax.dot_general(pick, gat1[:, i].reshape(W3, C3), NT, preferred_element_type=F32)
        return carry

    lax.fori_loop(0, H3, residual, 0)
    ring_step(1, gat2, 2, 2, 3)

    def norm4(slot, parts):
        block = st_d[(col + C - slot) % C]
        scale, shift = (jnp.sum(jnp.where(eye, block[j : j + 1], 0.0), axis=1, keepdims=True) for j in range(2))
        for i in parts:
            act4[slot, i] = halves(gat2[slot, i].astype(F32) * scale + shift).astype(BF16)

    def norm4_hop(hop):
        norm_hop(1, gat2, norm4, hop)

    arrived(st_d, "cols", 5)
    norm4_hop(0)
    norm4_hop(1)

    rates = group_rates(collect(st_b2, "cols", 3))
    scale2, shift2 = channel_rates(rates, group_matrix(C1, 10, 0, 1), flat(g1b), flat(b1b))
    near_ok = (place < W1) | ((place == W1) & (col < C - 1)) | ((place == WP - 1) & (col > 0))

    def act2_rows(first, last):
        for i in range(first, last):
            live = near_ok
            if i == 0:
                live = live & (row > 0)
            if i == H1 + 1:
                live = live & (row < R - 1)
            put_row(i, hid[i] * scale2 + shift2, live)

    act2_rows(0, 18)
    ring_step(1, gat2, 3, 0, 1)
    loads["w1b"].wait()

    def out1_rows(first, count):
        value = conv1(w1b, first, count, W1) + flat(c1b).reshape(1, 1, C1)
        o1[pl.ds(first, count)] = (lat[pl.ds(first, count)].astype(F32) + value).astype(BF16)

    out1_rows(0, 4)
    ring_step(1, gat2, 3, 2, 3)
    out1_rows(4, 4)
    norm4_hop(2)
    norm4_hop(3)
    loads["w3b"].wait()
    second3 = (w3b, lambda i: act4[:, i].reshape(C3, W3), (((1,), (0,)), ((), ())))
    bias3 = upright(c3b)
    ring_step(1, gat2, 4, 0)
    norm4_hop(4)
    ring_step(1, gat2, 4, 1)
    norm4_hop(5)
    border_taps(*second3)
    copies = edges_out(1)
    out1_rows(8, 4)
    other_taps(*second3)
    out1_rows(12, 4)
    write1 = local(o1, out1_h, 7)
    write1.start()
    for i in range(H3):
        res[i] = res[i] + combine(i) + bias3
    for copy in copies:
        copy.wait()
    low, high = edges_in(1)
    res[0] = res[0] + low
    res[H3 - 1] = res[H3 - 1] + high
    for i in range(H3):
        o3[i] = res[i].astype(BF16)
    write3 = local(o3, out3_h, 8)
    write3.start()
    for copy in sends:
        copy.wait_send()
    write1.wait()
    write3.wait()


def deliver(from1, from3, to1, to3, held1, held3, load_sem, store_sem):
    pieces = [(from3, held3, to3)]
    pieces += [tuple(x.at[pl.ds(4 * i, 4)] for x in (from1, held1, to1)) for i in range(H1 // 4)]
    loads = [pltpu.make_async_copy(a, b, load_sem.at[i]) for i, (a, b, _) in enumerate(pieces)]
    stores = [pltpu.make_async_copy(b, c, store_sem.at[i]) for i, (_, b, c) in enumerate(pieces)]
    for copy in loads:
        copy.start()
    for load, store in zip(loads, stores):
        load.wait()
        store.start()
    for copy in stores:
        copy.wait()


def body(
    latent1, norm1a_g, norm1a_b, conv1a_w, norm1b_g, norm1b_b, conv1b_w, conv1b_b,
    feat3, adapter3, norm3a_g, norm3a_b, conv3a_w, norm3b_g, norm3b_b, conv3b_w, conv3b_b,
):
    def wide(w):
        return w.reshape(3, 3 * C1, C1)

    def tall(w):
        return jnp.swapaxes(w, 2, 3).reshape(9 * OC, C3)

    any_spec = pl.BlockSpec(memory_space=pl.ANY)
    operands = [
        (latent1, any_spec), (norm1a_g, any_spec), (norm1a_b, any_spec), (wide(conv1a_w), any_spec),
        (norm1b_g, any_spec), (norm1b_b, any_spec), (wide(conv1b_w), any_spec), (conv1b_b, any_spec),
        (feat3, any_spec), (adapter3, any_spec), (norm3a_g, any_spec), (norm3a_b, any_spec),
        (tall(conv3a_w), any_spec), (norm3b_g, any_spec), (norm3b_b, any_spec),
        (tall(conv3b_w), any_spec), (conv3b_b, any_spec),
    ]
    out1, out3 = pl.pallas_call(
        kernel,
        out_shape=(
            jax.ShapeDtypeStruct((H1, W1, C1), BF16),
            jax.ShapeDtypeStruct((H3, OC, W3), BF16),
        ),
        in_specs=[spec for _, spec in operands],
        out_specs=(any_spec, any_spec),
        scratch_shapes=[
            *[pltpu.VMEM((n,), F32) for n in (C1, C1, C1, C1, C1, C3, C3, OC, OC, OC)],
            pltpu.VMEM((H1, W1, C1), BF16),
            pltpu.VMEM((2, W1, C1), BF16),
            pltpu.VMEM((2, W1, C1), BF16),
            pltpu.VMEM((2, 2, 24, C1), F32),
            pltpu.VMEM((2, 2, 24, C1), F32),
            pltpu.VMEM((H1 + 4, WP, 3 * C1), BF16),
            pltpu.VMEM((H1 + 2, WP, C1), F32),
            pltpu.VMEM((3, 3 * C1, C1), BF16),
            pltpu.VMEM((3, 3 * C1, C1), BF16),
            pltpu.VMEM((9 * OC, C3), BF16),
            pltpu.VMEM((9 * OC, C3), BF16),
            pltpu.VMEM((H3, 16, C3), BF16),
            pltpu.VMEM((H3, 16, C3), BF16),
            pltpu.VMEM((C, H3, 16, C3), BF16),
            pltpu.VMEM((C, H3, 16, C3), BF16),
            pltpu.VMEM((C, H3, OC, W3), BF16),
            pltpu.VMEM((H3, 9 * OC, W3), F32),
            pltpu.VMEM((2, 2, OC, W3), BF16),
            pltpu.VMEM((2, 2, OC, W3), BF16),
            pltpu.VMEM((H3, OC, W3), F32),
            pltpu.VMEM((H3, OC, W3), F32),
            pltpu.VMEM((H1, W1, C1), BF16),
            pltpu.VMEM((H3, OC, W3), BF16),
            pltpu.VMEM((16, 8, 128), F32),
            pltpu.VMEM((16, 8, 128), F32),
            pltpu.VMEM((16, 8, 128), F32),
            pltpu.VMEM((16, 8, 128), F32),
            pltpu.VMEM((16, 8, 128), F32),
            pltpu.VMEM((16, 8, 128), F32),
            pltpu.VMEM((C, H3, OC, W3), BF16),
            pltpu.SemaphoreType.DMA((19,)),
            pltpu.SemaphoreType.DMA((6,)),
            pltpu.SemaphoreType.DMA((6,)),
            pltpu.SemaphoreType.DMA((2, 2, 4, 4)),
            pltpu.SemaphoreType.DMA((2, 2, 4, 4)),
            pltpu.SemaphoreType.DMA((2, 2, 6)),
            pltpu.SemaphoreType.DMA((2, 2, 6)),
            pltpu.SemaphoreType.DMA((4,)),
            pltpu.SemaphoreType.DMA((4,)),
            pltpu.SemaphoreType.DMA((2, 2)),
            pltpu.SemaphoreType.DMA((2, 2)),
        ],
        compiler_params=pltpu.CompilerParams(
            collective_id=0, has_side_effects=True, vmem_limit_bytes=56 * 1024 * 1024
        ),
    )(*[value for value, _ in operands])
    out1, out3 = pl.pallas_call(
        deliver,
        out_shape=(
            jax.ShapeDtypeStruct((H1, W1, C1), BF16),
            jax.ShapeDtypeStruct((H3, OC, W3), BF16),
        ),
        in_specs=[any_spec, any_spec],
        out_specs=(any_spec, any_spec),
        scratch_shapes=[
            pltpu.VMEM((H1, W1, C1), BF16),
            pltpu.VMEM((H3, OC, W3), BF16),
            pltpu.SemaphoreType.DMA((5,)),
            pltpu.SemaphoreType.DMA((5,)),
        ],
    )(out1, out3)
    return out1, jnp.swapaxes(out3, 1, 2)


def solution(mesh):
    return jax.shard_map(
        body,
        mesh=mesh,
        in_specs=(
            P("rows", "cols", None), P(), P(), P(), P(), P(), P(), P(),
            P("rows", "cols", None), P("rows", "cols", None), P(), P(),
            P(None, None, None, "cols"), P("cols"), P("cols"), P(None, None, None, "cols"), P("cols"),
        ),
        out_specs=(P("rows", "cols", None), P("rows", None, "cols")),
        check_vma=False,
    )
```

```python
import functools

import jax
import jax.numpy as jnp
from jax import lax
from jax.experimental import pallas as pl
from jax.experimental.pallas import tpu as pltpu
from jax.sharding import PartitionSpec as P

MESH = pl.DeviceIdType.MESH
F32 = jnp.float32
BF16 = jnp.bfloat16
EPS = 1e-05
R, C = 16, 16
Z = 8
C1, C3, OC = 320, 1280, 80
H1, W1 = 16, 64
H3, W3 = 4, 256
WP = 80
ORDERS = ((0, 3, 1, 2), (1, 2, 0, 3))
NT = (((1,), (1,)), ((), ()))
COUNT1 = float(R * H1 * C * W1 * (C1 // 32))
COUNT3 = float(R * H3 * W3 * (C3 // 32))


def iota(shape, dim):
    return lax.broadcasted_iota(jnp.int32, shape, dim)


def group_matrix(chans, width, offset, dim):
    shape = (chans, 128) if dim == 0 else (128, chans)
    chan = iota(shape, dim)
    first = (iota(shape, 1 - dim) - offset) * width
    return jnp.where((chan >= first) & (chan < first + width), 1.0, 0.0).astype(BF16)


def exact_dot(a, ones):
    high = a.astype(BF16)
    rest = a - high.astype(F32)
    middle = rest.astype(BF16)
    low = (rest - middle.astype(F32)).astype(BF16)
    n = a.shape[0]
    out = jnp.dot(jnp.concatenate([high, middle, low], axis=0), ones, preferred_element_type=F32)
    return out[0:n] + out[n : 2 * n] + out[2 * n :]


def group_sums(sums, squares, ones, offset):
    both = exact_dot(jnp.concatenate([sums, squares], axis=0), ones)
    first = pltpu.roll(both[0:8], offset, 1) if offset else both[0:8]
    return first + pltpu.roll(both[8:16], offset + 32, 1)


def flat(ref):
    return ref[...].reshape(1, -1)


def halves(value):
    return value + value * jnp.tanh(value)


def kernel(
    lat_h, g1a_h, b1a_h, w1a_h, g1b_h, b1b_h, w1b_h, c1b_h,
    feat_h, adap_h, g3a_h, b3a_h, w3a_h, g3b_h, b3b_h, w3b_h, c3b_h,
    out1_h, out3_h,
    g1a, b1a, g1b, b1b, c1b, g3a, b3a, g3b, b3b, c3b,
    lat, top, bottom, pack, side, act, hid, w1a, w1b, w3a, w3b, feat, adap, gat1, act3, gat2, prod,
    edge_s, edge_r, hid3, res, o1, o3, st_a1, st_a2, st_b1, st_b2, st_c, st_d, act4,
    local_sem, ar_send, ar_recv, ring_send, ring_recv, mate_send, mate_recv,
    halo_send, halo_recv, edge_send, edge_recv,
):
    row = lax.axis_index("rows")
    col = lax.axis_index("cols")
    z = col // 2
    core = col % 2
    up = (row + R - 1) % R
    down = (row + 1) % R
    left = (col + C - 1) % C
    right = (col + 1) % C
    mate = z * 2 + (1 - core)

    def local(src, dst, index):
        return pltpu.make_async_copy(src, dst, local_sem.at[index])

    loads = {
        "feat": local(feat_h, feat, 0),
        "adap": local(adap_h, adap, 1),
        "lat": local(lat_h, lat, 2),
        "w1a": local(w1a_h, w1a, 3),
        "w3a": local(w3a_h, w3a, 4),
        "w1b": local(w1b_h, w1b, 5),
        "w3b": local(w3b_h, w3b, 6),
    }
    small = [
        local(src, dst, 9 + i)
        for i, (src, dst) in enumerate(
            (
                (g1a_h, g1a), (b1a_h, b1a), (g1b_h, g1b), (b1b_h, b1b), (c1b_h, c1b),
                (g3a_h, g3a), (b3a_h, b3a), (g3b_h, g3b), (b3b_h, b3b), (c3b_h, c3b),
            )
        )
    ]
    for name in ("feat", "adap", "lat"):
        loads[name].start()

    barrier = pltpu.get_barrier_semaphore()
    for step in range(1, R):
        pl.semaphore_signal(barrier, inc=1, device_id={"rows": (row + step) % R}, device_id_type=MESH)
    for step in range(1, C):
        pl.semaphore_signal(barrier, inc=1, device_id={"cols": (col + step) % C}, device_id_type=MESH)

    def spread(buf, axis, index):
        me = row if axis == "rows" else col

        def send(step, carry):
            pltpu.make_async_remote_copy(
                src_ref=buf.at[0],
                dst_ref=buf.at[step],
                send_sem=ar_send.at[index],
                recv_sem=ar_recv.at[index],
                device_id={axis: (me + step) % 16},
                device_id_type=MESH,
            ).start()
            return carry

        lax.fori_loop(1, 16, send, 0)

    def arrived(buf, axis, index):
        rest = pltpu.make_async_remote_copy(
            src_ref=buf.at[pl.ds(1, 15)],
            dst_ref=buf.at[pl.ds(1, 15)],
            send_sem=ar_send.at[index],
            recv_sem=ar_recv.at[index],
            device_id={axis: ((row if axis == "rows" else col) + 1) % 16},
            device_id_type=MESH,
        )
        rest.wait_recv()
        rest.wait_send()

    def collect(buf, axis, index):
        arrived(buf, axis, index)
        return jnp.sum(buf[...], axis=0)

    def origin(direction, hop):
        return (z + Z - hop) % Z if direction == 0 else (z + hop) % Z

    def chunk(gat, slot, half):
        return gat.at[slot, half]

    def ring_copy(which, gat, direction, hop, half):
        slot = 2 * origin(direction, hop - 1) + core
        target = 2 * ((z + 1) % Z if direction == 0 else (z + Z - 1) % Z) + core
        return pltpu.make_async_remote_copy(
            src_ref=chunk(gat, slot, half),
            dst_ref=chunk(gat, slot, half),
            send_sem=ring_send.at[which, direction, hop - 1, half],
            recv_sem=ring_recv.at[which, direction, hop - 1, half],
            device_id={"cols": target},
            device_id_type=MESH,
        )

    def ring_wait(which, gat, direction, hop, half):
        slot = 2 * origin(direction, hop) + core
        target = 2 * ((z + 1) % Z if direction == 0 else (z + Z - 1) % Z) + core
        pltpu.make_async_remote_copy(
            src_ref=chunk(gat, slot, half),
            dst_ref=chunk(gat, slot, half),
            send_sem=ring_send.at[which, direction, hop - 1, half],
            recv_sem=ring_recv.at[which, direction, hop - 1, half],
            device_id={"cols": target},
            device_id_type=MESH,
        ).wait_recv()

    def mate_copy(which, gat, direction, hop, side_core):
        part = gat.at[2 * origin(direction, min(hop, 4)) + side_core]
        if hop >= 4:
            part = part.at[dict(arrivals(which, 4, hop - 4))[direction]]
        return pltpu.make_async_remote_copy(
            src_ref=part,
            dst_ref=part,
            send_sem=mate_send.at[which, direction, hop],
            recv_sem=mate_recv.at[which, direction, hop],
            device_id={"cols": mate},
            device_id_type=MESH,
        )

    def arrivals(which, hop, k):
        order = ORDERS[which]
        if hop == 4:
            return list(enumerate(sorted(order[2 * k : 2 * k + 2])))
        return [(0, order[k]), (1, order[k])]

    sends = []

    def go(copy):
        copy.start()
        sends.append(copy)

    def ring_start(which, gat, parts):
        for part in parts:
            for direction in range(2):
                go(ring_copy(which, gat, direction, 1, part))
        if 3 in parts:
            go(mate_copy(which, gat, 0, 0, core))

    def ring_step(which, gat, hop, *ks):
        last = [pair for k in range(2) for pair in arrivals(which, 4, k)]
        for k in ks:
            for direction, part in arrivals(which, hop, k):
                ring_wait(which, gat, direction, hop, part)
                if hop < 3 or (hop == 3 and (direction, part) in last):
                    go(ring_copy(which, gat, direction, hop + 1, part))
                if hop == 4:
                    go(mate_copy(which, gat, direction, 4 + k, core))
                elif k == 3:
                    go(mate_copy(which, gat, direction, hop, core))

    def mate_step(which, gat, hop):
        for direction in range(1 if hop == 0 else 2):
            mate_copy(which, gat, direction, hop, 1 - core).wait_recv()

    loads["feat"].wait()
    loads["adap"].wait()
    for copy in small:
        copy.start()
    for name in ("w1a", "w3a", "w1b", "w3b"):
        loads[name].start()
    js = jnp.zeros((8, C3), F32)
    jq = jnp.zeros((8, C3), F32)
    for i in range(H3):
        value = (feat[i].astype(F32) + adap[i].astype(F32)).astype(BF16)
        gat1[col, i] = value
        value = value.astype(F32).reshape(2, 8, C3)
        js = js + jnp.sum(value, axis=0)
        jq = jq + jnp.sum(value * value, axis=0)

    pl.semaphore_wait(barrier, R - 1 + C - 1)
    ring_start(0, gat1, ORDERS[0])
    joined_sums = group_sums(js, jq, group_matrix(C3, 40, 0, 0), 64)

    loads["lat"].wait()

    def halo_copy(src, dst, index, target):
        return pltpu.make_async_remote_copy(
            src_ref=src,
            dst_ref=dst,
            send_sem=halo_send.at[index],
            recv_sem=halo_recv.at[index],
            device_id=target,
            device_id_type=MESH,
        )

    to_down = halo_copy(lat.at[pl.ds(H1 - 2, 2)], top, 0, {"rows": down})
    to_up = halo_copy(lat.at[pl.ds(0, 2)], bottom, 1, {"rows": up})
    to_down.start()
    to_up.start()

    ls = jnp.zeros((8, C1), F32)
    lq = jnp.zeros((8, C1), F32)
    for i in range(H1):
        value = lat[i].astype(F32).reshape(8, 8, C1)
        ls = ls + jnp.sum(value, axis=0)
        lq = lq + jnp.sum(value * value, axis=0)
    ones1 = group_matrix(C1, 10, 0, 0)
    st_a1[0] = group_sums(ls, lq, ones1, 0) + joined_sums
    spread(st_a1, "rows", 0)
    ring_step(0, gat1, 1, 0, 1, 2)

    to_down.wait()
    to_up.wait()

    def extended_row(i):
        if i < 2:
            return top[i]
        if i < H1 + 2:
            return lat[i - 2]
        return bottom[i - H1 - 2]

    for block in range(3):
        rows_here = [i for i in range(8 * block, 8 * block + 8) if i < H1 + 4]
        tiles = [jnp.zeros((8, C1), F32) for _ in range(4)]
        for i in rows_here:
            value = extended_row(i)
            first = value[0:16].astype(F32)
            last = value[48:64].astype(F32)
            here = iota((8, C1), 0) == i - 8 * block
            for j, piece in enumerate((last[14:15], last[15:16], first[0:1], first[1:2])):
                tiles[j] = jnp.where(here, jnp.broadcast_to(piece, (8, C1)), tiles[j])
        for j in range(4):
            pack[j // 2, j % 2, pl.ds(8 * block, 8), :] = tiles[j]
    to_right = halo_copy(pack.at[0], side.at[0], 2, {"cols": right})
    to_left = halo_copy(pack.at[1], side.at[1], 3, {"cols": left})
    to_right.start()
    to_left.start()

    ring_step(0, gat1, 1, 3)
    st_a2[0] = collect(st_a1, "rows", 0)
    spread(st_a2, "cols", 1)
    ring_step(0, gat1, 2, 0, 1, 2, 3)
    def group_rates(total):
        total = jnp.sum(total, axis=0, keepdims=True)
        total = jnp.broadcast_to(total, (8, 128))
        lane = iota((8, 128), 1)
        count = jnp.where(lane < 64, COUNT1, COUNT3)
        squares = pltpu.roll(total, 96, 1)
        mean = total / count
        spread_of = squares / count - mean * mean
        live = (lane < 32) | ((lane >= 64) & (lane < 96))
        inverse = lax.rsqrt(jnp.where(live, spread_of, 1.0) + EPS)
        return jnp.where(live, mean, 0.0), jnp.where(live, inverse, 0.0)

    def channel_rates(rates, matrix, gain, shift):
        both = exact_dot(jnp.where(iota((8, 128), 0) == 0, *rates), matrix)
        mean, inverse = both[0:1], both[1:2]
        scale = inverse * gain
        return 0.5 * scale, 0.5 * (shift - mean * scale)

    for copy in small:
        copy.wait()
    rates = group_rates(collect(st_a2, "cols", 1))
    scale1, shift1 = channel_rates(rates, group_matrix(C1, 10, 0, 1), flat(g1a), flat(b1a))

    def put_row(i, value, live):
        value = jnp.where(live, halves(value), 0.0)
        act[i, :, 0:C1] = pltpu.roll(value, 1, 0).astype(BF16)
        act[i, :, C1 : 2 * C1] = value.astype(BF16)
        act[i, :, 2 * C1 : 3 * C1] = pltpu.roll(value, WP - 1, 0).astype(BF16)

    place = iota((WP, C1), 0)

    slab_place = iota((16, C1), 0)
    wide_ok = (place < W1) | ((place < W1 + 2) & (col < C - 1)) | ((place >= WP - 2) & (col > 0))

    def act1_rows(first, last):
        for i in range(first, last):
            slab = jnp.zeros((16, C1), F32)
            base = 8 * (i // 8)
            for target, which, j in ((0, 1, 0), (1, 1, 1), (14, 0, 0), (15, 0, 1)):
                piece = side[which, j, pl.ds(base, 8), :][i - base : i - base + 1]
                slab = jnp.where(slab_place == target, jnp.broadcast_to(piece, (16, C1)), slab)
            value = jnp.concatenate([extended_row(i).astype(F32), slab], axis=0)
            live = wide_ok
            if i < 2:
                live = live & (row > 0)
            if i >= H1 + 2:
                live = live & (row < R - 1)
            put_row(i, value * scale1 + shift1, live)

    to_right.wait()
    to_left.wait()
    act1_rows(0, 20)
    ring_step(0, gat1, 3, 0, 1)

    def conv1(weights, first, count, width):
        total = None
        for dy in range(3):
            block = act[pl.ds(first + dy, count), 0:width, :].reshape(count * width, 3 * C1)
            part = jnp.dot(block, weights[dy], preferred_element_type=F32)
            total = part if total is None else total + part
        return total.reshape(count, width, C1)

    def norm3(slot, parts):
        for i in parts:
            value = gat1[slot, i].astype(F32) * scale3 + shift3
            act3[slot, i] = halves(value).astype(BF16)

    def norm_hop(which, gat, norm, hop):
        mate_step(which, gat, hop)
        parts = range(H3) if hop < 4 else ORDERS[which][2 * hop - 8 : 2 * hop - 6]
        for direction in range(1 if hop == 0 or hop >= 4 else 2):
            for k in range(2):
                norm(2 * origin(direction, min(hop, 4)) + k, parts)

    def norm3_hop(hop):
        norm_hop(0, gat1, norm3, hop)

    loads["w1a"].wait()
    hid[pl.ds(0, 6)] = conv1(w1a, 0, 6, WP)
    ring_step(0, gat1, 3, 2, 3)
    scale3, shift3 = channel_rates(rates, group_matrix(C3, 40, 64, 1), flat(g3a), flat(b3a))
    hid[pl.ds(6, 6)] = conv1(w1a, 6, 6, WP)
    for hop in range(4):
        norm3_hop(hop)

    def taps(weights, source, dims, i, first, last):
        prod[i, pl.ds(first, last - first), :] = lax.dot_general(
            weights[pl.ds(first, last - first), :], source(i), dims, preferred_element_type=F32
        )

    BAND = 3 * OC

    def border_taps(*args):
        taps(*args, 0, 2 * BAND, 3 * BAND)
        taps(*args, 3, 0, BAND)

    def other_taps(*args):
        for i in (1, 2):
            taps(*args, i, 0, 3 * BAND)
        taps(*args, 0, 0, 2 * BAND)
        taps(*args, 3, BAND, 3 * BAND)

    lane3 = iota((OC, W3), 1)

    def combine(target):
        columns = []
        for dx in range(3):
            total = None
            for dy in range(3):
                i = target + dy - 1
                if 0 <= i < H3:
                    part = prod[i, pl.ds((3 * dy + dx) * OC, OC), :]
                    total = part if total is None else total + part
            columns.append(total)
        before = jnp.where(lane3 == 0, 0.0, pltpu.roll(columns[0], 1, 1))
        after = jnp.where(lane3 == W3 - 1, 0.0, pltpu.roll(columns[2], W3 - 1, 1))
        return before + columns[1] + after

    def edge_copies(which):
        return [
            pltpu.make_async_remote_copy(
                src_ref=edge_s.at[which, j],
                dst_ref=edge_r.at[which, j],
                send_sem=edge_send.at[which, j],
                recv_sem=edge_recv.at[which, j],
                device_id={"rows": target},
                device_id_type=MESH,
            )
            for j, target in ((0, down), (1, up))
        ]

    def edges_out(which):
        edge_s[which, 0] = combine(H3).astype(BF16)
        edge_s[which, 1] = combine(-1).astype(BF16)
        copies = edge_copies(which)
        for copy in copies:
            copy.start()
        return copies

    def edges_in(which):
        low = jnp.where(row > 0, edge_r[which, 0].astype(F32), 0.0)
        high = jnp.where(row < R - 1, edge_r[which, 1].astype(F32), 0.0)
        return low, high

    loads["w3a"].wait()
    first3 = (w3a, lambda i: act3[:, i].reshape(W3, C3), NT)
    ring_step(0, gat1, 4, 0)
    norm3_hop(4)
    border_taps(*first3)
    copies = edges_out(0)
    ring_step(0, gat1, 4, 1)
    norm3_hop(5)
    other_taps(*first3)
    for i in (1, 2):
        value = combine(i)
        hid3[i] = value
        gat2[col, i] = value.astype(BF16)
    ring_start(1, gat2, (1, 2))
    for i in (0, 3):
        hid3[i] = combine(i)
    for copy in copies:
        copy.wait()
    for i, border in zip((0, 3), edges_in(0)):
        value = hid3[i] + border
        hid3[i] = value
        gat2[col, i] = value.astype(BF16)
    ring_start(1, gat2, (0, 3))

    fs = jnp.zeros((OC, W3), F32)
    fq = jnp.zeros((OC, W3), F32)
    for i in range(H3):
        value = hid3[i]
        fs = fs + value
        fq = fq + value * value
    fs = jnp.sum(fs, axis=1, keepdims=True)
    fq = jnp.sum(fq, axis=1, keepdims=True)
    lane = iota((OC, 128), 1)
    second = iota((OC, 128), 0) >= OC // 2
    group = jnp.where(second, 1, 0)
    laid = jnp.where(lane == group, fs, 0.0) + jnp.where(lane == group + 2, fq, 0.0)
    st_c[0] = jnp.sum(laid.reshape(OC // 8, 8, 128), axis=0)
    spread(st_c, "rows", 4)

    hid[pl.ds(12, 6)] = conv1(w1a, 12, 6, WP)
    hs = jnp.zeros((8, C1), F32)
    hq = jnp.zeros((8, C1), F32)
    for i in range(H1):
        value = hid[i + 1, 0:W1, :].reshape(8, 8, C1)
        hs = hs + jnp.sum(value, axis=0)
        hq = hq + jnp.sum(value * value, axis=0)
    st_b1[0] = group_sums(hs, hq, ones1, 0)
    spread(st_b1, "rows", 2)

    ring_step(1, gat2, 1, 0, 1, 2, 3)

    total = jnp.sum(collect(st_c, "rows", 4), axis=0, keepdims=True)
    total = jnp.broadcast_to(total, (OC, 128)) / COUNT3
    mean = jnp.sum(jnp.where(lane == group, total, 0.0), axis=1, keepdims=True)
    square = jnp.sum(jnp.where(lane == group + 2, total, 0.0), axis=1, keepdims=True)
    inverse = lax.rsqrt(square - mean * mean + EPS)

    def upright(ref):
        eye = iota((OC, OC), 0) == iota((OC, OC), 1)
        return jnp.sum(jnp.where(eye, jnp.broadcast_to(flat(ref), (OC, OC)), 0.0), axis=1, keepdims=True)

    scale4 = inverse * upright(g3b)
    shift4 = 0.5 * (upright(b3b) - mean * scale4)
    scale4 = 0.5 * scale4
    eye = iota((OC, 128), 0) == iota((OC, 128), 1)
    as_rows = [jnp.sum(jnp.where(eye, x, 0.0), axis=0, keepdims=True) for x in (scale4, shift4)]
    st_d[0] = jnp.where(iota((8, 128), 0) == 0, *as_rows)
    spread(st_d, "cols", 5)

    st_b2[0] = collect(st_b1, "rows", 2)
    spread(st_b2, "cols", 3)
    ring_step(1, gat2, 2, 0, 1)

    pick = jnp.where(iota((OC, C3), 1) == iota((OC, C3), 0) + col * OC, 1.0, 0.0).astype(BF16)

    def residual(i, carry):
        res[i] = lax.dot_general(pick, gat1[:, i].reshape(W3, C3), NT, preferred_element_type=F32)
        return carry

    lax.fori_loop(0, H3, residual, 0)
    ring_step(1, gat2, 2, 2, 3)

    def norm4(slot, parts):
        block = st_d[(col + C - slot) % C]
        scale, shift = (jnp.sum(jnp.where(eye, block[j : j + 1], 0.0), axis=1, keepdims=True) for j in range(2))
        for i in parts:
            act4[slot, i] = halves(gat2[slot, i].astype(F32) * scale + shift).astype(BF16)

    def norm4_hop(hop):
        norm_hop(1, gat2, norm4, hop)

    arrived(st_d, "cols", 5)
    norm4_hop(0)
    norm4_hop(1)

    rates = group_rates(collect(st_b2, "cols", 3))
    scale2, shift2 = channel_rates(rates, group_matrix(C1, 10, 0, 1), flat(g1b), flat(b1b))
    near_ok = (place < W1) | ((place == W1) & (col < C - 1)) | ((place == WP - 1) & (col > 0))

    def act2_rows(first, last):
        for i in range(first, last):
            live = near_ok
            if i == 0:
                live = live & (row > 0)
            if i == H1 + 1:
                live = live & (row < R - 1)
            put_row(i, hid[i] * scale2 + shift2, live)

    act2_rows(0, 18)
    ring_step(1, gat2, 3, 0, 1)
    loads["w1b"].wait()

    def out1_rows(first, count):
        value = conv1(w1b, first, count, W1) + flat(c1b).reshape(1, 1, C1)
        o1[pl.ds(first, count)] = (lat[pl.ds(first, count)].astype(F32) + value).astype(BF16)

    out1_rows(0, 4)
    ring_step(1, gat2, 3, 2, 3)
    out1_rows(4, 4)
    norm4_hop(2)
    norm4_hop(3)
    loads["w3b"].wait()
    second3 = (w3b, lambda i: act4[:, i].reshape(C3, W3), (((1,), (0,)), ((), ())))
    bias3 = upright(c3b)
    ring_step(1, gat2, 4, 0)
    norm4_hop(4)
    ring_step(1, gat2, 4, 1)
    norm4_hop(5)
    border_taps(*second3)
    copies = edges_out(1)
    out1_rows(8, 4)
    other_taps(*second3)
    out1_rows(12, 4)
    write1 = local(o1, out1_h, 7)
    write1.start()
    for i in range(H3):
        res[i] = res[i] + combine(i) + bias3
    for copy in copies:
        copy.wait()
    low, high = edges_in(1)
    res[0] = res[0] + low
    res[H3 - 1] = res[H3 - 1] + high
    for i in range(H3):
        o3[i] = res[i].astype(BF16)
    write3 = local(o3, out3_h, 8)
    write3.start()
    for copy in sends:
        copy.wait_send()
    write1.wait()
    write3.wait()


def deliver(from1, from3, to1, to3, held1, held3, load_sem, store_sem):
    pieces = [(from3, held3, to3)]
    pieces += [tuple(x.at[pl.ds(4 * i, 4)] for x in (from1, held1, to1)) for i in range(H1 // 4)]
    loads = [pltpu.make_async_copy(a, b, load_sem.at[i]) for i, (a, b, _) in enumerate(pieces)]
    stores = [pltpu.make_async_copy(b, c, store_sem.at[i]) for i, (_, b, c) in enumerate(pieces)]
    for copy in loads:
        copy.start()
    for load, store in zip(loads, stores):
        load.wait()
        store.start()
    for copy in stores:
        copy.wait()


def body(
    latent1, norm1a_g, norm1a_b, conv1a_w, norm1b_g, norm1b_b, conv1b_w, conv1b_b,
    feat3, adapter3, norm3a_g, norm3a_b, conv3a_w, norm3b_g, norm3b_b, conv3b_w, conv3b_b,
):
    def wide(w):
        return w.reshape(3, 3 * C1, C1)

    def tall(w):
        return jnp.swapaxes(w, 2, 3).reshape(9 * OC, C3)

    any_spec = pl.BlockSpec(memory_space=pl.ANY)
    operands = [
        (latent1, any_spec), (norm1a_g, any_spec), (norm1a_b, any_spec), (wide(conv1a_w), any_spec),
        (norm1b_g, any_spec), (norm1b_b, any_spec), (wide(conv1b_w), any_spec), (conv1b_b, any_spec),
        (feat3, any_spec), (adapter3, any_spec), (norm3a_g, any_spec), (norm3a_b, any_spec),
        (tall(conv3a_w), any_spec), (norm3b_g, any_spec), (norm3b_b, any_spec),
        (tall(conv3b_w), any_spec), (conv3b_b, any_spec),
    ]
    out1, out3 = pl.pallas_call(
        kernel,
        out_shape=(
            jax.ShapeDtypeStruct((H1, W1, C1), BF16),
            jax.ShapeDtypeStruct((H3, OC, W3), BF16),
        ),
        in_specs=[spec for _, spec in operands],
        out_specs=(any_spec, any_spec),
        scratch_shapes=[
            *[pltpu.VMEM((n,), F32) for n in (C1, C1, C1, C1, C1, C3, C3, OC, OC, OC)],
            pltpu.VMEM((H1, W1, C1), BF16),
            pltpu.VMEM((2, W1, C1), BF16),
            pltpu.VMEM((2, W1, C1), BF16),
            pltpu.VMEM((2, 2, 24, C1), F32),
            pltpu.VMEM((2, 2, 24, C1), F32),
            pltpu.VMEM((H1 + 4, WP, 3 * C1), BF16),
            pltpu.VMEM((H1 + 2, WP, C1), F32),
            pltpu.VMEM((3, 3 * C1, C1), BF16),
            pltpu.VMEM((3, 3 * C1, C1), BF16),
            pltpu.VMEM((9 * OC, C3), BF16),
            pltpu.VMEM((9 * OC, C3), BF16),
            pltpu.VMEM((H3, 16, C3), BF16),
            pltpu.VMEM((H3, 16, C3), BF16),
            pltpu.VMEM((C, H3, 16, C3), BF16),
            pltpu.VMEM((C, H3, 16, C3), BF16),
            pltpu.VMEM((C, H3, OC, W3), BF16),
            pltpu.VMEM((H3, 9 * OC, W3), F32),
            pltpu.VMEM((2, 2, OC, W3), BF16),
            pltpu.VMEM((2, 2, OC, W3), BF16),
            pltpu.VMEM((H3, OC, W3), F32),
            pltpu.VMEM((H3, OC, W3), F32),
            pltpu.VMEM((H1, W1, C1), BF16),
            pltpu.VMEM((H3, OC, W3), BF16),
            pltpu.VMEM((16, 8, 128), F32),
            pltpu.VMEM((16, 8, 128), F32),
            pltpu.VMEM((16, 8, 128), F32),
            pltpu.VMEM((16, 8, 128), F32),
            pltpu.VMEM((16, 8, 128), F32),
            pltpu.VMEM((16, 8, 128), F32),
            pltpu.VMEM((C, H3, OC, W3), BF16),
            pltpu.SemaphoreType.DMA((19,)),
            pltpu.SemaphoreType.DMA((6,)),
            pltpu.SemaphoreType.DMA((6,)),
            pltpu.SemaphoreType.DMA((2, 2, 4, 4)),
            pltpu.SemaphoreType.DMA((2, 2, 4, 4)),
            pltpu.SemaphoreType.DMA((2, 2, 6)),
            pltpu.SemaphoreType.DMA((2, 2, 6)),
            pltpu.SemaphoreType.DMA((4,)),
            pltpu.SemaphoreType.DMA((4,)),
            pltpu.SemaphoreType.DMA((2, 2)),
            pltpu.SemaphoreType.DMA((2, 2)),
        ],
        compiler_params=pltpu.CompilerParams(
            collective_id=0, has_side_effects=True, vmem_limit_bytes=56 * 1024 * 1024
        ),
    )(*[value for value, _ in operands])
    out1, out3 = pl.pallas_call(
        deliver,
        out_shape=(
            jax.ShapeDtypeStruct((H1, W1, C1), BF16),
            jax.ShapeDtypeStruct((H3, OC, W3), BF16),
        ),
        in_specs=[any_spec, any_spec],
        out_specs=(any_spec, any_spec),
        scratch_shapes=[
            pltpu.VMEM((H1, W1, C1), BF16),
            pltpu.VMEM((H3, OC, W3), BF16),
            pltpu.SemaphoreType.DMA((5,)),
            pltpu.SemaphoreType.DMA((5,)),
        ],
    )(out1, out3)
    return out1, jnp.swapaxes(out3, 1, 2)


def solution(mesh):
    return jax.shard_map(
        body,
        mesh=mesh,
        in_specs=(
            P("rows", "cols", None), P(), P(), P(), P(), P(), P(), P(),
            P("rows", "cols", None), P("rows", "cols", None), P(), P(),
            P(None, None, None, "cols"), P("cols"), P("cols"), P(None, None, None, "cols"), P("cols"),
        ),
        out_specs=(P("rows", "cols", None), P("rows", None, "cols")),
        check_vma=False,
    )
```

```python
import functools

import jax
import jax.numpy as jnp
from jax import lax
from jax.experimental import pallas as pl
from jax.experimental.pallas import tpu as pltpu
from jax.sharding import PartitionSpec as P

MESH = pl.DeviceIdType.MESH
F32 = jnp.float32
BF16 = jnp.bfloat16
EPS = 1e-05
R, C = 16, 16
Z = 8
C1, C3, OC = 320, 1280, 80
H1, W1 = 16, 64
H3, W3 = 4, 256
WP = 80
ORDERS = ((0, 3, 1, 2), (1, 2, 0, 3))
NT = (((1,), (1,)), ((), ()))
COUNT1 = float(R * H1 * C * W1 * (C1 // 32))
COUNT3 = float(R * H3 * W3 * (C3 // 32))


def iota(shape, dim):
    return lax.broadcasted_iota(jnp.int32, shape, dim)


def group_matrix(chans, width, offset, dim):
    shape = (chans, 128) if dim == 0 else (128, chans)
    chan = iota(shape, dim)
    first = (iota(shape, 1 - dim) - offset) * width
    return jnp.where((chan >= first) & (chan < first + width), 1.0, 0.0).astype(BF16)


def exact_dot(a, ones):
    high = a.astype(BF16)
    rest = a - high.astype(F32)
    middle = rest.astype(BF16)
    low = (rest - middle.astype(F32)).astype(BF16)
    n = a.shape[0]
    out = jnp.dot(jnp.concatenate([high, middle, low], axis=0), ones, preferred_element_type=F32)
    return out[0:n] + out[n : 2 * n] + out[2 * n :]


def group_sums(sums, squares, ones, offset):
    both = exact_dot(jnp.concatenate([sums, squares], axis=0), ones)
    first = pltpu.roll(both[0:8], offset, 1) if offset else both[0:8]
    return first + pltpu.roll(both[8:16], offset + 32, 1)


def flat(ref):
    return ref[...].reshape(1, -1)


def halves(value):
    return value + value * jnp.tanh(value)


def kernel(
    lat_h, g1a_h, b1a_h, w1a_h, g1b_h, b1b_h, w1b_h, c1b_h,
    feat_h, adap_h, g3a_h, b3a_h, w3a_h, g3b_h, b3b_h, w3b_h, c3b_h,
    out1_h, out3_h,
    g1a, b1a, g1b, b1b, c1b, g3a, b3a, g3b, b3b, c3b,
    lat, top, bottom, pack, side, act, hid, w1a, w1b, w3a, w3b, feat, adap, gat1, act3, gat2, prod,
    edge_s, edge_r, hid3, res, o1, o3, st_a1, st_a2, st_b1, st_b2, st_c, st_d, act4,
    local_sem, ar_send, ar_recv, ring_send, ring_recv, mate_send, mate_recv,
    halo_send, halo_recv, edge_send, edge_recv,
):
    row = lax.axis_index("rows")
    col = lax.axis_index("cols")
    z = col // 2
    core = col % 2
    up = (row + R - 1) % R
    down = (row + 1) % R
    left = (col + C - 1) % C
    right = (col + 1) % C
    mate = z * 2 + (1 - core)

    def local(src, dst, index):
        return pltpu.make_async_copy(src, dst, local_sem.at[index])

    loads = {
        "feat": local(feat_h, feat, 0),
        "adap": local(adap_h, adap, 1),
        "lat": local(lat_h, lat, 2),
        "w1a": local(w1a_h, w1a, 3),
        "w3a": local(w3a_h, w3a, 4),
        "w1b": local(w1b_h, w1b, 5),
        "w3b": local(w3b_h, w3b, 6),
    }
    small = [
        local(src, dst, 9 + i)
        for i, (src, dst) in enumerate(
            (
                (g1a_h, g1a), (b1a_h, b1a), (g1b_h, g1b), (b1b_h, b1b), (c1b_h, c1b),
                (g3a_h, g3a), (b3a_h, b3a), (g3b_h, g3b), (b3b_h, b3b), (c3b_h, c3b),
            )
        )
    ]
    for name in ("feat", "adap", "lat"):
        loads[name].start()

    barrier = pltpu.get_barrier_semaphore()
    for step in range(1, R):
        pl.semaphore_signal(barrier, inc=1, device_id={"rows": (row + step) % R}, device_id_type=MESH)
    for step in range(1, C):
        pl.semaphore_signal(barrier, inc=1, device_id={"cols": (col + step) % C}, device_id_type=MESH)

    def spread(buf, axis, index):
        me = row if axis == "rows" else col

        def send(step, carry):
            pltpu.make_async_remote_copy(
                src_ref=buf.at[0],
                dst_ref=buf.at[step],
                send_sem=ar_send.at[index],
                recv_sem=ar_recv.at[index],
                device_id={axis: (me + step) % 16},
                device_id_type=MESH,
            ).start()
            return carry

        lax.fori_loop(1, 16, send, 0)

    def arrived(buf, axis, index):
        rest = pltpu.make_async_remote_copy(
            src_ref=buf.at[pl.ds(1, 15)],
            dst_ref=buf.at[pl.ds(1, 15)],
            send_sem=ar_send.at[index],
            recv_sem=ar_recv.at[index],
            device_id={axis: ((row if axis == "rows" else col) + 1) % 16},
            device_id_type=MESH,
        )
        rest.wait_recv()
        rest.wait_send()

    def collect(buf, axis, index):
        arrived(buf, axis, index)
        return jnp.sum(buf[...], axis=0)

    def origin(direction, hop):
        return (z + Z - hop) % Z if direction == 0 else (z + hop) % Z

    def chunk(gat, slot, half):
        return gat.at[slot, half]

    def ring_copy(which, gat, direction, hop, half):
        slot = 2 * origin(direction, hop - 1) + core
        target = 2 * ((z + 1) % Z if direction == 0 else (z + Z - 1) % Z) + core
        return pltpu.make_async_remote_copy(
            src_ref=chunk(gat, slot, half),
            dst_ref=chunk(gat, slot, half),
            send_sem=ring_send.at[which, direction, hop - 1, half],
            recv_sem=ring_recv.at[which, direction, hop - 1, half],
            device_id={"cols": target},
            device_id_type=MESH,
        )

    def ring_wait(which, gat, direction, hop, half):
        slot = 2 * origin(direction, hop) + core
        target = 2 * ((z + 1) % Z if direction == 0 else (z + Z - 1) % Z) + core
        pltpu.make_async_remote_copy(
            src_ref=chunk(gat, slot, half),
            dst_ref=chunk(gat, slot, half),
            send_sem=ring_send.at[which, direction, hop - 1, half],
            recv_sem=ring_recv.at[which, direction, hop - 1, half],
            device_id={"cols": target},
            device_id_type=MESH,
        ).wait_recv()

    def mate_copy(which, gat, direction, hop, side_core):
        part = gat.at[2 * origin(direction, min(hop, 4)) + side_core]
        if hop >= 4:
            part = part.at[dict(arrivals(which, 4, hop - 4))[direction]]
        return pltpu.make_async_remote_copy(
            src_ref=part,
            dst_ref=part,
            send_sem=mate_send.at[which, direction, hop],
            recv_sem=mate_recv.at[which, direction, hop],
            device_id={"cols": mate},
            device_id_type=MESH,
        )

    def arrivals(which, hop, k):
        order = ORDERS[which]
        if hop == 4:
            return list(enumerate(sorted(order[2 * k : 2 * k + 2])))
        return [(0, order[k]), (1, order[k])]

    sends = []

    def go(copy):
        copy.start()
        sends.append(copy)

    def ring_start(which, gat, parts):
        for part in parts:
            for direction in range(2):
                go(ring_copy(which, gat, direction, 1, part))
        if 3 in parts:
            go(mate_copy(which, gat, 0, 0, core))

    def ring_step(which, gat, hop, *ks):
        last = [pair for k in range(2) for pair in arrivals(which, 4, k)]
        for k in ks:
            for direction, part in arrivals(which, hop, k):
                ring_wait(which, gat, direction, hop, part)
                if hop < 3 or (hop == 3 and (direction, part) in last):
                    go(ring_copy(which, gat, direction, hop + 1, part))
                if hop == 4:
                    go(mate_copy(which, gat, direction, 4 + k, core))
                elif k == 3:
                    go(mate_copy(which, gat, direction, hop, core))

    def mate_step(which, gat, hop):
        for direction in range(1 if hop == 0 else 2):
            mate_copy(which, gat, direction, hop, 1 - core).wait_recv()

    loads["feat"].wait()
    loads["adap"].wait()
    for copy in small:
        copy.start()
    for name in ("w1a", "w3a", "w1b", "w3b"):
        loads[name].start()
    js = jnp.zeros((8, C3), F32)
    jq = jnp.zeros((8, C3), F32)
    for i in range(H3):
        value = (feat[i].astype(F32) + adap[i].astype(F32)).astype(BF16)
        gat1[col, i] = value
        value = value.astype(F32).reshape(2, 8, C3)
        js = js + jnp.sum(value, axis=0)
        jq = jq + jnp.sum(value * value, axis=0)

    pl.semaphore_wait(barrier, R - 1 + C - 1)
    ring_start(0, gat1, ORDERS[0])
    joined_sums = group_sums(js, jq, group_matrix(C3, 40, 0, 0), 64)

    loads["lat"].wait()

    def halo_copy(src, dst, index, target):
        return pltpu.make_async_remote_copy(
            src_ref=src,
            dst_ref=dst,
            send_sem=halo_send.at[index],
            recv_sem=halo_recv.at[index],
            device_id=target,
            device_id_type=MESH,
        )

    to_down = halo_copy(lat.at[pl.ds(H1 - 2, 2)], top, 0, {"rows": down})
    to_up = halo_copy(lat.at[pl.ds(0, 2)], bottom, 1, {"rows": up})
    to_down.start()
    to_up.start()

    ls = jnp.zeros((8, C1), F32)
    lq = jnp.zeros((8, C1), F32)
    for i in range(H1):
        value = lat[i].astype(F32).reshape(8, 8, C1)
        ls = ls + jnp.sum(value, axis=0)
        lq = lq + jnp.sum(value * value, axis=0)
    ones1 = group_matrix(C1, 10, 0, 0)
    st_a1[0] = group_sums(ls, lq, ones1, 0) + joined_sums
    spread(st_a1, "rows", 0)
    ring_step(0, gat1, 1, 0, 1, 2)
    st_a2[0] = collect(st_a1, "rows", 0)
    spread(st_a2, "cols", 1)

    to_down.wait()
    to_up.wait()

    def extended_row(i):
        if i < 2:
            return top[i]
        if i < H1 + 2:
            return lat[i - 2]
        return bottom[i - H1 - 2]

    for block in range(3):
        rows_here = [i for i in range(8 * block, 8 * block + 8) if i < H1 + 4]
        tiles = [jnp.zeros((8, C1), F32) for _ in range(4)]
        for i in rows_here:
            value = extended_row(i)
            first = value[0:16].astype(F32)
            last = value[48:64].astype(F32)
            here = iota((8, C1), 0) == i - 8 * block
            for j, piece in enumerate((last[14:15], last[15:16], first[0:1], first[1:2])):
                tiles[j] = jnp.where(here, jnp.broadcast_to(piece, (8, C1)), tiles[j])
        for j in range(4):
            pack[j // 2, j % 2, pl.ds(8 * block, 8), :] = tiles[j]
    to_right = halo_copy(pack.at[0], side.at[0], 2, {"cols": right})
    to_left = halo_copy(pack.at[1], side.at[1], 3, {"cols": left})
    to_right.start()
    to_left.start()

    ring_step(0, gat1, 1, 3)
    ring_step(0, gat1, 2, 0, 1, 2, 3)
    def group_rates(total):
        total = jnp.sum(total, axis=0, keepdims=True)
        total = jnp.broadcast_to(total, (8, 128))
        lane = iota((8, 128), 1)
        count = jnp.where(lane < 64, COUNT1, COUNT3)
        squares = pltpu.roll(total, 96, 1)
        mean = total / count
        spread_of = squares / count - mean * mean
        live = (lane < 32) | ((lane >= 64) & (lane < 96))
        inverse = lax.rsqrt(jnp.where(live, spread_of, 1.0) + EPS)
        return jnp.where(live, mean, 0.0), jnp.where(live, inverse, 0.0)

    def channel_rates(rates, matrix, gain, shift):
        both = exact_dot(jnp.where(iota((8, 128), 0) == 0, *rates), matrix)
        mean, inverse = both[0:1], both[1:2]
        scale = inverse * gain
        return 0.5 * scale, 0.5 * (shift - mean * scale)

    for copy in small:
        copy.wait()
    rates = group_rates(collect(st_a2, "cols", 1))
    scale1, shift1 = channel_rates(rates, group_matrix(C1, 10, 0, 1), flat(g1a), flat(b1a))

    def put_row(i, value, live):
        value = jnp.where(live, halves(value), 0.0)
        act[i, :, 0:C1] = pltpu.roll(value, 1, 0).astype(BF16)
        act[i, :, C1 : 2 * C1] = value.astype(BF16)
        act[i, :, 2 * C1 : 3 * C1] = pltpu.roll(value, WP - 1, 0).astype(BF16)

    place = iota((WP, C1), 0)

    slab_place = iota((16, C1), 0)
    wide_ok = (place < W1) | ((place < W1 + 2) & (col < C - 1)) | ((place >= WP - 2) & (col > 0))

    def act1_rows(first, last):
        for i in range(first, last):
            slab = jnp.zeros((16, C1), F32)
            base = 8 * (i // 8)
            for target, which, j in ((0, 1, 0), (1, 1, 1), (14, 0, 0), (15, 0, 1)):
                piece = side[which, j, pl.ds(base, 8), :][i - base : i - base + 1]
                slab = jnp.where(slab_place == target, jnp.broadcast_to(piece, (16, C1)), slab)
            value = jnp.concatenate([extended_row(i).astype(F32), slab], axis=0)
            live = wide_ok
            if i < 2:
                live = live & (row > 0)
            if i >= H1 + 2:
                live = live & (row < R - 1)
            put_row(i, value * scale1 + shift1, live)

    to_right.wait()
    to_left.wait()
    act1_rows(0, 20)
    ring_step(0, gat1, 3, 0, 1)

    def conv1(weights, first, count, width):
        total = None
        for dy in range(3):
            block = act[pl.ds(first + dy, count), 0:width, :].reshape(count * width, 3 * C1)
            part = jnp.dot(block, weights[dy], preferred_element_type=F32)
            total = part if total is None else total + part
        return total.reshape(count, width, C1)

    def norm3(slot, parts):
        for i in parts:
            value = gat1[slot, i].astype(F32) * scale3 + shift3
            act3[slot, i] = halves(value).astype(BF16)

    def norm_hop(which, gat, norm, hop):
        mate_step(which, gat, hop)
        parts = range(H3) if hop < 4 else ORDERS[which][2 * hop - 8 : 2 * hop - 6]
        for direction in range(1 if hop == 0 or hop >= 4 else 2):
            for k in range(2):
                norm(2 * origin(direction, min(hop, 4)) + k, parts)

    def norm3_hop(hop):
        norm_hop(0, gat1, norm3, hop)

    loads["w1a"].wait()
    hid[pl.ds(0, 6)] = conv1(w1a, 0, 6, WP)
    ring_step(0, gat1, 3, 2, 3)
    scale3, shift3 = channel_rates(rates, group_matrix(C3, 40, 64, 1), flat(g3a), flat(b3a))
    hid[pl.ds(6, 6)] = conv1(w1a, 6, 6, WP)
    for hop in range(4):
        norm3_hop(hop)

    def taps(weights, source, dims, i, first, last):
        prod[i, pl.ds(first, last - first), :] = lax.dot_general(
            weights[pl.ds(first, last - first), :], source(i), dims, preferred_element_type=F32
        )

    BAND = 3 * OC

    def border_taps(*args):
        taps(*args, 0, 2 * BAND, 3 * BAND)
        taps(*args, 3, 0, BAND)

    def other_taps(*args):
        for i in (1, 2):
            taps(*args, i, 0, 3 * BAND)
        taps(*args, 0, 0, 2 * BAND)
        taps(*args, 3, BAND, 3 * BAND)

    lane3 = iota((OC, W3), 1)

    def combine(target):
        columns = []
        for dx in range(3):
            total = None
            for dy in range(3):
                i = target + dy - 1
                if 0 <= i < H3:
                    part = prod[i, pl.ds((3 * dy + dx) * OC, OC), :]
                    total = part if total is None else total + part
            columns.append(total)
        before = jnp.where(lane3 == 0, 0.0, pltpu.roll(columns[0], 1, 1))
        after = jnp.where(lane3 == W3 - 1, 0.0, pltpu.roll(columns[2], W3 - 1, 1))
        return before + columns[1] + after

    def edge_copies(which):
        return [
            pltpu.make_async_remote_copy(
                src_ref=edge_s.at[which, j],
                dst_ref=edge_r.at[which, j],
                send_sem=edge_send.at[which, j],
                recv_sem=edge_recv.at[which, j],
                device_id={"rows": target},
                device_id_type=MESH,
            )
            for j, target in ((0, down), (1, up))
        ]

    def edges_out(which):
        edge_s[which, 0] = combine(H3).astype(BF16)
        edge_s[which, 1] = combine(-1).astype(BF16)
        copies = edge_copies(which)
        for copy in copies:
            copy.start()
        return copies

    def edges_in(which):
        low = jnp.where(row > 0, edge_r[which, 0].astype(F32), 0.0)
        high = jnp.where(row < R - 1, edge_r[which, 1].astype(F32), 0.0)
        return low, high

    loads["w3a"].wait()
    first3 = (w3a, lambda i: act3[:, i].reshape(W3, C3), NT)
    ring_step(0, gat1, 4, 0)
    norm3_hop(4)
    border_taps(*first3)
    copies = edges_out(0)
    ring_step(0, gat1, 4, 1)
    norm3_hop(5)
    other_taps(*first3)
    for i in (1, 2):
        value = combine(i)
        hid3[i] = value
        gat2[col, i] = value.astype(BF16)
    ring_start(1, gat2, (1, 2))
    for i in (0, 3):
        hid3[i] = combine(i)
    for copy in copies:
        copy.wait()
    for i, border in zip((0, 3), edges_in(0)):
        value = hid3[i] + border
        hid3[i] = value
        gat2[col, i] = value.astype(BF16)
    ring_start(1, gat2, (0, 3))

    fs = jnp.zeros((OC, W3), F32)
    fq = jnp.zeros((OC, W3), F32)
    for i in range(H3):
        value = hid3[i]
        fs = fs + value
        fq = fq + value * value
    fs = jnp.sum(fs, axis=1, keepdims=True)
    fq = jnp.sum(fq, axis=1, keepdims=True)
    lane = iota((OC, 128), 1)
    second = iota((OC, 128), 0) >= OC // 2
    group = jnp.where(second, 1, 0)
    laid = jnp.where(lane == group, fs, 0.0) + jnp.where(lane == group + 2, fq, 0.0)
    st_c[0] = jnp.sum(laid.reshape(OC // 8, 8, 128), axis=0)
    spread(st_c, "rows", 4)

    hid[pl.ds(12, 6)] = conv1(w1a, 12, 6, WP)
    hs = jnp.zeros((8, C1), F32)
    hq = jnp.zeros((8, C1), F32)
    for i in range(H1):
        value = hid[i + 1, 0:W1, :].reshape(8, 8, C1)
        hs = hs + jnp.sum(value, axis=0)
        hq = hq + jnp.sum(value * value, axis=0)
    st_b1[0] = group_sums(hs, hq, ones1, 0)
    spread(st_b1, "rows", 2)

    ring_step(1, gat2, 1, 0, 1, 2, 3)

    total = jnp.sum(collect(st_c, "rows", 4), axis=0, keepdims=True)
    total = jnp.broadcast_to(total, (OC, 128)) / COUNT3
    mean = jnp.sum(jnp.where(lane == group, total, 0.0), axis=1, keepdims=True)
    square = jnp.sum(jnp.where(lane == group + 2, total, 0.0), axis=1, keepdims=True)
    inverse = lax.rsqrt(square - mean * mean + EPS)

    def upright(ref):
        eye = iota((OC, OC), 0) == iota((OC, OC), 1)
        return jnp.sum(jnp.where(eye, jnp.broadcast_to(flat(ref), (OC, OC)), 0.0), axis=1, keepdims=True)

    scale4 = inverse * upright(g3b)
    shift4 = 0.5 * (upright(b3b) - mean * scale4)
    scale4 = 0.5 * scale4
    eye = iota((OC, 128), 0) == iota((OC, 128), 1)
    as_rows = [jnp.sum(jnp.where(eye, x, 0.0), axis=0, keepdims=True) for x in (scale4, shift4)]
    st_d[0] = jnp.where(iota((8, 128), 0) == 0, *as_rows)
    spread(st_d, "cols", 5)

    st_b2[0] = collect(st_b1, "rows", 2)
    spread(st_b2, "cols", 3)
    ring_step(1, gat2, 2, 0, 1)

    pick = jnp.where(iota((OC, C3), 1) == iota((OC, C3), 0) + col * OC, 1.0, 0.0).astype(BF16)

    def residual(i, carry):
        res[i] = lax.dot_general(pick, gat1[:, i].reshape(W3, C3), NT, preferred_element_type=F32)
        return carry

    lax.fori_loop(0, H3, residual, 0)
    ring_step(1, gat2, 2, 2, 3)

    def norm4(slot, parts):
        block = st_d[(col + C - slot) % C]
        scale, shift = (jnp.sum(jnp.where(eye, block[j : j + 1], 0.0), axis=1, keepdims=True) for j in range(2))
        for i in parts:
            act4[slot, i] = halves(gat2[slot, i].astype(F32) * scale + shift).astype(BF16)

    def norm4_hop(hop):
        norm_hop(1, gat2, norm4, hop)

    arrived(st_d, "cols", 5)
    norm4_hop(0)
    norm4_hop(1)

    rates = group_rates(collect(st_b2, "cols", 3))
    scale2, shift2 = channel_rates(rates, group_matrix(C1, 10, 0, 1), flat(g1b), flat(b1b))
    near_ok = (place < W1) | ((place == W1) & (col < C - 1)) | ((place == WP - 1) & (col > 0))

    def act2_rows(first, last):
        for i in range(first, last):
            live = near_ok
            if i == 0:
                live = live & (row > 0)
            if i == H1 + 1:
                live = live & (row < R - 1)
            put_row(i, hid[i] * scale2 + shift2, live)

    act2_rows(0, 18)
    ring_step(1, gat2, 3, 0, 1)
    loads["w1b"].wait()

    def out1_rows(first, count):
        value = conv1(w1b, first, count, W1) + flat(c1b).reshape(1, 1, C1)
        o1[pl.ds(first, count)] = (lat[pl.ds(first, count)].astype(F32) + value).astype(BF16)

    out1_rows(0, 4)
    ring_step(1, gat2, 3, 2, 3)
    out1_rows(4, 4)
    norm4_hop(2)
    norm4_hop(3)
    loads["w3b"].wait()
    second3 = (w3b, lambda i: act4[:, i].reshape(C3, W3), (((1,), (0,)), ((), ())))
    bias3 = upright(c3b)
    ring_step(1, gat2, 4, 0)
    norm4_hop(4)
    ring_step(1, gat2, 4, 1)
    norm4_hop(5)
    border_taps(*second3)
    copies = edges_out(1)
    out1_rows(8, 4)
    other_taps(*second3)
    out1_rows(12, 4)
    write1 = local(o1, out1_h, 7)
    write1.start()
    for i in range(H3):
        res[i] = res[i] + combine(i) + bias3
    for copy in copies:
        copy.wait()
    low, high = edges_in(1)
    res[0] = res[0] + low
    res[H3 - 1] = res[H3 - 1] + high
    for i in range(H3):
        o3[i] = res[i].astype(BF16)
    write3 = local(o3, out3_h, 8)
    write3.start()
    for copy in sends:
        copy.wait_send()
    write1.wait()
    write3.wait()


def deliver(from1, from3, to1, to3, held1, held3, load_sem, store_sem):
    pieces = [(from3, held3, to3)]
    pieces += [tuple(x.at[pl.ds(4 * i, 4)] for x in (from1, held1, to1)) for i in range(H1 // 4)]
    loads = [pltpu.make_async_copy(a, b, load_sem.at[i]) for i, (a, b, _) in enumerate(pieces)]
    stores = [pltpu.make_async_copy(b, c, store_sem.at[i]) for i, (_, b, c) in enumerate(pieces)]
    for copy in loads:
        copy.start()
    for load, store in zip(loads, stores):
        load.wait()
        store.start()
    for copy in stores:
        copy.wait()


def body(
    latent1, norm1a_g, norm1a_b, conv1a_w, norm1b_g, norm1b_b, conv1b_w, conv1b_b,
    feat3, adapter3, norm3a_g, norm3a_b, conv3a_w, norm3b_g, norm3b_b, conv3b_w, conv3b_b,
):
    def wide(w):
        return w.reshape(3, 3 * C1, C1)

    def tall(w):
        return jnp.swapaxes(w, 2, 3).reshape(9 * OC, C3)

    any_spec = pl.BlockSpec(memory_space=pl.ANY)
    operands = [
        (latent1, any_spec), (norm1a_g, any_spec), (norm1a_b, any_spec), (wide(conv1a_w), any_spec),
        (norm1b_g, any_spec), (norm1b_b, any_spec), (wide(conv1b_w), any_spec), (conv1b_b, any_spec),
        (feat3, any_spec), (adapter3, any_spec), (norm3a_g, any_spec), (norm3a_b, any_spec),
        (tall(conv3a_w), any_spec), (norm3b_g, any_spec), (norm3b_b, any_spec),
        (tall(conv3b_w), any_spec), (conv3b_b, any_spec),
    ]
    out1, out3 = pl.pallas_call(
        kernel,
        out_shape=(
            jax.ShapeDtypeStruct((H1, W1, C1), BF16),
            jax.ShapeDtypeStruct((H3, OC, W3), BF16),
        ),
        in_specs=[spec for _, spec in operands],
        out_specs=(any_spec, any_spec),
        scratch_shapes=[
            *[pltpu.VMEM((n,), F32) for n in (C1, C1, C1, C1, C1, C3, C3, OC, OC, OC)],
            pltpu.VMEM((H1, W1, C1), BF16),
            pltpu.VMEM((2, W1, C1), BF16),
            pltpu.VMEM((2, W1, C1), BF16),
            pltpu.VMEM((2, 2, 24, C1), F32),
            pltpu.VMEM((2, 2, 24, C1), F32),
            pltpu.VMEM((H1 + 4, WP, 3 * C1), BF16),
            pltpu.VMEM((H1 + 2, WP, C1), F32),
            pltpu.VMEM((3, 3 * C1, C1), BF16),
            pltpu.VMEM((3, 3 * C1, C1), BF16),
            pltpu.VMEM((9 * OC, C3), BF16),
            pltpu.VMEM((9 * OC, C3), BF16),
            pltpu.VMEM((H3, 16, C3), BF16),
            pltpu.VMEM((H3, 16, C3), BF16),
            pltpu.VMEM((C, H3, 16, C3), BF16),
            pltpu.VMEM((C, H3, 16, C3), BF16),
            pltpu.VMEM((C, H3, OC, W3), BF16),
            pltpu.VMEM((H3, 9 * OC, W3), F32),
            pltpu.VMEM((2, 2, OC, W3), BF16),
            pltpu.VMEM((2, 2, OC, W3), BF16),
            pltpu.VMEM((H3, OC, W3), F32),
            pltpu.VMEM((H3, OC, W3), F32),
            pltpu.VMEM((H1, W1, C1), BF16),
            pltpu.VMEM((H3, OC, W3), BF16),
            pltpu.VMEM((16, 8, 128), F32),
            pltpu.VMEM((16, 8, 128), F32),
            pltpu.VMEM((16, 8, 128), F32),
            pltpu.VMEM((16, 8, 128), F32),
            pltpu.VMEM((16, 8, 128), F32),
            pltpu.VMEM((16, 8, 128), F32),
            pltpu.VMEM((C, H3, OC, W3), BF16),
            pltpu.SemaphoreType.DMA((19,)),
            pltpu.SemaphoreType.DMA((6,)),
            pltpu.SemaphoreType.DMA((6,)),
            pltpu.SemaphoreType.DMA((2, 2, 4, 4)),
            pltpu.SemaphoreType.DMA((2, 2, 4, 4)),
            pltpu.SemaphoreType.DMA((2, 2, 6)),
            pltpu.SemaphoreType.DMA((2, 2, 6)),
            pltpu.SemaphoreType.DMA((4,)),
            pltpu.SemaphoreType.DMA((4,)),
            pltpu.SemaphoreType.DMA((2, 2)),
            pltpu.SemaphoreType.DMA((2, 2)),
        ],
        compiler_params=pltpu.CompilerParams(
            collective_id=0, has_side_effects=True, vmem_limit_bytes=56 * 1024 * 1024
        ),
    )(*[value for value, _ in operands])
    out1, out3 = pl.pallas_call(
        deliver,
        out_shape=(
            jax.ShapeDtypeStruct((H1, W1, C1), BF16),
            jax.ShapeDtypeStruct((H3, OC, W3), BF16),
        ),
        in_specs=[any_spec, any_spec],
        out_specs=(any_spec, any_spec),
        scratch_shapes=[
            pltpu.VMEM((H1, W1, C1), BF16),
            pltpu.VMEM((H3, OC, W3), BF16),
            pltpu.SemaphoreType.DMA((5,)),
            pltpu.SemaphoreType.DMA((5,)),
        ],
    )(out1, out3)
    return out1, jnp.swapaxes(out3, 1, 2)


def solution(mesh):
    return jax.shard_map(
        body,
        mesh=mesh,
        in_specs=(
            P("rows", "cols", None), P(), P(), P(), P(), P(), P(), P(),
            P("rows", "cols", None), P("rows", "cols", None), P(), P(),
            P(None, None, None, "cols"), P("cols"), P("cols"), P(None, None, None, "cols"), P("cols"),
        ),
        out_specs=(P("rows", "cols", None), P("rows", None, "cols")),
        check_vma=False,
    )
```
